32 devices in a mesh: wide: 8 (over z, x), narrow: 4 (over y, core).
Axes of the slice: x: 2, y: 2, z: 4, core: 2. Of those that a mesh axis runs over, the one named last changes fastest.
Arguments:
- tokens: bfloat16 [32768, 1024], P(('wide', 'narrow')), may hold values from -6 to 6
- cotangent: bfloat16 [32768, 1024], P(('wide', 'narrow')), may hold values from -6 to 6
- seq_lens: int32 [32, 4], P(('wide', 'narrow')), may hold values from 0 to 1024, as said below
- norm_gain: bfloat16 [1024], P(('wide', 'narrow')), may hold values from 0.099609375 to 1.8984375
- norm_bias: bfloat16 [1024], P(('wide', 'narrow')), may hold values from -4 to 4
- qkv_weight: bfloat16 [1024, 3072], P(('wide', 'narrow')), may hold values from -0.1875 to 0.1875
- qkv_bias: bfloat16 [3072], P(('wide', 'narrow')), may hold values from -4 to 4
- out_weight: bfloat16 [1024, 1024], P(('wide', 'narrow')), may hold values from -3 to 3
- out_bias: bfloat16 [1024], P(('wide', 'narrow')), may hold values from -4 to 4
- fc_in_weight: bfloat16 [1024, 4096], P(('wide', 'narrow')), may hold values from -0.1875 to 0.1875
- fc_in_bias: bfloat16 [4096], P(('wide', 'narrow')), may hold values from -4 to 4
- fc_out_weight: bfloat16 [4096, 1024], P(('wide', 'narrow')), may hold values from -0.09375 to 0.09375
- fc_out_bias: bfloat16 [1024], P(('wide', 'narrow')), may hold values from -4 to 4
Outputs:
- mixed: bfloat16 [32768, 1024], P(('wide', 'narrow'))
- tokens_grad: bfloat16 [32768, 1024], P(('wide', 'narrow'))
- norm_gain_grad: float32 [1024], P(('wide', 'narrow'))
- norm_bias_grad: float32 [1024], P(('wide', 'narrow'))
- qkv_weight_grad: float32 [1024, 3072], P(('wide', 'narrow'))
- qkv_bias_grad: float32 [3072], P(('wide', 'narrow'))
- out_weight_grad: float32 [1024, 1024], P(('wide', 'narrow'))
- out_bias_grad: float32 [1024], P(('wide', 'narrow'))
- fc_in_weight_grad: float32 [1024, 4096], P(('wide', 'narrow'))
- fc_in_bias_grad: float32 [4096], P(('wide', 'narrow'))
- fc_out_weight_grad: float32 [4096, 1024], P(('wide', 'narrow'))
- fc_out_bias_grad: float32 [1024], P(('wide', 'narrow'))
- stream_rms: float32 [32, 3], P(('wide', 'narrow'))
The draws below stay inside these ranges and needn't reach their ends.
Inputs may be any that keep to these rules, and one draw needn't show every extreme that they name: `seq_lens`: row r lists the sequences packed in order on device r: each length is 1024, half of it or a quarter of it (256), zeros come last, the lengths of a row add up to 1024; in every draw some device holds one single sequence of 1024 tokens.
All inputs are finite; a program needn't handle non-finite values.
Results may differ from the reference program's by a relative error of at most 0.0099.
Values may be sent and summed in bfloat16 or wider, within the bound.
A program may use at most 256 MiB of HBM per device.

```python
import jax
import jax.numpy as jnp
from jax import lax

D = 1024
HEADS = 16
FF = 4096
HEAD = 64
ROT = 16
TOK_DEV = 1024
TOKENS = 32768
N_WIDE = 8
N_NARROW = 4


def draw_seq_lens(key, part):
    key = jax.random.fold_in(key, 7)
    first_key, second_key = jax.random.split(key)
    devices_all = N_WIDE * N_NARROW
    shortest = TOK_DEV // 4
    patterns = jnp.array([[4, 0, 0, 0], [2, 2, 0, 0], [2, 1, 1, 0], [1, 1, 2, 0], [1, 2, 1, 0], [1, 1, 1, 1]], dtype=jnp.int32) * shortest
    picked = jax.random.randint(first_key, (devices_all,), 0, 6)
    single = jax.random.randint(second_key, (), 0, devices_all)
    picked = jnp.where(jnp.arange(devices_all) == single, 0, picked)
    return patterns[picked]


def with_spikes(values, stream_key, source, target, shards_of, factor):
    def block_of(dim):
        return (jnp.arange(values.shape[dim]) // (values.shape[dim] // shards_of)).reshape((-1,) + (1,) * (values.ndim - 1 - dim))

    one_side = jax.random.permutation(stream_key, shards_of)[block_of(target)]
    far = (block_of(target) + shards_of // 2) % shards_of
    return jnp.where((block_of(source) == one_side) | (block_of(source) == far), factor * values, values)


def block_levels(key, extent, cuts, low, top_value):
    def one(dim, parts):
        draws = jax.random.uniform(jax.random.fold_in(jax.random.fold_in(key, 6), dim), (parts,), jnp.float32, low / len(cuts), top_value / len(cuts))
        return jnp.repeat(jnp.exp(draws), extent[dim] // parts).reshape((-1,) + (1,) * (len(extent) - dim - 1))

    factor_of = one(*cuts[0])
    for cut in cuts[1:]:
        factor_of = factor_of * one(*cut)
    return factor_of


def scatter_about(rng, dims, scale, reach, cuts=(), kind=jnp.bfloat16):
    entries = jax.random.normal(rng, dims, jnp.float32) * scale
    if len(cuts) > 0:
        entries = block_levels(rng, dims, cuts, -0.22, 0.18) * entries
    return jnp.clip(entries, min=-reach, max=reach).astype(kind)


def noise_with(stream_key, shape, scale, limit, pieces, heavy, held_as=jnp.bfloat16):
    drawn = scale * jax.random.normal(stream_key, shape, jnp.float32)
    if pieces:
        drawn = drawn * block_levels(stream_key, shape, pieces, -0.22, 0.18)
    return jnp.clip(with_spikes(drawn, jax.random.fold_in(stream_key, 3), *heavy), -limit, limit).astype(held_as)


def setup_inputs(seed: int = 0) -> dict:
    seeds = jax.random.split(jax.random.key(seed), 14)
    tokens = noise_with(seeds[0], (TOKENS, D), 1.0, 6.0, ((0, 32),), (0, 1, 32, 2.75))
    cotangent = noise_with(seeds[1], (TOKENS, D), 1.0, 6.0, ((0, 32),), (0, 1, 32, 2.75))
    seq_lens = draw_seq_lens(jax.random.fold_in(seeds[13], 71), 0)
    norm_gain = jnp.clip(1.0 + 0.18 * jax.random.normal(seeds[3], (D,), jnp.float32), 0.099609375, 1.8984375).astype(jnp.bfloat16)
    norm_bias = scatter_about(seeds[4], (D,), 0.3, 4.0, ((0, 32),))
    qkv_weight = scatter_about(seeds[5], (D, 3 * D), D ** -0.5, 0.1875, ((0, 32),))
    qkv_bias = scatter_about(seeds[6], (3 * D,), 0.3, 4.0, ((0, 32),))
    out_weight = scatter_about(seeds[7], (D, D), (4 * D // TOK_DEV) ** -0.5, 3.0, ((0, 32),))
    out_bias = scatter_about(seeds[8], (D,), 0.3, 4.0, ((0, 32),))
    fc_in_weight = scatter_about(seeds[9], (D, FF), D ** -0.5, 0.1875, ((0, 32),))
    fc_in_bias = scatter_about(seeds[10], (FF,), 0.3, 4.0, ((0, 32),))
    fc_out_weight = scatter_about(seeds[11], (FF, D), FF ** -0.5, 0.09375, ((0, 32),))
    fc_out_bias = scatter_about(seeds[12], (D,), 0.3, 4.0, ((0, 32),))
    return {"tokens": tokens, "cotangent": cotangent, "seq_lens": seq_lens, "norm_gain": norm_gain, "norm_bias": norm_bias, "qkv_weight": qkv_weight, "qkv_bias": qkv_bias, "out_weight": out_weight, "out_bias": out_bias, "fc_in_weight": fc_in_weight, "fc_in_bias": fc_in_bias, "fc_out_weight": fc_out_weight, "fc_out_bias": fc_out_bias}


epsilon = 1e-05
highest = lax.Precision.HIGHEST

@jax.custom_vjp
def low(v):
    return lax.optimization_barrier(v.astype(jnp.bfloat16)).astype(jnp.float32)

@jax.custom_vjp
def low_back(v):
    return v

def low_keep(v):
    return (low(v), None)

def low_pass(kept, grad):
    return (grad,)

def back_keep(v):
    return (v, None)

def back_low(kept, grad):
    return (low(grad),)
low.defvjp(low_keep, low_pass)
low_back.defvjp(back_keep, back_low)

def positions(lengths, count):
    lengths = lengths.astype(jnp.int32)
    ends = jnp.cumsum(lengths).astype(jnp.int32)
    places = jnp.arange(count, dtype=jnp.int32)
    segment = lax.optimization_barrier(jnp.sum((places[:, None] >= ends[None, :]).astype(jnp.int32), axis=1))
    starts = ends - lengths
    slots = jnp.arange(lengths.shape[0], dtype=jnp.int32)
    begin = lax.optimization_barrier(jnp.sum(jnp.where(segment[:, None] == slots[None, :], starts[None, :], 0), axis=1))
    return (segment, places, (places - begin).astype(jnp.float32))

def rotate(vector, cosine, sine):
    half = ROT // 2
    first = vector[..., :half]
    second = vector[..., half:ROT]
    return jnp.concatenate([first * cosine - second * sine, second * cosine + first * sine, vector[..., ROT:]], axis=-1)

def layer(inputs, lengths, gain, shift, qkv_w, qkv_b, out_w, out_b, in_w, in_b, down_w, down_b):
    count = inputs.shape[0]
    centred = inputs - lax.optimization_barrier(jnp.mean(inputs, axis=-1, keepdims=True))
    inverse = lax.rsqrt(lax.optimization_barrier(jnp.mean(centred * centred, axis=-1, keepdims=True)) + epsilon)
    hidden = low(centred * inverse * gain + shift)
    qkv = low_back(jnp.dot(hidden, qkv_w, precision=highest) + qkv_b)
    queries = qkv[:, :D].reshape(count, HEADS, HEAD)
    keys = qkv[:, D:2 * D].reshape(count, HEADS, HEAD)
    values = qkv[:, 2 * D:].reshape(count, HEADS, HEAD)
    segment, places, offset = positions(lengths, count)
    freqs = 10000.0 ** (-jnp.arange(ROT // 2, dtype=jnp.float32) * 2.0 / ROT)
    angle = offset[:, None] * freqs[None, :]
    cosine = jnp.cos(angle)[:, None, :]
    sine = jnp.sin(angle)[:, None, :]
    q_low = low(rotate(queries, cosine, sine))
    k_low = low(rotate(keys, cosine, sine))
    v_low = low(values)
    raw = jnp.einsum('qhd,khd->hqk', q_low, k_low, precision=highest)
    scores = low_back(raw * HEAD ** (-0.5))
    allowed = (segment[:, None] == segment[None, :]) & (places[None, :] <= places[:, None])
    scores = jnp.where(allowed[None], scores, -1e+30)
    row_max = lax.optimization_barrier(jnp.max(scores, axis=-1, keepdims=True))
    expo = jnp.exp(scores - row_max)
    probs = low(expo / lax.optimization_barrier(jnp.sum(expo, axis=-1, keepdims=True)))
    attended = jnp.einsum('hqk,khd->qhd', probs, v_low, precision=highest).reshape(count, D)
    att_low = low(low_back(attended))
    attn_out = jnp.dot(att_low, out_w, precision=highest) + out_b
    pre = low_back(jnp.dot(hidden, in_w, precision=highest) + in_b)
    act = low(jax.nn.gelu(pre, approximate=False))
    mlp = jnp.dot(act, down_w, precision=highest) + down_b
    result = inputs + attn_out + mlp
    stats = jnp.sqrt(jnp.stack([jnp.mean(inputs * inputs), jnp.mean(attn_out * attn_out), jnp.mean(mlp * mlp)]))
    return (result, stats)

def reference(tokens, cotangent, seq_lens, norm_gain, norm_bias, qkv_weight, qkv_bias, out_weight, out_bias, fc_in_weight, fc_in_bias, fc_out_weight, fc_out_bias):
    devices_all = N_WIDE * N_NARROW
    params = tuple((p.astype(jnp.float32) for p in (norm_gain, norm_bias, qkv_weight, qkv_bias, out_weight, out_bias, fc_in_weight, fc_in_bias, fc_out_weight, fc_out_bias)))
    checked = jax.checkpoint(layer)

    def whole(inputs, *weights):

        def step(carry, item):
            block, lengths = item
            result, stats = checked(block, lengths, *weights)
            return (carry, (result, stats))
        _, (results, stats) = lax.scan(step, jnp.zeros((), jnp.float32), (inputs.reshape(devices_all, TOK_DEV, D), seq_lens))
        return (results.reshape(devices_all * TOK_DEV, D), stats)
    result, pull, stats = jax.vjp(whole, tokens.astype(jnp.float32), *params, has_aux=True)
    grads = pull(cotangent.astype(jnp.float32))
    return (result.astype(jnp.bfloat16), grads[0].astype(jnp.bfloat16), grads[1], grads[2], grads[3], grads[4], grads[5], grads[6], grads[7], grads[8], grads[9], grads[10], stats)
```

```python
from functools import partial

import jax
import jax.numpy as jnp
from jax import lax
from jax.experimental import pallas as pl
from jax.experimental.pallas import tpu as pltpu
from jax.sharding import PartitionSpec as P

HEADS = 16
HEAD = 64
ROT = 16
MESH = pl.DeviceIdType.MESH
bf16 = jnp.bfloat16
f32 = jnp.float32
ALL = slice(None)

epsilon = 1e-05


def positions(lengths, count):
    ends = jnp.cumsum(lengths)
    places = jnp.arange(count, dtype=jnp.int32)
    segment = jnp.sum((places[:, None] >= ends[None, :]).astype(jnp.int32), axis=1)
    starts = ends - lengths
    slots = jnp.arange(lengths.shape[0], dtype=jnp.int32)
    begin = jnp.sum(jnp.where(segment[:, None] == slots[None, :], starts[None, :], 0), axis=1)
    return (segment, places, (places - begin).astype(jnp.float32))


def rotate(vector, cosine, sine):
    half = ROT // 2
    first = vector[..., :half]
    second = vector[..., half:ROT]
    return jnp.concatenate(
        [first * cosine - second * sine, second * cosine + first * sine, vector[..., ROT:]], axis=-1
    )


def unrotate(grad, cosine, sine):
    half = ROT // 2
    first = grad[..., :half]
    second = grad[..., half:ROT]
    return jnp.concatenate(
        [first * cosine + second * sine, second * cosine - first * sine, grad[..., ROT:]], axis=-1
    )


def times_transposed(left, right):
    return lax.dot_general(
        left, right, (((1,), (1,)), ((), ())), preferred_element_type=jnp.float32
    )


def transposed_times(left, right):
    return lax.dot_general(
        left, right, (((0,), (0,)), ((), ())), preferred_element_type=jnp.float32
    )


def block_scores(query_block, key_low, seg_query, seg_key, place_query, place_key):
    raw = jnp.einsum(
        "qhd,khd->hqk", query_block, key_low, preferred_element_type=jnp.float32
    ) * HEAD ** (-0.5)
    allowed = (seg_query[:, None] == seg_key[None, :]) & (
        place_key[None, :] <= place_query[:, None]
    )
    return (jnp.where(allowed[None], raw, -1e30), allowed)


QG = 4
MC = 8


class Place:
    def __init__(self):
        wide, narrow = lax.axis_index("wide"), lax.axis_index("narrow")
        self.z, self.x = wide // 2, wide % 2
        self.y, self.c = narrow // 2, narrow % 2
        self.me = (self.z, self.x, self.y, self.c)
        self.zs = [(self.z + d) % 4 for d in (1, 2, 3)]

    def device(self, z, x, y, c):
        return (z * 2 + x, y * 2 + c)

    def partners(self):
        z, x, y, c = self.me
        return [self.device(p, x, y, c) for p in self.zs] + [
            self.device(z, 1 - x, y, c),
            self.device(z, x, 1 - y, c),
            self.device(z, x, y, 1 - c),
        ]

    def greet(self):
        barrier = pltpu.get_barrier_semaphore()
        for other in self.partners():
            pl.semaphore_signal(barrier, inc=1, device_id=other, device_id_type=MESH)
        pl.semaphore_wait(barrier, 6)


class Gather:
    def __init__(self, place, view, x_first, send, recv):
        self.p, self.view, self.x_first, self.send, self.recv = place, view, x_first, send, recv
        self.started = []

    def _copy(self, part, device, slot):
        copy = pltpu.make_async_remote_copy(
            src_ref=self.view(*part),
            dst_ref=self.view(*part),
            send_sem=self.send(slot),
            recv_sem=self.recv(slot),
            device_id=device,
            device_id_type=MESH,
        )
        copy.start()
        self.started.append(copy)
        return copy

    def along_z(self):
        z, x, y, c = self.p.me
        self.waiting = [
            self._copy(self.p.me, self.p.device(other, x, y, c), i)
            for i, other in enumerate(self.p.zs)
        ]

    def arrived(self):
        for copy in self.waiting:
            copy.wait_recv()
        self.waiting = []

    def second(self):
        self.arrived()
        z, x, y, c = self.p.me
        to = (z, 1 - x, y, c) if self.x_first else (z, x, 1 - y, c)
        self.waiting = [self._copy((ALL, x, y, c), self.p.device(*to), 3)]

    def third(self):
        self.arrived()
        z, x, y, c = self.p.me
        if self.x_first:
            part, to = (ALL, ALL, y, c), (z, x, 1 - y, c)
        else:
            part, to = (ALL, x, ALL, c), (z, 1 - x, y, c)
        self.waiting = [self._copy(part, self.p.device(*to), 4)]

    def sibling(self):
        self.arrived()
        z, x, y, c = self.p.me
        self.waiting = [
            self._copy((ALL, ALL, ALL, c), self.p.device(z, x, y, 1 - c), 5)
        ]

    def close(self):
        for copy in self.started:
            copy.wait_send()
        self.started = []


class Scatter:
    def __init__(self, place, part, bufs, x_last, send, recv):
        self.p, self.part, self.bufs, self.x_last = place, part, bufs, x_last
        self.send, self.recv = send, recv

    def _copy(self, src, dst, device, slot):
        copy = pltpu.make_async_remote_copy(
            src_ref=src,
            dst_ref=dst,
            send_sem=self.send(slot),
            recv_sem=self.recv(slot),
            device_id=device,
            device_id_type=MESH,
        )
        copy.start()
        return copy

    def sibling(self):
        z, x, y, c = self.p.me
        self.started = [
            self._copy(
                self.part(ALL, ALL, ALL, 1 - c),
                self.bufs[0],
                self.p.device(z, x, y, 1 - c),
                5,
            )
        ]

    def add(self, part, buf):
        part[...] = part[...] + buf[...]

    def second(self):
        z, x, y, c = self.p.me
        self.started[-1].wait_recv()
        self.add(self.part(ALL, ALL, ALL, c), self.bufs[0])
        if self.x_last:
            part, to = (ALL, ALL, 1 - y, c), (z, x, 1 - y, c)
        else:
            part, to = (ALL, 1 - x, ALL, c), (z, 1 - x, y, c)
        self.started.append(
            self._copy(self.part(*part), self.bufs[1], self.p.device(*to), 4)
        )

    def third(self):
        z, x, y, c = self.p.me
        self.started[-1].wait_recv()
        part = (ALL, ALL, y, c) if self.x_last else (ALL, x, ALL, c)
        self.add(self.part(*part), self.bufs[1])
        if self.x_last:
            part, to = (ALL, 1 - x, y, c), (z, 1 - x, y, c)
        else:
            part, to = (ALL, x, 1 - y, c), (z, x, 1 - y, c)
        self.started.append(
            self._copy(self.part(*part), self.bufs[2], self.p.device(*to), 3)
        )

    def along_z(self):
        z, x, y, c = self.p.me
        self.started[-1].wait_recv()
        self.add(self.part(ALL, x, y, c), self.bufs[2])
        for i, other in enumerate(self.p.zs):
            self.started.append(
                self._copy(
                    self.part(other, x, y, c),
                    self.bufs[3].at[i],
                    self.p.device(other, x, y, c),
                    i,
                )
            )

    def total(self):
        for copy in self.started[-3:]:
            copy.wait_recv()
        out = self.part(*self.p.me)[...].astype(f32)
        for i in range(3):
            out = out + self.bufs[3][i].astype(f32)
        for copy in self.started:
            copy.wait_send()
        return out


def gather_kernel(
    qkv, out, fc_in, down, small, ag_q, ag_o, ag_i, ag_d, ag_s, own, send, recv
):
    place = Place()
    me = place.me
    units = []
    locals_ = []

    def own_copy(src, dst):
        copy = pltpu.make_async_copy(src, dst, own.at[len(locals_)])
        copy.start()
        locals_.append(copy)
        return copy

    def unit(copies, views):
        n = len(units)
        units.append(
            (
                copies,
                [
                    Gather(
                        place,
                        view,
                        k == 0,
                        lambda s, n=n, k=k: send.at[n, k, s],
                        lambda s, n=n, k=k: recv.at[n, k, s],
                    )
                    for k, view in enumerate(views)
                ],
            )
        )

    def q_unit(g):
        copies = [
            own_copy(
                qkv.at[:, pl.ds(1024 * j + 256 * g, 256)],
                ag_q.at[(g,) + me + (ALL, pl.ds(256 * j, 256))],
            )
            for j in range(3)
        ]
        unit(
            copies,
            [
                lambda *i, h=h: ag_q.at[(g,) + i + (pl.ds(16 * h, 16),)]
                for h in range(2)
            ],
        )

    unit([own_copy(small, ag_s.at[me])], [lambda *i: ag_s.at[i]])
    q_unit(0)
    unit(
        [own_copy(out, ag_o.at[me])],
        [lambda *i, h=h: ag_o.at[i + (pl.ds(16 * h, 16),)] for h in range(2)],
    )
    for g in range(1, QG):
        q_unit(g)
    for j in range(MC):
        unit(
            [
                own_copy(fc_in.at[:, pl.ds(512 * j, 512)], ag_i.at[(j,) + me]),
                own_copy(down.at[pl.ds(16 * j, 16)], ag_d.at[(j,) + me]),
            ],
            [lambda *i, j=j: ag_i.at[(j,) + i], lambda *i, j=j: ag_d.at[(j,) + i]],
        )
    place.greet()
    count = len(units)
    ahead = 2
    for t in range(-ahead, count + 4):
        n = t + ahead
        if n < count:
            for copy in units[n][0]:
                copy.wait()
            for array in units[n][1]:
                array.along_z()
        for lag, step in ((1, "second"), (2, "third"), (3, "sibling"), (4, "arrived")):
            if 0 <= t - lag < count:
                for array in units[t - lag][1]:
                    getattr(array, step)()
    for _, arrays in units:
        for array in arrays:
            array.close()


def scatter_kernel(
    gq, go, gi, gd, gs, out_q, out_o, out_i, out_d, out_s,
    part, r1, r2, r3, rz, part_s, s1, s2, s3, sz, load, send, recv,
):
    place = Place()
    place.greet()
    units = []

    def unit(sources, width, store):
        n = len(units)
        slot = n % 2
        arrays = []
        for k in range(2):
            arrays.append(
                Scatter(
                    place,
                    lambda *i, k=k: part.at[(k, slot) + i + (ALL, pl.ds(0, width))],
                    [
                        b.at[(k, slot) + (ALL,) * d + (ALL, pl.ds(0, width))]
                        for b, d in ((r1, 3), (r2, 2), (r3, 1), (rz, 1))
                    ],
                    k == 0,
                    lambda s, n=n, k=k: send.at[n, k, s],
                    lambda s, n=n, k=k: recv.at[n, k, s],
                )
            )
        units.append((sources, arrays, store))

    def q_store(g):
        def store(totals):
            for h in range(2):
                for j in range(3):
                    out_q[pl.ds(16 * h, 16), pl.ds(1024 * j + 256 * g, 256)] = totals[h][
                        :, 256 * j : 256 * (j + 1)
                    ]

        return store

    def o_store(totals):
        for h in range(2):
            out_o[pl.ds(16 * h, 16), :] = totals[h]

    def m_store(j):
        def store(totals):
            for h in range(2):
                out_i[pl.ds(16 * h, 16), pl.ds(512 * j, 512)] = totals[0][
                    :, 512 * h : 512 * (h + 1)
                ]
            out_d[pl.ds(16 * j, 16), :] = totals[1]

        return store

    for g in range(QG):
        unit([gq.at[g, h] for h in range(2)], 768, q_store(g))
    unit([go.at[h] for h in range(2)], 1024, o_store)
    for j in range(MC):
        unit([gi.at[j], gd.at[j]], 1024, m_store(j))
    count = len(units)

    def begin(n):
        sources, arrays, _ = units[n]
        copies = []
        for k in range(2):
            copy = pltpu.make_async_copy(
                sources[k],
                arrays[k].part(ALL, ALL, ALL, ALL),
                load.at[k],
            )
            copy.start()
            copies.append(copy)
        for k in range(2):
            copies[k].wait()
            arrays[k].sibling()

    def end(n):
        _, arrays, store = units[n]
        store([array.total() for array in arrays])

    for t in range(0, 2 * count + 4):
        for n in range(count):
            step = t - 2 * n
            if step == 4:
                end(n)
        for n in range(count):
            step = t - 2 * n
            if 1 <= step <= 3:
                for array in units[n][1]:
                    (array.second, array.third, array.along_z)[step - 1]()
            if step == 0:
                begin(n)
    tiny = Scatter(
        place,
        lambda *i: part_s.at[i],
        [s1, s2, s3, sz],
        True,
        lambda s: send.at[count, 0, s],
        lambda s: recv.at[count, 0, s],
    )
    copy = pltpu.make_async_copy(gs, part_s, load.at[0])
    copy.start()
    copy.wait()
    tiny.sibling()
    tiny.second()
    tiny.third()
    tiny.along_z()
    out_s[...] = tiny.total()


def gather_all(qkv, out, fc_in, down, small):
    any_ = pl.BlockSpec(memory_space=pl.ANY)
    sd = jax.ShapeDtypeStruct
    ranks = (4, 2, 2, 2)
    return pl.pallas_call(
        gather_kernel,
        out_shape=[
            sd((QG,) + ranks + (32, 768), bf16),
            sd(ranks + (32, 1024), bf16),
            sd((MC,) + ranks + (32, 512), bf16),
            sd((MC,) + ranks + (16, 1024), bf16),
            sd(ranks + (16, 128), bf16),
        ],
        in_specs=[any_] * 5,
        out_specs=[any_] * 5,
        scratch_shapes=[
            pltpu.SemaphoreType.DMA((30,)),
            pltpu.SemaphoreType.DMA((14, 2, 6)),
            pltpu.SemaphoreType.DMA((14, 2, 6)),
        ],
        compiler_params=pltpu.CompilerParams(collective_id=0, has_side_effects=True),
    )(qkv, out, fc_in, down, small)


def scatter_all(gq, go, gi, gd, gs):
    any_ = pl.BlockSpec(memory_space=pl.ANY)
    vmem = pl.BlockSpec(memory_space=pltpu.VMEM)
    sd = jax.ShapeDtypeStruct
    return pl.pallas_call(
        scatter_kernel,
        out_shape=[
            sd((32, 3072), f32),
            sd((32, 1024), f32),
            sd((32, 4096), f32),
            sd((128, 1024), f32),
            sd((8, 128), f32),
        ],
        in_specs=[any_] * 5,
        out_specs=[vmem] * 5,
        scratch_shapes=[
            pltpu.VMEM((2, 2, 4, 2, 2, 2, 16, 1024), bf16),
            pltpu.VMEM((2, 2, 4, 2, 2, 16, 1024), bf16),
            pltpu.VMEM((2, 2, 4, 2, 16, 1024), bf16),
            pltpu.VMEM((2, 2, 4, 16, 1024), bf16),
            pltpu.VMEM((2, 2, 3, 16, 1024), bf16),
            pltpu.VMEM((4, 2, 2, 2, 8, 128), f32),
            pltpu.VMEM((4, 2, 2, 8, 128), f32),
            pltpu.VMEM((4, 2, 8, 128), f32),
            pltpu.VMEM((4, 8, 128), f32),
            pltpu.VMEM((3, 8, 128), f32),
            pltpu.SemaphoreType.DMA((2,)),
            pltpu.SemaphoreType.DMA((14, 2, 6)),
            pltpu.SemaphoreType.DMA((14, 2, 6)),
        ],
        compiler_params=pltpu.CompilerParams(
            collective_id=1, has_side_effects=True, vmem_limit_bytes=40 * 2**20
        ),
    )(gq, go, gi, gd, gs)


def layer_math(
    tokens, cotangent, seq_lens, gain, shift, qkv_matrix, qkv_b, out_matrix, out_b,
    in_matrix, in_b, down_matrix, down_b,
):
    gain_full, shift_full = gain.astype(f32), shift.astype(f32)
    row_count, width = tokens.shape
    inputs = tokens.astype(f32)
    centred = inputs - jnp.mean(inputs, axis=-1, keepdims=True)
    inverse = lax.rsqrt(jnp.mean(centred * centred, axis=-1, keepdims=True) + epsilon)
    normed = centred * inverse
    hid_low = (normed * gain_full + shift_full).astype(bf16)
    qkv = jnp.dot(hid_low, qkv_matrix, preferred_element_type=f32) + qkv_b.astype(f32)
    segment, places, offset = positions(seq_lens[0], row_count)
    freqs = 10000.0 ** (-jnp.arange(ROT // 2, dtype=f32) * 2.0 / ROT)
    angle = offset[:, None] * freqs[None, :]
    cosine = jnp.cos(angle)[:, None, :]
    sine = jnp.sin(angle)[:, None, :]
    heads = (row_count, HEADS, HEAD)
    q_low = rotate(qkv[:, :width].reshape(heads), cosine, sine).astype(bf16)
    k_low = rotate(qkv[:, width : 2 * width].reshape(heads), cosine, sine).astype(bf16)
    v_low = qkv[:, 2 * width :].reshape(heads).astype(bf16)
    block_rows = min(512, row_count)
    block_count = row_count // block_rows
    outputs = []
    kept_lse = []
    for block in range(block_count):
        lower = block * block_rows
        upper = lower + block_rows
        scores, allowed = block_scores(
            q_low[lower:upper], k_low[:upper], segment[lower:upper], segment[:upper],
            places[lower:upper], places[:upper],
        )
        row_max = jnp.max(scores, axis=-1, keepdims=True)
        expo = jnp.exp(scores - row_max)
        totals = jnp.sum(expo, axis=-1, keepdims=True)
        soft_low = (expo / totals).astype(bf16)
        kept_lse.append(row_max + jnp.log(totals))
        outputs.append(
            jnp.einsum("hqk,khd->qhd", soft_low, v_low[:upper], preferred_element_type=f32)
        )
    att_low = jnp.concatenate(outputs, axis=0).reshape(row_count, width).astype(bf16)
    attn_out = jnp.dot(att_low, out_matrix, preferred_element_type=f32) + out_b.astype(f32)
    pre = jnp.dot(hid_low, in_matrix, preferred_element_type=f32) + in_b.astype(f32)
    gelu_exact = partial(jax.nn.gelu, approximate=False)
    act_low = gelu_exact(pre).astype(bf16)
    mlp = jnp.dot(act_low, down_matrix, preferred_element_type=f32) + down_b.astype(f32)
    mixed = (inputs + attn_out + mlp).astype(bf16)
    stream_rms = jnp.sqrt(
        jnp.stack([jnp.mean(inputs * inputs), jnp.mean(attn_out * attn_out), jnp.mean(mlp * mlp)])
    )[None, :]
    upstream = cotangent.astype(f32)
    grad_down = transposed_times(act_low, cotangent)
    grad_out = transposed_times(att_low, cotangent)
    grad_sum = jnp.sum(upstream, axis=0)
    act_grad = times_transposed(cotangent, down_matrix)
    _, gelu_pull = jax.vjp(gelu_exact, pre)
    pre_grad_low = gelu_pull(act_grad)[0].astype(bf16)
    grad_in = transposed_times(hid_low, pre_grad_low)
    grad_in_b = jnp.sum(pre_grad_low.astype(f32), axis=0)
    att_grad_low = times_transposed(cotangent, out_matrix).astype(bf16).reshape(heads)
    query_grads = []
    key_grad = jnp.zeros(heads, f32)
    value_grad = jnp.zeros(heads, f32)
    for block in range(block_count):
        lower = block * block_rows
        upper = lower + block_rows
        query_block = q_low[lower:upper]
        scores, allowed = block_scores(
            query_block, k_low[:upper], segment[lower:upper], segment[:upper],
            places[lower:upper], places[:upper],
        )
        soft = jnp.where(allowed[None], jnp.exp(scores - kept_lse[block]), 0.0)
        soft_low = soft.astype(bf16)
        out_grad = att_grad_low[lower:upper]
        value_part = jnp.einsum("hqk,qhd->khd", soft_low, out_grad, preferred_element_type=f32)
        prob_grad = jnp.einsum("qhd,khd->hqk", out_grad, v_low[:upper], preferred_element_type=f32)
        score_grad = soft * (prob_grad - jnp.sum(soft * prob_grad, axis=-1, keepdims=True))
        score_low = score_grad.astype(bf16)
        query_grads.append(
            jnp.einsum("hqk,khd->qhd", score_low, k_low[:upper], preferred_element_type=f32)
            * HEAD ** (-0.5)
        )
        key_part = jnp.einsum(
            "hqk,qhd->khd", score_low, query_block, preferred_element_type=f32
        ) * HEAD ** (-0.5)
        padding = ((0, row_count - upper), (0, 0), (0, 0))
        key_grad = key_grad + jnp.pad(key_part, padding)
        value_grad = value_grad + jnp.pad(value_part, padding)
    query_grad = unrotate(jnp.concatenate(query_grads, axis=0), cosine, sine)
    key_grad = unrotate(key_grad, cosine, sine)
    qkv_grad_low = jnp.concatenate(
        [g.reshape(row_count, width) for g in (query_grad, key_grad, value_grad)], axis=1
    ).astype(bf16)
    grad_qkv = transposed_times(hid_low, qkv_grad_low)
    grad_qkv_b = jnp.sum(qkv_grad_low.astype(f32), axis=0)
    hidden_grad = times_transposed(qkv_grad_low, qkv_matrix) + times_transposed(
        pre_grad_low, in_matrix
    )
    grad_gain = jnp.sum(hidden_grad * normed, axis=0)
    grad_shift = jnp.sum(hidden_grad, axis=0)
    scaled = hidden_grad * gain_full
    input_grad = upstream + inverse * (
        scaled
        - jnp.mean(scaled, axis=-1, keepdims=True)
        - normed * jnp.mean(scaled * normed, axis=-1, keepdims=True)
    )
    return (
        mixed, input_grad.astype(bf16), grad_gain, grad_shift, grad_qkv, grad_qkv_b,
        grad_out, grad_sum, grad_in, grad_in_b, grad_down, grad_sum, stream_rms,
    )


def generic(tokens, cotangent, seq_lens, *shards):
    axes = ("wide", "narrow")
    whole = [lax.all_gather(s, axes, axis=0, tiled=True) for s in shards]
    results = layer_math(tokens, cotangent, seq_lens, *whole)
    summed = [
        lax.psum_scatter(g, axes, scatter_dimension=0, tiled=True) for g in results[2:12]
    ]
    return (*results[:2], *summed, results[12])


def local(
    tokens, cotangent, seq_lens, norm_gain, norm_bias, qkv_weight, qkv_bias, out_weight,
    out_bias, fc_in_weight, fc_in_bias, fc_out_weight, fc_out_bias,
):
    in_mixed = fc_in_weight.reshape(32, 32, MC, 16).transpose(0, 2, 1, 3).reshape(32, 4096)
    row0 = jnp.concatenate([norm_gain, norm_bias, out_bias, fc_out_bias])
    small = jnp.zeros((16, 128), bf16)
    small = small.at[0].set(row0).at[1, :96].set(qkv_bias).at[2].set(fc_in_bias)
    ag_q, ag_o, ag_i, ag_d, ag_s = gather_all(
        qkv_weight, out_weight, in_mixed, fc_out_weight, small
    )
    ag_s = ag_s.reshape(32, 16, 128)
    gain, shift, out_b, down_b = (
        ag_s[:, 0, 32 * i : 32 * (i + 1)].reshape(1024) for i in range(4)
    )
    qkv_b = ag_s[:, 1, :96].reshape(3072)
    in_b = ag_s[:, 2].reshape(32, MC, 16).transpose(1, 0, 2).reshape(4096)
    qkv_matrix = (
        ag_q.reshape(QG, 1024, 3, 256).transpose(1, 2, 0, 3).reshape(1024, 3072)
    )
    out_matrix = ag_o.reshape(1024, 1024)
    in_matrix = ag_i.reshape(MC, 1024, 512).transpose(1, 0, 2).reshape(1024, 4096)
    down_matrix = ag_d.reshape(4096, 1024)
    (
        mixed, tokens_grad, g_gain, g_shift, g_qkv, g_qkv_b, g_out, g_sum, g_in, g_in_b,
        g_down, _, stream_rms,
    ) = layer_math(
        tokens, cotangent, seq_lens, gain, shift, qkv_matrix, qkv_b, out_matrix, out_b,
        in_matrix, in_b, down_matrix, down_b,
    )
    ranks = (4, 2, 2, 2)
    gq = (
        g_qkv.astype(bf16)
        .reshape(32, 2, 16, 3, QG, 256)
        .transpose(4, 1, 0, 2, 3, 5)
        .reshape((QG, 2) + ranks + (16, 768))
    )
    go = g_out.astype(bf16).reshape(32, 2, 16, 1024).transpose(1, 0, 2, 3)
    go = go.reshape((2,) + ranks + (16, 1024))
    gi = g_in.astype(bf16).reshape(32, 2, 16, MC, 512).transpose(3, 0, 2, 1, 4)
    gi = gi.reshape((MC,) + ranks + (16, 1024))
    gd = g_down.astype(bf16).reshape((MC,) + ranks + (16, 1024))
    rows = [
        jnp.concatenate([g.reshape(32, 32) for g in (g_gain, g_shift, g_sum, g_sum)], axis=1),
        jnp.pad(g_qkv_b.reshape(32, 96), ((0, 0), (0, 32))),
        g_in_b.reshape(MC, 32, 16).transpose(1, 0, 2).reshape(32, 128),
    ]
    gs = jnp.pad(jnp.stack(rows, axis=1), ((0, 0), (0, 5), (0, 0)))
    out_q, out_o, out_i, out_d, out_s = scatter_all(
        gq, go, gi, gd, gs.reshape(ranks + (8, 128))
    )
    out_i = out_i.reshape(32, MC, 32, 16).transpose(0, 2, 1, 3).reshape(32, 4096)
    return (
        mixed, tokens_grad, out_s[0, :32], out_s[0, 32:64], out_q, out_s[1, :96], out_o,
        out_s[0, 64:96], out_i, out_s[2], out_d, out_s[0, 96:], stream_rms,
    )


def solution(mesh):
    rows, flat = P(("wide", "narrow"), None), P(("wide", "narrow"))
    fits = mesh.shape["wide"] == 8 and mesh.shape["narrow"] == 4
    return jax.shard_map(
        local if fits else generic,
        mesh=mesh,
        in_specs=(rows, rows, rows, flat, flat, rows, flat, rows, flat, rows, flat, rows, flat),
        out_specs=(rows, rows, flat, flat, rows, flat, rows, flat, rows, flat, rows, flat, rows),
        check_vma=False,
    )
```

```python
from functools import partial

import jax
import jax.numpy as jnp
from jax import lax
from jax.experimental import pallas as pl
from jax.experimental.pallas import tpu as pltpu
from jax.sharding import PartitionSpec as P

HEADS = 16
HEAD = 64
ROT = 16
MESH = pl.DeviceIdType.MESH
bf16 = jnp.bfloat16
f32 = jnp.float32
ALL = slice(None)

epsilon = 1e-05


def positions(lengths, count):
    ends = jnp.cumsum(lengths)
    places = jnp.arange(count, dtype=jnp.int32)
    segment = jnp.sum((places[:, None] >= ends[None, :]).astype(jnp.int32), axis=1)
    starts = ends - lengths
    slots = jnp.arange(lengths.shape[0], dtype=jnp.int32)
    begin = jnp.sum(jnp.where(segment[:, None] == slots[None, :], starts[None, :], 0), axis=1)
    return (segment, places, (places - begin).astype(jnp.float32))


def rotate(vector, cosine, sine):
    half = ROT // 2
    first = vector[..., :half]
    second = vector[..., half:ROT]
    return jnp.concatenate(
        [first * cosine - second * sine, second * cosine + first * sine, vector[..., ROT:]], axis=-1
    )


def unrotate(grad, cosine, sine):
    half = ROT // 2
    first = grad[..., :half]
    second = grad[..., half:ROT]
    return jnp.concatenate(
        [first * cosine + second * sine, second * cosine - first * sine, grad[..., ROT:]], axis=-1
    )


def times_transposed(left, right):
    return lax.dot_general(
        left, right, (((1,), (1,)), ((), ())), preferred_element_type=jnp.float32
    )


def transposed_times(left, right):
    return lax.dot_general(
        left, right, (((0,), (0,)), ((), ())), preferred_element_type=jnp.float32
    )


def block_scores(query_block, key_low, seg_query, seg_key, place_query, place_key):
    raw = jnp.einsum(
        "qhd,khd->hqk", query_block, key_low, preferred_element_type=jnp.float32
    ) * HEAD ** (-0.5)
    allowed = (seg_query[:, None] == seg_key[None, :]) & (
        place_key[None, :] <= place_query[:, None]
    )
    return (jnp.where(allowed[None], raw, -1e30), allowed)


QG = 4
LOG2E = 1.4426950408889634
LN2 = 0.6931471805599453
T = 1024
MC = 8


class Place:
    def __init__(self):
        wide, narrow = lax.axis_index("wide"), lax.axis_index("narrow")
        self.z, self.x = wide // 2, wide % 2
        self.y, self.c = narrow // 2, narrow % 2
        self.me = (self.z, self.x, self.y, self.c)
        self.zs = [(self.z + d) % 4 for d in (1, 2, 3)]

    def device(self, z, x, y, c):
        return (z * 2 + x, y * 2 + c)

    def targets(self, axis):
        z, x, y, c = self.me
        if axis == "z":
            return [(i, (other, x, y, c)) for i, other in enumerate(self.zs)]
        return [
            {"x": (3, (z, 1 - x, y, c)), "y": (4, (z, x, 1 - y, c)), "c": (5, (z, x, y, 1 - c))}[axis]
        ]

    def partners(self):
        z, x, y, c = self.me
        return [self.device(p, x, y, c) for p in self.zs] + [
            self.device(z, 1 - x, y, c),
            self.device(z, x, 1 - y, c),
            self.device(z, x, y, 1 - c),
        ]

    def greet(self):
        barrier = pltpu.get_barrier_semaphore()
        for other in self.partners():
            pl.semaphore_signal(barrier, inc=1, device_id=other, device_id_type=MESH)
        pl.semaphore_wait(barrier, 6)


def dg(a, b, ca, cb):
    return lax.dot_general(a, b, (((ca,), (cb,)), ((), ())), preferred_element_type=f32)


def exact(a, b, ca, cb):
    return lax.dot_general(
        a, b, (((ca,), (cb,)), ((), ())), precision=lax.Precision.HIGHEST,
        preferred_element_type=f32,
    )


def remote(src, dst, send, recv, device):
    return pltpu.make_async_remote_copy(
        src_ref=src, dst_ref=dst, send_sem=send, recv_sem=recv,
        device_id=device, device_id_type=MESH,
    )


class Gather:
    def __init__(self, place, view, order, send, recv):
        self.p, self.view, self.axes = place, view, order + "c"
        self.send, self.recv = send, recv

    def copies(self, i):
        me, axis = self.p.me, self.axes[i]
        part = [ALL if a in self.axes[:i] else me["zxyc".index(a)] for a in "zxyc"]
        return [
            remote(
                self.view(*part), self.view(*part), self.send(slot), self.recv(slot),
                self.p.device(*to),
            )
            for slot, to in self.p.targets(axis)
        ]

    def step(self, i):
        if i > 0:
            for copy in self.copies(i - 1):
                copy.wait_recv()
        if i < 4:
            for copy in self.copies(i):
                copy.start()

    def close(self):
        for i in range(4):
            for copy in self.copies(i):
                copy.wait_send()


class Scatter:
    def __init__(self, place, part, bufs, order, send, recv):
        self.p, self.part, self.bufs = place, part, bufs
        self.axes = "c" + order[::-1]
        self.send, self.recv = send, recv

    def index(self, i, value):
        return [
            value if a == self.axes[i] else (self.p.me[k] if a in self.axes[:i] else ALL)
            for k, a in enumerate("zxyc")
        ]

    def landing(self, i):
        buf = self.bufs[i]
        return [buf.at[n] for n in range(3)] if self.axes[i] == "z" else [buf]

    def copies(self, i):
        at = "zxyc".index(self.axes[i])
        return [
            remote(
                self.part(*self.index(i, to[at])), land, self.send(slot), self.recv(slot),
                self.p.device(*to),
            )
            for land, (slot, to) in zip(self.landing(i), self.p.targets(self.axes[i]))
        ]

    def step(self, i):
        if i > 0:
            for copy in self.copies(i - 1):
                copy.wait_recv()
            part = self.part(*self.index(i - 1, self.p.me["zxyc".index(self.axes[i - 1])]))
            for buf in self.landing(i - 1):
                part[...] = part[...] + buf[...]
        for copy in self.copies(i):
            copy.start()

    def total(self):
        for copy in self.copies(3):
            copy.wait_recv()
        out = self.part(*self.p.me)[...].astype(f32)
        for buf in self.landing(3):
            out = out + buf[...].astype(f32)
        for i in range(4):
            for copy in self.copies(i):
                copy.wait_send()
        return out


def begins(ends, t):
    first = jnp.zeros_like(t)
    for e in ends:
        first = jnp.where(t >= e, e, first)
    return first


def tables(ends, cos_ref, up_ref, down_ref):
    t = lax.broadcasted_iota(jnp.int32, (T, 128), 0)
    d = lax.broadcasted_iota(jnp.int32, (T, 128), 1) % 64
    offset = (t - begins(ends, t)).astype(f32)
    freq = jnp.exp((d % 8).astype(f32) * (-2.0 / 16 * 9.210340371976184))
    angle = offset * freq
    cos, sin = jnp.cos(angle), jnp.sin(angle)
    cos_ref[...] = jnp.where(d < 16, cos, 1.0)
    up_ref[...] = jnp.where(d < 8, -sin, 0.0)
    down_ref[...] = jnp.where((d >= 8) & (d < 16), sin, 0.0)


def turn(v, cos, up, down, sign):
    out = []
    for i in range(2):
        w = v[:, 128 * i : 128 * (i + 1)]
        r = pltpu.roll(w, 120, 1) * up + pltpu.roll(w, 8, 1) * down
        out.append(w * cos + r if sign > 0 else w * cos - r)
    return jnp.concatenate(out, axis=1)


def attention_group(flag, hid, g, W, Wo, bias, tabs, bufs, attT, dqkv, pump):
    q_s, k_s, v_s, qT, kT, vT, doT, E, DS, dv, dk, dqT = bufs
    R = 512
    for i in range(T // R):
        rows = pl.ds(i * R, R)
        tb = [t[rows, :] for t in tabs]
        h = hid[rows, :]
        q = turn(dg(h, W(0), 1, 0) + bias(0), *tb, 1) * (LOG2E / 8)
        q = q.astype(bf16)
        q_s[rows, :] = q
        qT[:, rows] = q.T
        k = turn(dg(h, W(1), 1, 0) + bias(1), *tb, 1).astype(bf16)
        k_s[rows, :] = k
        kT[:, rows] = k.T
        v = (dg(h, W(2), 1, 0) + bias(2)).astype(bf16)
        v_s[rows, :] = v
        vT[:, rows] = v.T
    pump(0)
    for i in range(T // R):
        rows = pl.ds(i * R, R)
        do = dg(g[rows, :], Wo, 1, 1).astype(bf16)
        doT[:, rows] = do.T
    head_row = lax.broadcasted_iota(jnp.int32, (256, 256), 0) // 64
    head_lane = lax.broadcasted_iota(jnp.int32, (256, 256), 1) // 64
    causal = lax.broadcasted_iota(jnp.int32, (256, 256), 0) <= lax.broadcasted_iota(
        jnp.int32, (256, 256), 1
    )
    for qb in range(T // 256):
        kk = 256 * (qb + 1)
        cols = pl.ds(256 * qb, 256)

        def head(h):
            hc, hr = pl.ds(h * 256, 256), pl.ds(h * 64, 64)
            s = dg(k_s[0:kk, :], jnp.where(head_row == h, qT[:, cols], 0), 1, 0)
            blocks = [s[256 * b : 256 * (b + 1)] for b in range(qb + 1)]
            blocks[qb] = jnp.where(causal, blocks[qb], -1e30)
            m = jnp.max(blocks[qb], axis=0, keepdims=True)
            for b in range(qb):
                top = jnp.max(blocks[b], axis=0, keepdims=True)
                m = jnp.maximum(m, jnp.where(flag(b, qb), top, -1e30))
            total = None
            for b in range(qb + 1):
                e = jnp.exp2(blocks[b] - (m if b == qb else jnp.where(flag(b, qb), m, 1e30)))
                t = jnp.sum(e, axis=0, keepdims=True)
                total = t if total is None else total + t
                E[256 * b : 256 * (b + 1), hc] = e.astype(bf16)
            inv = 1.0 / total
            oT = dg(vT[hr, 0:kk], E[0:kk, hc], 1, 0) * inv
            attT[hr, cols] = oT.astype(bf16)
            dot = jnp.sum(doT[hr, cols].astype(f32) * oT, axis=0, keepdims=True) * inv
            doz = jnp.where(head_row == h, doT[:, cols].astype(f32) * inv, 0.0).astype(bf16)
            dp = dg(v_s[0:kk, :], doz, 1, 0)
            DS[0:kk, hc] = (E[0:kk, hc].astype(f32) * (dp - dot)).astype(bf16)
            dqT[hr, cols] = dg(kT[hr, 0:kk], DS[0:kk, hc], 1, 0)
            return doz.T

        doz = jnp.concatenate([head(h) for h in range(4)], axis=0)
        q = q_s[cols, :]
        qz = jnp.concatenate([jnp.where(head_lane == h, q, 0) for h in range(4)], axis=0)
        pv = dg(E[0:kk, :], doz, 1, 0)
        pk = dg(DS[0:kk, :], qz, 1, 0)
        if qb > 0:
            dv[0 : 256 * qb, :] += pv[0 : 256 * qb]
            dk[0 : 256 * qb, :] += pk[0 : 256 * qb]
        dv[256 * qb : kk, :] = pv[256 * qb :]
        dk[256 * qb : kk, :] = pk[256 * qb :]
        pump(qb + 1)
    for i in range(T // R):
        rows = pl.ds(i * R, R)
        tb = [t[rows, :] for t in tabs]
        dqkv[rows, 0:256] = turn(dqT[:, rows].T * 0.125, *tb, -1).astype(bf16)
        dqkv[rows, 256:512] = turn(dk[rows, :] * LN2, *tb, -1).astype(bf16)
        dqkv[rows, 512:768] = dv[rows, :].astype(bf16)


def gelu_parts(x):
    a1, a2, a3, a4, a5 = 0.254829592, -0.284496736, 1.421413741, -1.453152027, 1.061405429
    ex = jnp.exp2(x * x * (-0.5 * LOG2E))
    t = 1.0 / (1.0 + (0.3275911 * 0.7071067811865476) * jnp.abs(x))
    half = ((((0.5 * a5 * t + 0.5 * a4) * t + 0.5 * a3) * t + 0.5 * a2) * t + 0.5 * a1) * t * ex
    phi = jnp.where(x < 0, half, 1.0 - half)
    return x * phi, phi + x * ex * 0.3989422804014327


def spread(kind, width):
    lane = lax.broadcasted_iota(jnp.int32, (128, width), 0)
    at = lax.broadcasted_iota(jnp.int32, (128, width), 1)
    col = lax.broadcasted_iota(jnp.int32, (32, width), 1)
    rank = lax.broadcasted_iota(jnp.int32, (32, width), 0)
    if kind == "qkv":
        return lane == at % 96, col // 96 == rank
    if kind == "fc_in":
        return lane == at // 512 * 16 + at % 16, col % 512 // 16 == rank
    return lane == at % 32 + 32 * kind, col // 32 == rank


def from_ranks(rows, kind, width):
    hot, mine = spread(kind, width)
    t = dg(rows, jnp.where(hot, 1.0, 0.0).astype(bf16), 1, 0)
    return jnp.sum(jnp.where(mine, t, 0.0), axis=0, keepdims=True)


def to_ranks(vector, kind, width):
    hot, mine = spread(kind, width)
    return exact(jnp.where(mine, vector, 0.0), jnp.where(hot, 1.0, 0.0), 1, 1)


def normalised(x):
    centred = x - jnp.mean(x, axis=-1, keepdims=True)
    inverse = lax.rsqrt(jnp.mean(centred * centred, axis=-1, keepdims=True) + epsilon)
    return centred * inverse, inverse


NP = 3
NR = 2


def lanes(start, size):
    return pl.ds(pl.multiple_of(start, 128), size)


def layer_kernel(
    lens, tokens, cot, qkv, out, fc_in, down, small,
    mixed, tokens_grad, out_q, out_o, out_i, out_d, out_s, stats,
    ag_q, ag_o, ag_i, ag_d, ag_s,
    hid, hidT, g, hgrad, attT, vecs, gvecs, wide_b, wide_g, sv,
    cos, up, turn_down, wo, wq, wd, dqkv, q_s, k_s, v_s, qT, kT, vT, doT, E, DS, mlp, dqT,
    part, r1, r2, r3, rz, part_s, s1, s2, s3, sz,
    own, io, fetch, send, recv, gsend, grecv,
):
    place = Place()
    me = place.me

    def gather(n, views, orders=("zxy", "zyx")):
        return [
            Gather(place, view, order, lambda s, k=k: gsend.at[n, k, s], lambda s, k=k: grecv.at[n, k, s])
            for k, (view, order) in enumerate(zip(views, orders))
        ]

    def gather_q(i):
        return gather(
            i, [lambda *a, h=h: ag_q.at[(i,) + a + (pl.ds(16 * h, 16),)] for h in range(2)]
        )

    def gather_o():
        return gather(4, [lambda *a, h=h: ag_o.at[a + (pl.ds(16 * h, 16),)] for h in range(2)])

    def gather_m(j):
        return gather(5 + j, [lambda *a: ag_i.at[(j,) + a], lambda *a: ag_d.at[(j,) + a]])

    def step(arrays, i):
        for array in arrays:
            array.step(i)

    vectors = gather(13, [lambda *a: ag_s.at[a]])

    def sums(n, width):
        return [
            Scatter(
                place,
                lambda *a, k=k: part.at[(k, n % NP) + a + (ALL, pl.ds(0, width))],
                [
                    b.at[(k, n % NR) + (ALL,) * d + (ALL, pl.ds(0, width))]
                    for b, d in ((r1, 3), (r2, 2), (r3, 1), (rz, 1))
                ],
                ("zxy", "zyx")[k],
                lambda s, k=k: send.at[n, k, s],
                lambda s, k=k: recv.at[n, k, s],
            )
            for k in range(2)
        ]

    def end_q(i):
        totals = [array.total() for array in sums(i, 768)]
        for h in range(2):
            for j in range(3):
                out_q[pl.ds(16 * h, 16), lanes(1024 * j + 256 * i, 256)] = totals[h][
                    :, 256 * j : 256 * (j + 1)
                ]

    def end_m(n):
        totals = [array.total() for array in sums(n, 1024)]

        @pl.when(n == 4)
        def _():
            for h in range(2):
                out_o[pl.ds(16 * h, 16), :] = totals[h]

        @pl.when(n > 4)
        def _():
            j = jnp.maximum(n - 5, 0)
            for h in range(2):
                out_i[pl.ds(16 * h, 16), lanes(512 * j, 512)] = totals[0][
                    :, 512 * h : 512 * (h + 1)
                ]
            out_d[pl.ds(pl.multiple_of(16 * j, 16), 16), :] = totals[1]

    own_copies = []

    def own_copy(src, dst):
        copy = pltpu.make_async_copy(src, dst, own.at[len(own_copies)])
        copy.start()
        own_copies.append(copy)
        return copy

    own_copy(small, ag_s.at[me])
    for i in range(QG):
        for j in range(3):
            own_copy(
                qkv.at[:, pl.ds(1024 * j + 256 * i, 256)],
                ag_q.at[(i,) + me + (ALL, pl.ds(256 * j, 256))],
            )
        if i == 0:
            own_copy(out, ag_o.at[me])
    for j in range(MC):
        own_copy(fc_in.at[:, pl.ds(512 * j, 512)], ag_i.at[(j,) + me])
        own_copy(down.at[pl.ds(16 * j, 16)], ag_d.at[(j,) + me])
    load_x = pltpu.make_async_copy(tokens, attT, io.at[0])
    load_x.start()
    load_g = pltpu.make_async_copy(cot, g, io.at[1])
    load_g.start()
    place.greet()
    own_copies[0].wait()
    step(vectors, 0)
    for copy in own_copies[1:5]:
        copy.wait()
    q0, o = gather_q(0), gather_o()
    step(q0, 0)
    step(o, 0)
    for copy in own_copies[5:]:
        copy.wait()
    ends = [lens[0, 0], lens[0, 0] + lens[0, 1], lens[0, 0] + lens[0, 1] + lens[0, 2]]

    def flag(b, qb):
        return 256 * b >= begins(ends, jnp.full((1, 256), 256 * qb, jnp.int32))

    tables(ends, cos, up, turn_down)
    step(vectors, 1)
    step(q0, 1)
    step(vectors, 2)
    step(gather_q(1), 0)
    step(vectors, 3)
    step(o, 1)
    step(vectors, 4)
    load_s = pltpu.make_async_copy(ag_s, sv, io.at[2])
    load_s.start()
    step(q0, 2)
    load_s.wait()
    rows = sv[...].reshape(32, 8, 128)
    row0, row1, row2 = (rows[:, i, :].astype(bf16) for i in range(3))
    for i in range(4):
        vecs[i : i + 1, :] = from_ranks(row0, i, 1024)
    wide_b[0:1, 0:3072] = from_ranks(row1, "qkv", 3072)
    wide_b[1:2, :] = from_ranks(row2, "fc_in", 4096)
    step(o, 2)
    step(gather_m(0), 0)
    step(gather_m(1), 0)
    step(q0, 3)
    load_x.wait()
    for i in range(4):
        rows = pl.ds(256 * i, 256)
        normed, _ = normalised(attT[rows, :].astype(f32))
        h = (normed * vecs[0:1, :] + vecs[1:2, :]).astype(bf16)
        hid[rows, :] = h
        hidT[:, rows] = h.T
    hgrad[...] = jnp.zeros_like(hgrad)
    step(q0, 4)

    def fetch_q(i):
        return pltpu.make_async_copy(ag_q.at[i], wq.at[i % 2], fetch.at[i % 2])

    fetch_q(0).start()
    step(o, 3)
    step(o, 4)
    fetch_o = pltpu.make_async_copy(ag_o, wo, fetch.at[2])
    fetch_o.start()
    load_g.wait()
    fetch_o.wait()

    bufs = (
        q_s, k_s, v_s, qT, kT, vT, doT, E, DS,
        mlp.at[:, pl.ds(0, 256)], mlp.at[:, pl.ds(256, 256)], dqT,
    )

    def attention_step(i, carry):
        fetch_q(i).wait()
        more, before = i < QG - 1, i > 0
        a, b = gather_m(2 * i), gather_m(2 * i + 1)

        @pl.when(more)
        def _():
            step(gather_q(i + 1), 1)

            @pl.when(i < QG - 2)
            def _():
                step(gather_q(i + 2), 0)

        step(a, 1)

        def pump(p):
            if p == 0:
                step(b, 1)

                @pl.when(before)
                def _():
                    step(sums(i - 1, 768), 1)

                @pl.when(more)
                def _():
                    step(gather_m(2 * i + 2), 0)

            elif p == 1:

                @pl.when(more)
                def _():
                    step(gather_q(i + 1), 2)
                    step(gather_m(2 * i + 3), 0)

            elif p == 2:
                step(a, 2)

                @pl.when(before)
                def _():
                    step(sums(i - 1, 768), 2)

            elif p == 3:

                @pl.when(more)
                def _():
                    step(gather_q(i + 1), 3)

                step(b, 2)
            elif p == 4:
                step(a, 3)

                @pl.when(more)
                def _():
                    step(gather_q(i + 1), 4)
                    fetch_q(i + 1).start()

                @pl.when(before)
                def _():
                    step(sums(i - 1, 768), 3)

            elif p == 5:
                step(b, 3)
            else:
                step(a, 4)
                step(b, 4)

                @pl.when(before)
                def _():
                    end_q(i - 1)

        def W(j):
            return wq[i % 2, :, :, :, :, :, 256 * j : 256 * (j + 1)].reshape(T, 256)

        def bias(j):
            return wide_b[0:1, lanes(1024 * j + 256 * i, 256)]

        attention_group(
            flag, hid, g, W, wo[i].reshape(256, T), bias, (cos, up, turn_down), bufs,
            attT.at[pl.ds(pl.multiple_of(256 * i, 256), 256)], dqkv, pump,
        )
        for b_ in range(2):
            v = dg(hidT[512 * b_ : 512 * (b_ + 1), :], dqkv[...], 1, 0).astype(bf16)
            v = v.reshape(2, 2, 2, 2, 2, 16, 768)
            for h in range(2):
                part[h, i % NP, 2 * b_ : 2 * b_ + 2, :, :, :, :, 0:768] = v[:, :, :, :, h]
        step(sums(i, 768), 0)
        pump(5)
        total = jnp.sum(dqkv[...].astype(f32), axis=0, keepdims=True)
        for j in range(3):
            wide_g[0:1, lanes(1024 * j + 256 * i, 256)] = total[:, 256 * j : 256 * (j + 1)]
        whole_w = wq[i % 2].reshape(T, 768)
        for b_ in range(2):
            rows = pl.ds(512 * b_, 512)
            hgrad[rows, :] += dg(dqkv[rows, :], whole_w, 1, 1)
        pump(6)
        return carry

    lax.fori_loop(0, QG, attention_step, 0)

    def fetch_m(j):
        return [
            pltpu.make_async_copy(
                ag_i.at[j], wq.at[j % 2, :, :, :, :, :, pl.ds(0, 512)], fetch.at[j % 2]
            ),
            pltpu.make_async_copy(ag_d.at[j], wd.at[j % 2], fetch.at[2 + j % 2]),
        ]

    for copy in fetch_m(0):
        copy.start()
    step(sums(3, 768), 1)
    for b in range(2):
        v = dg(attT[512 * b : 512 * (b + 1), :], g[...], 1, 0).astype(bf16)
        v = v.reshape(2, 2, 2, 2, 2, 16, T)
        for h in range(2):
            part[h, 4 % NP, 2 * b : 2 * b + 2] = v[:, :, :, :, h]
    step(sums(4, 1024), 0)
    step(sums(3, 768), 2)
    step(sums(4, 1024), 1)
    step(sums(3, 768), 3)
    mlp[...] = jnp.zeros_like(mlp)
    end_q(3)

    act, pg = DS.at[:, pl.ds(0, 512)], DS.at[:, pl.ds(512, 512)]

    def mlp_step(j, carry):
        for copy in fetch_m(j):
            copy.wait()

        @pl.when(j < MC - 1)
        def _():
            for copy in fetch_m(j + 1):
                copy.start()

        w_in = wq[j % 2, :, :, :, :, :, 0:512].reshape(T, 512)
        w_down = wd[j % 2].reshape(512, T)
        bias = wide_b[1:2, lanes(512 * j, 512)]
        for b in range(2):
            rows = pl.ds(512 * b, 512)
            pre = dg(hid[rows, :], w_in, 1, 0) + bias
            a, d = gelu_parts(pre)
            act[rows, :] = a.astype(bf16)
            pg[rows, :] = (dg(g[rows, :], w_down, 1, 1) * d).astype(bf16)
        wide_g[1:2, lanes(512 * j, 512)] = jnp.sum(pg[...].astype(f32), axis=0, keepdims=True)

        @pl.when(j > 0)
        def _():
            end_m(j + 3)

        slot = (j + 5) % NP
        for b in range(2):
            v = dg(hidT[512 * b : 512 * (b + 1), :], pg[...], 1, 0).astype(bf16)
            v = v.reshape(2, 2, 2, 2, 2, 16, 512)
            for h in range(2):
                part[0, slot, 2 * b : 2 * b + 2, :, :, :, :, 512 * h : 512 * (h + 1)] = v[
                    :, :, :, :, h
                ]
            v = dg(act[:, 256 * b : 256 * (b + 1)], g[...], 0, 0).astype(bf16)
            part[1, slot, 2 * b : 2 * b + 2] = v.reshape(2, 2, 2, 2, 16, T)
        step(sums(j + 5, 1024), 0)
        step(sums(j + 4, 1024), 2)
        for b in range(2):
            rows = pl.ds(512 * b, 512)
            mlp[rows, :] += dg(act[rows, :], w_down, 1, 0)
            hgrad[rows, :] += dg(pg[rows, :], w_in, 1, 1)
        step(sums(j + 5, 1024), 1)
        step(sums(j + 4, 1024), 3)
        return carry

    lax.fori_loop(0, MC, mlp_step, 0)

    last = MC + 4
    reload_x = pltpu.make_async_copy(tokens, hid, io.at[0])
    reload_x.start()
    reload_x.wait()
    for i in range(4):
        rows = pl.ds(256 * i, 256)
        normed, inverse = normalised(hid[rows, :].astype(f32))
        h = hgrad[rows, :]
        up_g = g[rows, :].astype(f32)
        for k, v in enumerate((h * normed, h, up_g)):
            v = jnp.sum(v, axis=0, keepdims=True)
            gvecs[k : k + 1, :] = v if i == 0 else gvecs[k : k + 1, :] + v
        n = h * vecs[0:1, :]
        d = n - jnp.mean(n, axis=-1, keepdims=True)
        d = d - normed * jnp.mean(n * normed, axis=-1, keepdims=True)
        hidT[rows, :] = (up_g + inverse * d).astype(bf16)
    put_tg = pltpu.make_async_copy(hidT, tokens_grad, io.at[1])
    put_tg.start()
    step(sums(last, 1024), 2)
    end_m(jnp.int32(last - 1))
    row0 = sum(to_ranks(gvecs[min(k, 2) : min(k, 2) + 1, :], k, 1024) for k in range(4))
    row1 = to_ranks(wide_g[0:1, 0:3072], "qkv", 3072)
    row2 = to_ranks(wide_g[1:2, :], "fc_in", 4096)
    for r in range(32):
        part_s[r // 8, r // 4 % 2, r // 2 % 2, r % 2] = jnp.concatenate(
            [row0[r : r + 1], row1[r : r + 1], row2[r : r + 1], jnp.zeros((5, 128), f32)]
        )
    tiny = Scatter(
        place, lambda *a: part_s.at[a], [s1, s2, s3, sz], "zxy",
        lambda s: send.at[13, 0, s], lambda s: recv.at[13, 0, s],
    )
    tiny.step(0)
    step(sums(last, 1024), 3)
    tiny.step(1)
    w_out = wo[...].reshape(T, T)
    squares = [jnp.zeros((1, T), f32)] * 3
    for i in range(4):
        rows = pl.ds(256 * i, 256)
        x = hid[rows, :].astype(f32)
        a = dg(attT[:, rows], w_out, 0, 0) + vecs[2:3, :]
        m = mlp[rows, :] + vecs[3:4, :]
        hid[rows, :] = (x + a + m).astype(bf16)
        squares = [
            s + jnp.sum(v * v, axis=0, keepdims=True) for s, v in zip(squares, (x, a, m))
        ]
        if i == 1:
            tiny.step(2)
    put_mixed = pltpu.make_async_copy(hid, mixed, io.at[0])
    put_mixed.start()
    tiny.step(3)
    for i in range(3):
        total = jnp.sum(squares[i], axis=1, keepdims=True)
        stats[i : i + 1, :] = jnp.broadcast_to(total, (1, 128))
    end_m(jnp.int32(last))
    out_s[...] = tiny.total()
    put_tg.wait()
    put_mixed.wait()
    for arrays in [vectors, o] + [gather_q(i) for i in range(QG)]:
        for array in arrays:
            array.close()

    def close_m(j, carry):
        for array in gather_m(j):
            array.close()
        return carry

    lax.fori_loop(0, MC, close_m, 0)


def whole_layer(lens, tokens, cot, qkv, out, fc_in, down, small):
    any_ = pl.BlockSpec(memory_space=pl.ANY)
    vmem = pl.BlockSpec(memory_space=pltpu.VMEM)
    sd = jax.ShapeDtypeStruct
    ranks = (4, 2, 2, 2)
    dma = pltpu.SemaphoreType.DMA
    return pl.pallas_call(
        layer_kernel,
        out_shape=[
            sd((T, T), bf16),
            sd((T, T), bf16),
            sd((32, 3072), f32),
            sd((32, 1024), f32),
            sd((32, 4096), f32),
            sd((128, 1024), f32),
            sd((8, 128), f32),
            sd((8, 128), f32),
            sd((QG,) + ranks + (32, 768), bf16),
            sd(ranks + (32, 1024), bf16),
            sd((MC,) + ranks + (32, 512), bf16),
            sd((MC,) + ranks + (16, 1024), bf16),
            sd(ranks + (8, 128), f32),
        ],
        in_specs=[pl.BlockSpec(memory_space=pltpu.SMEM)] + [any_] * 7,
        out_specs=[any_] * 2 + [vmem] * 6 + [any_] * 5,
        scratch_shapes=[
            pltpu.VMEM((T, T), bf16),
            pltpu.VMEM((T, T), bf16),
            pltpu.VMEM((T, T), bf16),
            pltpu.VMEM((T, T), f32),
            pltpu.VMEM((T, T), bf16),
            pltpu.VMEM((8, 1024), f32),
            pltpu.VMEM((8, 1024), f32),
            pltpu.VMEM((8, 4096), f32),
            pltpu.VMEM((8, 4096), f32),
            pltpu.VMEM(ranks + (8, 128), f32),
            pltpu.VMEM((T, 128), f32),
            pltpu.VMEM((T, 128), f32),
            pltpu.VMEM((T, 128), f32),
            pltpu.VMEM(ranks + (32, 1024), bf16),
            pltpu.VMEM((2,) + ranks + (32, 768), bf16),
            pltpu.VMEM((2,) + ranks + (16, 1024), bf16),
            pltpu.VMEM((T, 768), bf16),
            pltpu.VMEM((T, 256), bf16),
            pltpu.VMEM((T, 256), bf16),
            pltpu.VMEM((T, 256), bf16),
            pltpu.VMEM((256, T), bf16),
            pltpu.VMEM((256, T), bf16),
            pltpu.VMEM((256, T), bf16),
            pltpu.VMEM((256, T), bf16),
            pltpu.VMEM((T, T), bf16),
            pltpu.VMEM((T, T), bf16),
            pltpu.VMEM((T, T), f32),
            pltpu.VMEM((256, T), f32),
            pltpu.VMEM((2, NP) + ranks + (16, 1024), bf16),
            pltpu.VMEM((2, NR, 4, 2, 2, 16, 1024), bf16),
            pltpu.VMEM((2, NR, 4, 2, 16, 1024), bf16),
            pltpu.VMEM((2, NR, 4, 16, 1024), bf16),
            pltpu.VMEM((2, NR, 3, 16, 1024), bf16),
            pltpu.VMEM(ranks + (8, 128), f32),
            pltpu.VMEM((4, 2, 2, 8, 128), f32),
            pltpu.VMEM((4, 2, 8, 128), f32),
            pltpu.VMEM((4, 8, 128), f32),
            pltpu.VMEM((3, 8, 128), f32),
            dma((30,)),
            dma((3,)),
            dma((4,)),
            dma((14, 2, 6)),
            dma((14, 2, 6)),
            dma((14, 2, 6)),
            dma((14, 2, 6)),
        ],
        compiler_params=pltpu.CompilerParams(
            collective_id=0, has_side_effects=True, vmem_limit_bytes=63 * 2**20
        ),
    )(lens, tokens, cot, qkv, out, fc_in, down, small)


def layer_math(
    tokens, cotangent, seq_lens, gain, shift, qkv_matrix, qkv_b, out_matrix, out_b,
    in_matrix, in_b, down_matrix, down_b,
):
    gain_full, shift_full = gain.astype(f32), shift.astype(f32)
    row_count, width = tokens.shape
    inputs = tokens.astype(f32)
    centred = inputs - jnp.mean(inputs, axis=-1, keepdims=True)
    inverse = lax.rsqrt(jnp.mean(centred * centred, axis=-1, keepdims=True) + epsilon)
    normed = centred * inverse
    hid_low = (normed * gain_full + shift_full).astype(bf16)
    qkv = jnp.dot(hid_low, qkv_matrix, preferred_element_type=f32) + qkv_b.astype(f32)
    segment, places, offset = positions(seq_lens[0], row_count)
    freqs = 10000.0 ** (-jnp.arange(ROT // 2, dtype=f32) * 2.0 / ROT)
    angle = offset[:, None] * freqs[None, :]
    cosine = jnp.cos(angle)[:, None, :]
    sine = jnp.sin(angle)[:, None, :]
    heads = (row_count, HEADS, HEAD)
    q_low = rotate(qkv[:, :width].reshape(heads), cosine, sine).astype(bf16)
    k_low = rotate(qkv[:, width : 2 * width].reshape(heads), cosine, sine).astype(bf16)
    v_low = qkv[:, 2 * width :].reshape(heads).astype(bf16)
    block_rows = min(512, row_count)
    block_count = row_count // block_rows
    outputs = []
    kept_lse = []
    for block in range(block_count):
        lower = block * block_rows
        upper = lower + block_rows
        scores, allowed = block_scores(
            q_low[lower:upper], k_low[:upper], segment[lower:upper], segment[:upper],
            places[lower:upper], places[:upper],
        )
        row_max = jnp.max(scores, axis=-1, keepdims=True)
        expo = jnp.exp(scores - row_max)
        totals = jnp.sum(expo, axis=-1, keepdims=True)
        soft_low = (expo / totals).astype(bf16)
        kept_lse.append(row_max + jnp.log(totals))
        outputs.append(
            jnp.einsum("hqk,khd->qhd", soft_low, v_low[:upper], preferred_element_type=f32)
        )
    att_low = jnp.concatenate(outputs, axis=0).reshape(row_count, width).astype(bf16)
    attn_out = jnp.dot(att_low, out_matrix, preferred_element_type=f32) + out_b.astype(f32)
    pre = jnp.dot(hid_low, in_matrix, preferred_element_type=f32) + in_b.astype(f32)
    gelu_exact = partial(jax.nn.gelu, approximate=False)
    act_low = gelu_exact(pre).astype(bf16)
    mlp = jnp.dot(act_low, down_matrix, preferred_element_type=f32) + down_b.astype(f32)
    mixed = (inputs + attn_out + mlp).astype(bf16)
    stream_rms = jnp.sqrt(
        jnp.stack([jnp.mean(inputs * inputs), jnp.mean(attn_out * attn_out), jnp.mean(mlp * mlp)])
    )[None, :]
    upstream = cotangent.astype(f32)
    grad_down = transposed_times(act_low, cotangent)
    grad_out = transposed_times(att_low, cotangent)
    grad_sum = jnp.sum(upstream, axis=0)
    act_grad = times_transposed(cotangent, down_matrix)
    _, gelu_pull = jax.vjp(gelu_exact, pre)
    pre_grad_low = gelu_pull(act_grad)[0].astype(bf16)
    grad_in = transposed_times(hid_low, pre_grad_low)
    grad_in_b = jnp.sum(pre_grad_low.astype(f32), axis=0)
    att_grad_low = times_transposed(cotangent, out_matrix).astype(bf16).reshape(heads)
    query_grads = []
    key_grad = jnp.zeros(heads, f32)
    value_grad = jnp.zeros(heads, f32)
    for block in range(block_count):
        lower = block * block_rows
        upper = lower + block_rows
        query_block = q_low[lower:upper]
        scores, allowed = block_scores(
            query_block, k_low[:upper], segment[lower:upper], segment[:upper],
            places[lower:upper], places[:upper],
        )
        soft = jnp.where(allowed[None], jnp.exp(scores - kept_lse[block]), 0.0)
        soft_low = soft.astype(bf16)
        out_grad = att_grad_low[lower:upper]
        value_part = jnp.einsum("hqk,qhd->khd", soft_low, out_grad, preferred_element_type=f32)
        prob_grad = jnp.einsum("qhd,khd->hqk", out_grad, v_low[:upper], preferred_element_type=f32)
        score_grad = soft * (prob_grad - jnp.sum(soft * prob_grad, axis=-1, keepdims=True))
        score_low = score_grad.astype(bf16)
        query_grads.append(
            jnp.einsum("hqk,khd->qhd", score_low, k_low[:upper], preferred_element_type=f32)
            * HEAD ** (-0.5)
        )
        key_part = jnp.einsum(
            "hqk,qhd->khd", score_low, query_block, preferred_element_type=f32
        ) * HEAD ** (-0.5)
        padding = ((0, row_count - upper), (0, 0), (0, 0))
        key_grad = key_grad + jnp.pad(key_part, padding)
        value_grad = value_grad + jnp.pad(value_part, padding)
    query_grad = unrotate(jnp.concatenate(query_grads, axis=0), cosine, sine)
    key_grad = unrotate(key_grad, cosine, sine)
    qkv_grad_low = jnp.concatenate(
        [g.reshape(row_count, width) for g in (query_grad, key_grad, value_grad)], axis=1
    ).astype(bf16)
    grad_qkv = transposed_times(hid_low, qkv_grad_low)
    grad_qkv_b = jnp.sum(qkv_grad_low.astype(f32), axis=0)
    hidden_grad = times_transposed(qkv_grad_low, qkv_matrix) + times_transposed(
        pre_grad_low, in_matrix
    )
    grad_gain = jnp.sum(hidden_grad * normed, axis=0)
    grad_shift = jnp.sum(hidden_grad, axis=0)
    scaled = hidden_grad * gain_full
    input_grad = upstream + inverse * (
        scaled
        - jnp.mean(scaled, axis=-1, keepdims=True)
        - normed * jnp.mean(scaled * normed, axis=-1, keepdims=True)
    )
    return (
        mixed, input_grad.astype(bf16), grad_gain, grad_shift, grad_qkv, grad_qkv_b,
        grad_out, grad_sum, grad_in, grad_in_b, grad_down, grad_sum, stream_rms,
    )


def generic(tokens, cotangent, seq_lens, *shards):
    axes = ("wide", "narrow")
    whole = [lax.all_gather(s, axes, axis=0, tiled=True) for s in shards]
    results = layer_math(tokens, cotangent, seq_lens, *whole)
    summed = [
        lax.psum_scatter(g, axes, scatter_dimension=0, tiled=True) for g in results[2:12]
    ]
    return (*results[:2], *summed, results[12])


def local(
    tokens, cotangent, seq_lens, norm_gain, norm_bias, qkv_weight, qkv_bias, out_weight,
    out_bias, fc_in_weight, fc_in_bias, fc_out_weight, fc_out_bias,
):
    in_mixed = fc_in_weight.reshape(32, 32, MC, 16).transpose(0, 2, 1, 3).reshape(32, 4096)
    row0 = jnp.concatenate([norm_gain, norm_bias, out_bias, fc_out_bias])
    row1 = jnp.pad(qkv_bias, (0, 32))
    small = jnp.stack([row0, row1, fc_in_bias] + [jnp.zeros_like(row0)] * 5).astype(f32)
    mixed, tokens_grad, out_q, out_o, out_i, out_d, out_s, stats, *_ = whole_layer(
        seq_lens, tokens, cotangent, qkv_weight, out_weight, in_mixed, fc_out_weight, small
    )
    out_i = out_i.reshape(32, MC, 32, 16).transpose(0, 2, 1, 3).reshape(32, 4096)
    stream_rms = jnp.sqrt(stats[0:3, 0] / (tokens.shape[0] * tokens.shape[1]))[None, :]
    return (
        mixed, tokens_grad, out_s[0, :32], out_s[0, 32:64], out_q, out_s[1, :96], out_o,
        out_s[0, 64:96], out_i, out_s[2], out_d, out_s[0, 96:], stream_rms,
    )


def solution(mesh):
    rows, flat = P(("wide", "narrow"), None), P(("wide", "narrow"))
    fits = mesh.shape["wide"] == 8 and mesh.shape["narrow"] == 4
    return jax.shard_map(
        local if fits else generic,
        mesh=mesh,
        in_specs=(rows, rows, rows, flat, flat, rows, flat, rows, flat, rows, flat, rows, flat),
        out_specs=(rows, rows, flat, flat, rows, flat, rows, flat, rows, flat, rows, flat, rows),
        check_vma=False,
    )
```

```python
import itertools
from functools import partial

import jax
import jax.numpy as jnp
from jax import lax
from jax.experimental import pallas as pl
from jax.experimental.pallas import tpu as pltpu
from jax.sharding import PartitionSpec as P

HEADS = 16
HEAD = 64
ROT = 16
MESH = pl.DeviceIdType.MESH
bf16 = jnp.bfloat16
f32 = jnp.float32
ALL = slice(None)

epsilon = 1e-05


def positions(lengths, count):
    ends = jnp.cumsum(lengths)
    places = jnp.arange(count, dtype=jnp.int32)
    segment = jnp.sum((places[:, None] >= ends[None, :]).astype(jnp.int32), axis=1)
    starts = ends - lengths
    slots = jnp.arange(lengths.shape[0], dtype=jnp.int32)
    begin = jnp.sum(jnp.where(segment[:, None] == slots[None, :], starts[None, :], 0), axis=1)
    return (segment, places, (places - begin).astype(jnp.float32))


def rotate(vector, cosine, sine):
    half = ROT // 2
    first = vector[..., :half]
    second = vector[..., half:ROT]
    return jnp.concatenate(
        [first * cosine - second * sine, second * cosine + first * sine, vector[..., ROT:]], axis=-1
    )


def unrotate(grad, cosine, sine):
    half = ROT // 2
    first = grad[..., :half]
    second = grad[..., half:ROT]
    return jnp.concatenate(
        [first * cosine + second * sine, second * cosine - first * sine, grad[..., ROT:]], axis=-1
    )


def times_transposed(left, right):
    return lax.dot_general(
        left, right, (((1,), (1,)), ((), ())), preferred_element_type=jnp.float32
    )


def transposed_times(left, right):
    return lax.dot_general(
        left, right, (((0,), (0,)), ((), ())), preferred_element_type=jnp.float32
    )


def block_scores(query_block, key_low, seg_query, seg_key, place_query, place_key):
    raw = jnp.einsum(
        "qhd,khd->hqk", query_block, key_low, preferred_element_type=jnp.float32
    ) * HEAD ** (-0.5)
    allowed = (seg_query[:, None] == seg_key[None, :]) & (
        place_key[None, :] <= place_query[:, None]
    )
    return (jnp.where(allowed[None], raw, -1e30), allowed)


QG = 4
LOG2E = 1.4426950408889634
LN2 = 0.6931471805599453
T = 1024
MC = 8


class Place:
    def __init__(self):
        wide, narrow = lax.axis_index("wide"), lax.axis_index("narrow")
        self.z, self.x = wide // 2, wide % 2
        self.y, self.c = narrow // 2, narrow % 2
        self.me = (self.z, self.x, self.y, self.c)
        self.zs = [(self.z + d) % 4 for d in (1, 2, 3)]

    def device(self, z, x, y, c):
        return (z * 2 + x, y * 2 + c)

    def targets(self, axis):
        z, x, y, c = self.me
        if axis == "z":
            return [(i, (other, x, y, c)) for i, other in enumerate(self.zs)]
        return [
            {"x": (3, (z, 1 - x, y, c)), "y": (4, (z, x, 1 - y, c)), "c": (5, (z, x, y, 1 - c))}[axis]
        ]

    def partners(self):
        z, x, y, c = self.me
        return [self.device(p, x, y, c) for p in self.zs] + [
            self.device(z, 1 - x, y, c),
            self.device(z, x, 1 - y, c),
            self.device(z, x, y, 1 - c),
        ]

    def greet(self):
        barrier = pltpu.get_barrier_semaphore()
        for other in self.partners():
            pl.semaphore_signal(barrier, inc=1, device_id=other, device_id_type=MESH)
        pl.semaphore_wait(barrier, 6)


def dg(a, b, ca, cb):
    return lax.dot_general(a, b, (((ca,), (cb,)), ((), ())), preferred_element_type=f32)


def exact(a, b, ca, cb):
    return lax.dot_general(
        a, b, (((ca,), (cb,)), ((), ())), precision=lax.Precision.HIGHEST,
        preferred_element_type=f32,
    )


def remote(src, dst, send, recv, device):
    return pltpu.make_async_remote_copy(
        src_ref=src, dst_ref=dst, send_sem=send, recv_sem=recv,
        device_id=device, device_id_type=MESH,
    )


class Gather:
    def __init__(self, place, view, order, send, recv):
        self.p, self.view, self.axes = place, view, order + "c"
        self.send, self.recv = send, recv

    def copies(self, i):
        me, axis = self.p.me, self.axes[i]
        part = [ALL if a in self.axes[:i] else me["zxyc".index(a)] for a in "zxyc"]
        return [
            remote(
                self.view(*part), self.view(*part), self.send(slot), self.recv(slot),
                self.p.device(*to),
            )
            for slot, to in self.p.targets(axis)
        ]

    def step(self, i):
        if i > 0:
            for copy in self.copies(i - 1):
                copy.wait_recv()
        if i < 4:
            for copy in self.copies(i):
                copy.start()

    def close(self):
        for i in range(4):
            for copy in self.copies(i):
                copy.wait_send()


class Scatter:
    def __init__(self, place, part, bufs, order, send, recv):
        self.p, self.part, self.bufs = place, part, bufs
        self.axes = "c" + order[::-1]
        self.send, self.recv = send, recv

    def index(self, i, value):
        return [
            value if a == self.axes[i] else (self.p.me[k] if a in self.axes[:i] else ALL)
            for k, a in enumerate("zxyc")
        ]

    def landing(self, i):
        buf = self.bufs[i]
        return [buf.at[n] for n in range(3)] if self.axes[i] == "z" else [buf]

    def copies(self, i):
        at = "zxyc".index(self.axes[i])
        return [
            remote(
                self.part(*self.index(i, to[at])), land, self.send(slot), self.recv(slot),
                self.p.device(*to),
            )
            for land, (slot, to) in zip(self.landing(i), self.p.targets(self.axes[i]))
        ]

    def step(self, i):
        if i > 0:
            for copy in self.copies(i - 1):
                copy.wait_recv()
            part = self.part(*self.index(i - 1, self.p.me["zxyc".index(self.axes[i - 1])]))
            for buf in self.landing(i - 1):
                for at in itertools.product(*(range(n) for n in buf.shape[:-2])):
                    part[at] = part[at] + buf[at]
        for copy in self.copies(i):
            copy.start()

    def total(self):
        for copy in self.copies(3):
            copy.wait_recv()
        out = self.part(*self.p.me)[...].astype(f32)
        for buf in self.landing(3):
            out = out + buf[...].astype(f32)
        for i in range(4):
            for copy in self.copies(i):
                copy.wait_send()
        return out


def begins(ends, t):
    first = jnp.zeros_like(t)
    for e in ends:
        first = jnp.where(t >= e, e, first)
    return first


def tables(ends, cos_ref, sin_ref):
    t = lax.broadcasted_iota(jnp.int32, (T, 128), 0)
    d = lax.broadcasted_iota(jnp.int32, (T, 128), 1) % 64
    offset = (t - begins(ends, t)).astype(f32)
    freq = jnp.exp((d % 8).astype(f32) * (-2.0 / 16 * 9.210340371976184))
    angle = offset * freq
    cos_ref[...] = jnp.where(d < 16, jnp.cos(angle), 1.0)
    sin_ref[...] = jnp.where(d < 16, jnp.where(d < 8, -1.0, 1.0) * jnp.sin(angle), 0.0)


def turn(v, cos, sin, sign):
    first = lax.broadcasted_iota(jnp.int32, cos.shape, 1) % 64 < 8
    out = []
    for i in range(2):
        w = v[:, 128 * i : 128 * (i + 1)]
        r = jnp.where(first, pltpu.roll(w, 120, 1), pltpu.roll(w, 8, 1)) * sin
        out.append(w * cos + r if sign > 0 else w * cos - r)
    return jnp.concatenate(out, axis=1)


def attention_group(flag, hid, g, W, Wo, bias, tabs, bufs, attT, dqkv, pump):
    q_s, k_s, v_s, qT, kT, vT, doT, E, DS, dv, dk, dqT = bufs
    R = 512
    for i in range(T // R):
        rows = pl.ds(i * R, R)
        tb = [t[rows, :] for t in tabs]
        h = hid[rows, :]
        q = turn(dg(h, W(0), 1, 0) + bias(0), *tb, 1) * (LOG2E / 8)
        q = q.astype(bf16)
        q_s[rows, :] = q
        qT[:, rows] = q.T
        k = turn(dg(h, W(1), 1, 0) + bias(1), *tb, 1).astype(bf16)
        k_s[rows, :] = k
        kT[:, rows] = k.T
        v = (dg(h, W(2), 1, 0) + bias(2)).astype(bf16)
        v_s[rows, :] = v
        vT[:, rows] = v.T
    pump(0)
    for i in range(T // R):
        rows = pl.ds(i * R, R)
        do = dg(g[rows, :], Wo, 1, 1).astype(bf16)
        doT[:, rows] = do.T
    head_row = lax.broadcasted_iota(jnp.int32, (256, 256), 0) // 64
    head_lane = lax.broadcasted_iota(jnp.int32, (256, 256), 1) // 64
    causal = lax.broadcasted_iota(jnp.int32, (256, 256), 0) <= lax.broadcasted_iota(
        jnp.int32, (256, 256), 1
    )
    for qb in range(T // 256):
        kk = 256 * (qb + 1)
        cols = pl.ds(256 * qb, 256)

        def head(h):
            hc, hr = pl.ds(h * 256, 256), pl.ds(h * 64, 64)
            s = dg(k_s[0:kk, :], jnp.where(head_row == h, qT[:, cols], 0), 1, 0)
            blocks = [s[256 * b : 256 * (b + 1)] for b in range(qb + 1)]
            blocks[qb] = jnp.where(causal, blocks[qb], -1e30)
            m = jnp.max(blocks[qb], axis=0, keepdims=True)
            for b in range(qb):
                top = jnp.max(blocks[b], axis=0, keepdims=True)
                m = jnp.maximum(m, jnp.where(flag(b, qb), top, -1e30))
            total = None
            for b in range(qb + 1):
                e = jnp.exp2(blocks[b] - (m if b == qb else jnp.where(flag(b, qb), m, 1e30)))
                t = jnp.sum(e, axis=0, keepdims=True)
                total = t if total is None else total + t
                E[256 * b : 256 * (b + 1), hc] = e.astype(bf16)
            inv = 1.0 / total
            oT = dg(vT[hr, 0:kk], E[0:kk, hc], 1, 0) * inv
            attT[hr, cols] = oT.astype(bf16)
            dot = jnp.sum(doT[hr, cols].astype(f32) * oT, axis=0, keepdims=True) * inv
            doz = jnp.where(head_row == h, doT[:, cols].astype(f32) * inv, 0.0).astype(bf16)
            dp = dg(v_s[0:kk, :], doz, 1, 0)
            DS[0:kk, hc] = (E[0:kk, hc].astype(f32) * (dp - dot)).astype(bf16)
            dqT[pl.ds(256 * qb + 64 * h, 64), :] = dg(kT[hr, 0:kk], DS[0:kk, hc], 1, 0)
            return doz.T

        doz = jnp.concatenate([head(h) for h in range(4)], axis=0)
        q = q_s[cols, :]
        qz = jnp.concatenate([jnp.where(head_lane == h, q, 0) for h in range(4)], axis=0)
        pv = dg(E[0:kk, :], doz, 1, 0)
        pk = dg(DS[0:kk, :], qz, 1, 0)
        if qb > 0:
            dv[0 : 256 * qb, :] += pv[0 : 256 * qb]
            dk[0 : 256 * qb, :] += pk[0 : 256 * qb]
        dv[256 * qb : kk, :] = pv[256 * qb :]
        dk[256 * qb : kk, :] = pk[256 * qb :]
        pump(qb + 1)
    for i in range(T // R):
        rows = pl.ds(i * R, R)
        tb = [t[rows, :] for t in tabs]
        dq = jnp.concatenate(
            [dqT[R * i + 256 * b : R * i + 256 * (b + 1), :].T for b in range(R // 256)]
        )
        dqkv[rows, 0:256] = turn(dq * 0.125, *tb, -1).astype(bf16)
        dqkv[rows, 256:512] = turn(dk[rows, :] * LN2, *tb, -1).astype(bf16)
        dqkv[rows, 512:768] = dv[rows, :].astype(bf16)


def gelu_parts(x):
    a1, a2, a3, a4, a5 = 0.254829592, -0.284496736, 1.421413741, -1.453152027, 1.061405429
    ex = jnp.exp2(x * x * (-0.5 * LOG2E))
    t = 1.0 / (1.0 + (0.3275911 * 0.7071067811865476) * jnp.abs(x))
    half = ((((0.5 * a5 * t + 0.5 * a4) * t + 0.5 * a3) * t + 0.5 * a2) * t + 0.5 * a1) * t * ex
    phi = jnp.where(x < 0, half, 1.0 - half)
    return x * phi, phi + x * ex * 0.3989422804014327


def spread(kind, width):
    lane = lax.broadcasted_iota(jnp.int32, (128, width), 0)
    at = lax.broadcasted_iota(jnp.int32, (128, width), 1)
    col = lax.broadcasted_iota(jnp.int32, (32, width), 1)
    rank = lax.broadcasted_iota(jnp.int32, (32, width), 0)
    if kind == "qkv":
        return lane == at % 96, col // 96 == rank
    if kind == "fc_in":
        return lane == at // 512 * 16 + at % 16, col % 512 // 16 == rank
    return lane == at % 32 + 32 * kind, col // 32 == rank


def from_ranks(rows, kind, width):
    hot, mine = spread(kind, width)
    t = dg(rows, jnp.where(hot, 1.0, 0.0).astype(bf16), 1, 0)
    return jnp.sum(jnp.where(mine, t, 0.0), axis=0, keepdims=True)


def to_ranks(vector, kind, width):
    hot, mine = spread(kind, width)
    return exact(jnp.where(mine, vector, 0.0), jnp.where(hot, 1.0, 0.0), 1, 1)


def normalised(x):
    centred = x - jnp.mean(x, axis=-1, keepdims=True)
    inverse = lax.rsqrt(jnp.mean(centred * centred, axis=-1, keepdims=True) + epsilon)
    return centred * inverse, inverse


def swap_blocks(tiles):
    block = lax.broadcasted_iota(jnp.int32, tiles[0].shape, 1) // 16
    out = []
    for b in range(8):
        tile = None
        for a in range(8):
            moved = tiles[a] if a == b else pltpu.roll(tiles[a], (16 * (a - b)) % 128, 1)
            tile = moved if tile is None else jnp.where(block == a, moved, tile)
        out.append(tile)
    return out


NP = 4


def lanes(start, size):
    return pl.ds(pl.multiple_of(start, 128), size)


def layer_kernel(
    lens, tokens, cot, qkv, out, fc_in, down,
    v_gain, v_shift, v_out, v_down, v_qkv, v_in,
    mixed, tokens_grad, out_q, out_o, out_i, out_d, out_s, stats,
    ag_q, ag_o, ag_i, ag_d, ag_s,
    hid, g, hgrad, attT, vecs, gvecs, wide_b, wide_g, sv,
    cos, sin, wo, wq, wd, dqkv, q_s, k_s, v_s, qT, kT, vT, doT, E, DS, mlp,
    packed, mixed_in, part, r1, r2, r3, rz, part_s, s1, s2, s3, sz,
    own, io, fetch, send, recv, gsend, grecv,
):
    place = Place()
    me = place.me

    def gather(n, views, orders=("zxy", "zyx")):
        return [
            Gather(place, view, order, lambda s, k=k: gsend.at[n, k, s], lambda s, k=k: grecv.at[n, k, s])
            for k, (view, order) in enumerate(zip(views, orders))
        ]

    def gather_q(i):
        return gather(
            i, [lambda *a, h=h: ag_q.at[(i,) + a + (pl.ds(16 * h, 16),)] for h in range(2)]
        )

    def gather_o():
        views = [lambda *a, h=h: ag_o.at[a + (pl.ds(16 * h, 16),)] for h in range(2)]
        return gather(4, views)

    def gather_m(j):
        return gather(5 + j, [lambda *a: ag_i.at[(j,) + a], lambda *a: ag_d.at[(j,) + a]])

    def step(arrays, i):
        for array in arrays:
            array.step(i)

    vectors = gather(13, [lambda *a: ag_s.at[a]])

    def sums(n, width):
        return [
            Scatter(
                place,
                lambda *a, k=k: part.at[(k, n % NP) + a + (ALL, pl.ds(0, width))],
                [
                    b.at[(k, n % count) + (ALL,) * d + (ALL, pl.ds(0, width))]
                    for b, d, count in ((r1, 3, 2), (r2, 2, 4), (r3, 1, 4), (rz, 1, 4))
                ],
                ("zxy", "zyx")[k],
                lambda s, k=k: send.at[n, k, s],
                lambda s, k=k: recv.at[n, k, s],
            )
            for k in range(2)
        ]

    def end_q(i):
        totals = [array.total() for array in sums(i, 768)]
        for h in range(2):
            for j in range(3):
                out_q[pl.ds(16 * h, 16), lanes(1024 * j + 256 * i, 256)] = totals[h][
                    :, 256 * j : 256 * (j + 1)
                ]

    def end_o():
        totals = [array.total() for array in sums(4, 1024)]
        for h in range(2):
            out_o[pl.ds(16 * h, 16), :] = totals[h]

    def end_m(j):
        totals = [array.total() for array in sums(5 + j, 1024)]
        for h in range(2):
            out_i[pl.ds(16 * h, 16), lanes(512 * j, 512)] = totals[0][
                :, 512 * h : 512 * (h + 1)
            ]
        out_d[pl.ds(pl.multiple_of(16 * j, 16), 16), :] = totals[1]

    own_copies = []

    def own_copy(src, dst):
        copy = pltpu.make_async_copy(src, dst, own.at[len(own_copies)])
        copy.start()
        own_copies.append(copy)
        return copy

    for i in range(QG):
        for j in range(3):
            own_copy(
                qkv.at[:, pl.ds(1024 * j + 256 * i, 256)],
                ag_q.at[(i,) + me + (ALL, pl.ds(256 * j, 256))],
            )
        if i == 0:
            own_copy(out, ag_o.at[me])
    for j in range(MC):
        own_copy(down.at[pl.ds(16 * j, 16)], ag_d.at[(j,) + me])
    load_x = pltpu.make_async_copy(tokens, attT, io.at[0])
    load_x.start()
    load_g = pltpu.make_async_copy(cot, g, io.at[1])
    load_g.start()
    packed[...] = jnp.zeros_like(packed)
    for i, vector in enumerate((v_gain, v_shift, v_out, v_down)):
        packed[0:1, 32 * i : 32 * (i + 1)] = vector[...].astype(f32)
    packed[1:2, 0:96] = v_qkv[...].astype(f32)
    packed[2:3, :] = v_in[...].astype(f32)
    own_s = pltpu.make_async_copy(packed, ag_s.at[me], io.at[2])
    own_s.start()
    place.greet()
    own_s.wait()
    step(vectors, 0)
    for copy in own_copies[:4]:
        copy.wait()
    q0, o = gather_q(0), gather_o()
    step(q0, 0)
    step(o, 0)
    for t in range(4):
        tiles = [fc_in[:, 128 * (8 * t + r) : 128 * (8 * t + r + 1)].astype(f32) for r in range(8)]
        for j, tile in enumerate(swap_blocks(tiles)):
            mixed_in[j, :, 128 * t : 128 * (t + 1)] = tile.astype(bf16)
    for j in range(MC):
        own_copy(mixed_in.at[j], ag_i.at[(j,) + me])
    step(vectors, 1)
    ends = [lens[0, 0], lens[0, 0] + lens[0, 1], lens[0, 0] + lens[0, 1] + lens[0, 2]]

    def flag(b, qb):
        return 256 * b >= begins(ends, jnp.full((1, 256), 256 * qb, jnp.int32))

    tables(ends, cos, sin)
    step(vectors, 2)
    step(q0, 1)
    for copy in own_copies[4:]:
        copy.wait()
    step(gather_q(1), 0)
    step(o, 1)
    step(vectors, 3)
    step(gather_m(0), 0)
    step(vectors, 4)
    load_s = pltpu.make_async_copy(ag_s, sv, io.at[2])
    load_s.start()
    step(q0, 2)
    step(o, 2)
    step(gather_m(1), 0)
    load_s.wait()
    rows = sv[...].reshape(32, 8, 128)
    row0, row1, row2 = (rows[:, i, :].astype(bf16) for i in range(3))
    for i in range(4):
        vecs[i : i + 1, :] = from_ranks(row0, i, 1024)
    wide_b[0:1, 0:3072] = from_ranks(row1, "qkv", 3072)
    wide_b[1:2, :] = from_ranks(row2, "fc_in", 4096)
    step(gather_q(1), 1)
    step(gather_q(2), 0)
    step(q0, 3)
    load_x.wait()
    for i in range(4):
        rows = pl.ds(256 * i, 256)
        normed, _ = normalised(attT[rows, :].astype(f32))
        hid[rows, :] = (normed * vecs[0:1, :] + vecs[1:2, :]).astype(bf16)
    hgrad[...] = jnp.zeros_like(hgrad)
    step(q0, 4)

    def fetch_q(i):
        return pltpu.make_async_copy(ag_q.at[i], wq.at[i % 2], fetch.at[i % 2])

    fetch_q(0).start()
    step(o, 3)
    step(gather_m(0), 1)
    load_g.wait()
    step(o, 4)
    fetch_o = pltpu.make_async_copy(ag_o, wo, fetch.at[2])
    fetch_o.start()
    fetch_o.wait()

    bufs = (
        q_s, k_s, v_s, qT, kT, vT, doT, E, DS,
        mlp.at[:, pl.ds(0, 256)], mlp.at[:, pl.ds(256, 256)], mlp.at[:, pl.ds(512, 256)],
    )

    def attention_step(i, carry):
        fetch_q(i).wait()
        more, before = i < QG - 1, i > 0
        a, b = gather_m(2 * i), gather_m(2 * i + 1)

        @pl.when(more)
        def _():
            step(gather_q(i + 1), 2)
            step(gather_m(2 * i + 2), 0)

        def pump(p):
            if p == 0:

                @pl.when(before)
                def _():
                    step(sums(i - 1, 768), 1)

                step(b, 1)

                @pl.when(more)
                def _():
                    step(gather_m(2 * i + 3), 0)

            elif p == 1:
                step(a, 2)

                @pl.when(i < QG - 2)
                def _():
                    step(gather_q(i + 2), 1)

            elif p == 2:

                @pl.when(more)
                def _():
                    step(gather_q(i + 1), 3)

                @pl.when(before)
                def _():
                    step(sums(i - 1, 768), 2)
                    step(gather_m(2 * i - 2), 4)
                    step(gather_m(2 * i - 1), 4)

            elif p == 3:
                step(b, 2)

                @pl.when(i < QG - 3)
                def _():
                    step(gather_q(i + 3), 0)

            elif p == 4:
                step(a, 3)

                @pl.when(more)
                def _():
                    step(gather_q(i + 1), 4)
                    fetch_q(i + 1).start()
                    step(gather_m(2 * i + 2), 1)

                @pl.when(before)
                def _():
                    step(sums(i - 1, 768), 3)

            elif p == 6:
                step(b, 3)

                @pl.when(before)
                def _():
                    end_q(i - 1)

        def W(j):
            return wq[i % 2, :, :, :, :, :, 256 * j : 256 * (j + 1)].reshape(T, 256)

        def bias(j):
            return wide_b[0:1, lanes(1024 * j + 256 * i, 256)]

        attention_group(
            flag, hid, g, W, wo[i].reshape(256, T), bias, (cos, sin), bufs,
            attT.at[pl.ds(pl.multiple_of(256 * i, 256), 256)], dqkv, pump,
        )
        for b_ in range(2):
            v = dg(hid[:, 512 * b_ : 512 * (b_ + 1)], dqkv[...], 0, 0).astype(bf16)
            v = v.reshape(2, 2, 2, 2, 2, 16, 768)
            for h in range(2):
                part[h, i % NP, 2 * b_ : 2 * b_ + 2, :, :, :, :, 0:768] = v[:, :, :, :, h]
        step(sums(i, 768), 0)
        pump(5)
        total = jnp.sum(dqkv[...].astype(f32), axis=0, keepdims=True)
        for j in range(3):
            wide_g[0:1, lanes(1024 * j + 256 * i, 256)] = total[:, 256 * j : 256 * (j + 1)]
        whole_w = wq[i % 2].reshape(T, 768)
        for b_ in range(2):
            rows = pl.ds(512 * b_, 512)
            hgrad[rows, :] += dg(dqkv[rows, :], whole_w, 1, 1)
        pump(6)
        return carry

    lax.fori_loop(0, QG, attention_step, 0)

    def fetch_m(j):
        return [
            pltpu.make_async_copy(
                ag_i.at[j], wq.at[j % 2, :, :, :, :, :, pl.ds(0, 512)], fetch.at[j % 2]
            ),
            pltpu.make_async_copy(ag_d.at[j], wd.at[j % 2], fetch.at[2 + j % 2]),
        ]

    for copy in fetch_m(0):
        copy.start()
    for b in range(2):
        v = dg(attT[512 * b : 512 * (b + 1), :], g[...], 1, 0).astype(bf16)
        v = v.reshape(2, 2, 2, 2, 2, 16, T)
        for h in range(2):
            part[h, 4 % NP, 2 * b : 2 * b + 2] = v[:, :, :, :, h]
    step(sums(3, 768), 1)
    step(sums(4, 1024), 0)
    mlp[...] = jnp.zeros_like(mlp)
    step(gather_m(MC - 2), 4)
    step(gather_m(MC - 1), 4)

    act, pg = DS.at[:, pl.ds(0, 512)], DS.at[:, pl.ds(512, 512)]

    def mlp_step(j, carry):
        for copy in fetch_m(j):
            copy.wait()

        @pl.when(j < MC - 1)
        def _():
            for copy in fetch_m(j + 1):
                copy.start()

        w_in = wq[j % 2, :, :, :, :, :, 0:512].reshape(T, 512)
        w_down = wd[j % 2].reshape(512, T)
        bias = wide_b[1:2, lanes(512 * j, 512)]
        for b in range(2):
            rows = pl.ds(512 * b, 512)
            pre = dg(hid[rows, :], w_in, 1, 0) + bias
            a, d = gelu_parts(pre)
            act[rows, :] = a.astype(bf16)
            pg[rows, :] = (dg(g[rows, :], w_down, 1, 1) * d).astype(bf16)
            if b == 0:
                step(sums(j + 4, 1024), 1)
        wide_g[1:2, lanes(512 * j, 512)] = jnp.sum(pg[...].astype(f32), axis=0, keepdims=True)

        @pl.when(j == 0)
        def _():
            step(sums(3, 768), 2)

        @pl.when(j == 1)
        def _():
            step(sums(3, 768), 3)

        @pl.when(j == 2)
        def _():
            end_q(3)
            step(sums(4, 1024), 3)

        @pl.when(j == 3)
        def _():
            end_o()

        @pl.when(j > 3)
        def _():
            end_m(j - 4)

        @pl.when(j > 2)
        def _():
            step(sums(j + 2, 1024), 3)

        @pl.when(j > 0)
        def _():
            step(sums(j + 3, 1024), 2)

        slot = (j + 5) % NP
        for b in range(2):
            v = dg(hid[:, 512 * b : 512 * (b + 1)], pg[...], 0, 0).astype(bf16)
            v = v.reshape(2, 2, 2, 2, 2, 16, 512)
            for h in range(2):
                part[0, slot, 2 * b : 2 * b + 2, :, :, :, :, 512 * h : 512 * (h + 1)] = v[
                    :, :, :, :, h
                ]
            v = dg(act[:, 256 * b : 256 * (b + 1)], g[...], 0, 0).astype(bf16)
            part[1, slot, 2 * b : 2 * b + 2] = v.reshape(2, 2, 2, 2, 16, T)
        step(sums(j + 5, 1024), 0)
        for b in range(2):
            rows = pl.ds(512 * b, 512)
            mlp[rows, :] += dg(act[rows, :], w_down, 1, 0)
            hgrad[rows, :] += dg(pg[rows, :], w_in, 1, 1)
        return carry

    lax.fori_loop(0, MC, mlp_step, 0)

    last = MC + 4
    reload_x = pltpu.make_async_copy(tokens, hid, io.at[0])
    reload_x.start()
    step(sums(last, 1024), 1)
    step(sums(last - 1, 1024), 2)
    step(sums(last - 2, 1024), 3)
    end_m(MC - 4)
    reload_x.wait()
    for i in range(4):
        rows = pl.ds(256 * i, 256)
        normed, inverse = normalised(hid[rows, :].astype(f32))
        h = hgrad[rows, :]
        up_g = g[rows, :].astype(f32)
        for k, v in enumerate((h * normed, h, up_g)):
            v = jnp.sum(v, axis=0, keepdims=True)
            gvecs[k : k + 1, :] = v if i == 0 else gvecs[k : k + 1, :] + v
        n = h * vecs[0:1, :]
        d = n - jnp.mean(n, axis=-1, keepdims=True)
        d = d - normed * jnp.mean(n * normed, axis=-1, keepdims=True)
        E[rows, :] = (up_g + inverse * d).astype(bf16)
    put_tg = pltpu.make_async_copy(E, tokens_grad, io.at[1])
    put_tg.start()
    step(sums(last, 1024), 2)
    step(sums(last - 1, 1024), 3)
    row0 = sum(to_ranks(gvecs[min(k, 2) : min(k, 2) + 1, :], k, 1024) for k in range(4))
    row1 = to_ranks(wide_g[0:1, 0:3072], "qkv", 3072)
    row2 = to_ranks(wide_g[1:2, :], "fc_in", 4096)
    for r in range(32):
        part_s[r // 8, r // 4 % 2, r // 2 % 2, r % 2] = jnp.concatenate(
            [row0[r : r + 1], row1[r : r + 1], row2[r : r + 1], jnp.zeros((5, 128), f32)]
        )
    tiny = Scatter(
        place, lambda *a: part_s.at[a], [s1, s2, s3, sz], "zxy",
        lambda s: send.at[13, 0, s], lambda s: recv.at[13, 0, s],
    )
    tiny.step(0)
    end_m(MC - 3)
    tiny.step(1)
    step(sums(last, 1024), 3)
    tiny.step(2)
    w_out = wo[...].reshape(T, T)
    squares = [jnp.zeros((1, T), f32)] * 3
    for i in range(4):
        rows = pl.ds(256 * i, 256)
        x = hid[rows, :].astype(f32)
        a = dg(attT[:, rows], w_out, 0, 0) + vecs[2:3, :]
        m = mlp[rows, :] + vecs[3:4, :]
        hid[rows, :] = (x + a + m).astype(bf16)
        squares = [
            s + jnp.sum(v * v, axis=0, keepdims=True) for s, v in zip(squares, (x, a, m))
        ]
        if i == 1:
            tiny.step(3)
    put_mixed = pltpu.make_async_copy(hid, mixed, io.at[0])
    put_mixed.start()
    for i in range(3):
        total = jnp.sum(squares[i], axis=1, keepdims=True)
        stats[i : i + 1, :] = jnp.broadcast_to(total, (1, 128))
    end_m(MC - 2)
    end_m(MC - 1)
    out_s[...] = tiny.total()
    put_tg.wait()
    put_mixed.wait()
    for arrays in [vectors, o] + [gather_q(i) for i in range(QG)]:
        for array in arrays:
            array.close()

    def close_m(j, carry):
        for array in gather_m(j):
            array.close()
        return carry

    lax.fori_loop(0, MC, close_m, 0)


def whole_layer(lens, tokens, cot, qkv, out, fc_in, down, *vectors):
    any_ = pl.BlockSpec(memory_space=pl.ANY)
    vmem = pl.BlockSpec(memory_space=pltpu.VMEM)
    sd = jax.ShapeDtypeStruct
    ranks = (4, 2, 2, 2)
    dma = pltpu.SemaphoreType.DMA
    return pl.pallas_call(
        layer_kernel,
        out_shape=[
            sd((T, T), bf16),
            sd((T, T), bf16),
            sd((32, 3072), f32),
            sd((32, 1024), f32),
            sd((32, 4096), f32),
            sd((128, 1024), f32),
            sd((8, 128), f32),
            sd((8, 128), f32),
            sd((QG,) + ranks + (32, 768), bf16),
            sd(ranks + (32, 1024), bf16),
            sd((MC,) + ranks + (32, 512), bf16),
            sd((MC,) + ranks + (16, 1024), bf16),
            sd(ranks + (8, 128), f32),
        ],
        in_specs=[pl.BlockSpec(memory_space=pltpu.SMEM)]
        + [any_] * 2
        + [vmem] * 10,
        out_specs=[any_] * 2 + [vmem] * 6 + [any_] * 5,
        scratch_shapes=[
            pltpu.VMEM((T, T), bf16),
            pltpu.VMEM((T, T), bf16),
            pltpu.VMEM((T, T), f32),
            pltpu.VMEM((T, T), bf16),
            pltpu.VMEM((8, 1024), f32),
            pltpu.VMEM((8, 1024), f32),
            pltpu.VMEM((8, 4096), f32),
            pltpu.VMEM((8, 4096), f32),
            pltpu.VMEM(ranks + (8, 128), f32),
            pltpu.VMEM((T, 128), f32),
            pltpu.VMEM((T, 128), f32),
            pltpu.VMEM(ranks + (32, 1024), bf16),
            pltpu.VMEM((2,) + ranks + (32, 768), bf16),
            pltpu.VMEM((2,) + ranks + (16, 1024), bf16),
            pltpu.VMEM((T, 768), bf16),
            pltpu.VMEM((T, 256), bf16),
            pltpu.VMEM((T, 256), bf16),
            pltpu.VMEM((T, 256), bf16),
            pltpu.VMEM((256, T), bf16),
            pltpu.VMEM((256, T), bf16),
            pltpu.VMEM((256, T), bf16),
            pltpu.VMEM((256, T), bf16),
            pltpu.VMEM((T, T), bf16),
            pltpu.VMEM((T, T), bf16),
            pltpu.VMEM((T, T), f32),
            pltpu.VMEM((8, 128), f32),
            pltpu.VMEM((MC, 32, 512), bf16),
            pltpu.VMEM((2, NP) + ranks + (16, 1024), bf16),
            pltpu.VMEM((2, 2, 4, 2, 2, 16, 1024), bf16),
            pltpu.VMEM((2, 4, 4, 2, 16, 1024), bf16),
            pltpu.VMEM((2, 4, 4, 16, 1024), bf16),
            pltpu.VMEM((2, 4, 3, 16, 1024), bf16),
            pltpu.VMEM(ranks + (8, 128), f32),
            pltpu.VMEM((4, 2, 2, 8, 128), f32),
            pltpu.VMEM((4, 2, 8, 128), f32),
            pltpu.VMEM((4, 8, 128), f32),
            pltpu.VMEM((3, 8, 128), f32),
            dma((30,)),
            dma((3,)),
            dma((4,)),
            dma((14, 2, 6)),
            dma((14, 2, 6)),
            dma((14, 2, 6)),
            dma((14, 2, 6)),
        ],
        compiler_params=pltpu.CompilerParams(
            collective_id=0, has_side_effects=True, vmem_limit_bytes=63 * 2**20
        ),
    )(lens, tokens, cot, qkv, out, fc_in, down, *vectors)


def finish_kernel(
    mixed, tokens_grad, q, o, i_, d, s, stats,
    f_mixed, f_tokens, f_gain, f_shift, f_q, f_qb, f_o, f_ob, f_i, f_ib, f_d, f_db, f_rms,
    held, sem,
):
    moves = []
    for n, (a, b) in enumerate(((mixed, f_mixed), (tokens_grad, f_tokens))):
        for k in range(4):
            rows = pl.ds(256 * k, 256)
            into = pltpu.make_async_copy(a.at[rows], held.at[n, rows], sem.at[n, k])
            into.start()
            moves.append((into, pltpu.make_async_copy(held.at[n, rows], b.at[rows], sem.at[n, k])))
    for into, out in moves:
        into.wait()
        out.start()
    f_q[...] = q[...]
    f_o[...] = o[...]
    f_d[...] = d[...]
    for t in range(4):
        tiles = [i_[:, 512 * j + 128 * t : 512 * j + 128 * (t + 1)] for j in range(MC)]
        for r, tile in enumerate(swap_blocks(tiles)):
            f_i[:, 128 * (8 * t + r) : 128 * (8 * t + r + 1)] = tile
    f_gain[...] = s[0:1, 0:32]
    f_shift[...] = s[0:1, 32:64]
    f_ob[...] = s[0:1, 64:96]
    f_db[...] = s[0:1, 96:128]
    f_qb[...] = s[1:2, 0:96]
    f_ib[...] = s[2:3, :]
    lane = lax.broadcasted_iota(jnp.int32, (1, 128), 1)
    mean = jnp.where(lane == 0, stats[0:1, :], jnp.where(lane == 1, stats[1:2, :], stats[2:3, :]))
    f_rms[...] = jnp.sqrt(mean * (1.0 / (T * T)))[:, 0:3]
    for _, out in moves:
        out.wait()


def finish(mixed, tokens_grad, q, o, i_, d, s, stats):
    any_ = pl.BlockSpec(memory_space=pl.ANY)
    vmem = pl.BlockSpec(memory_space=pltpu.VMEM)
    sd = jax.ShapeDtypeStruct
    return pl.pallas_call(
        finish_kernel,
        out_shape=[
            sd((T, T), bf16), sd((T, T), bf16), sd((1, 32), f32), sd((1, 32), f32),
            sd((32, 3072), f32), sd((1, 96), f32), sd((32, 1024), f32), sd((1, 32), f32),
            sd((32, 4096), f32), sd((1, 128), f32), sd((128, 1024), f32), sd((1, 32), f32),
            sd((1, 3), f32),
        ],
        in_specs=[any_] * 2 + [vmem] * 6,
        out_specs=[any_] * 2 + [vmem] * 11,
        scratch_shapes=[pltpu.VMEM((2, T, T), bf16), pltpu.SemaphoreType.DMA((2, 4))],
    )(mixed, tokens_grad, q, o, i_, d, s, stats)


def layer_math(
    tokens, cotangent, seq_lens, gain, shift, qkv_matrix, qkv_b, out_matrix, out_b,
    in_matrix, in_b, down_matrix, down_b,
):
    gain_full, shift_full = gain.astype(f32), shift.astype(f32)
    row_count, width = tokens.shape
    inputs = tokens.astype(f32)
    centred = inputs - jnp.mean(inputs, axis=-1, keepdims=True)
    inverse = lax.rsqrt(jnp.mean(centred * centred, axis=-1, keepdims=True) + epsilon)
    normed = centred * inverse
    hid_low = (normed * gain_full + shift_full).astype(bf16)
    qkv = jnp.dot(hid_low, qkv_matrix, preferred_element_type=f32) + qkv_b.astype(f32)
    segment, places, offset = positions(seq_lens[0], row_count)
    freqs = 10000.0 ** (-jnp.arange(ROT // 2, dtype=f32) * 2.0 / ROT)
    angle = offset[:, None] * freqs[None, :]
    cosine = jnp.cos(angle)[:, None, :]
    sine = jnp.sin(angle)[:, None, :]
    heads = (row_count, HEADS, HEAD)
    q_low = rotate(qkv[:, :width].reshape(heads), cosine, sine).astype(bf16)
    k_low = rotate(qkv[:, width : 2 * width].reshape(heads), cosine, sine).astype(bf16)
    v_low = qkv[:, 2 * width :].reshape(heads).astype(bf16)
    block_rows = min(512, row_count)
    block_count = row_count // block_rows
    outputs = []
    kept_lse = []
    for block in range(block_count):
        lower = block * block_rows
        upper = lower + block_rows
        scores, allowed = block_scores(
            q_low[lower:upper], k_low[:upper], segment[lower:upper], segment[:upper],
            places[lower:upper], places[:upper],
        )
        row_max = jnp.max(scores, axis=-1, keepdims=True)
        expo = jnp.exp(scores - row_max)
        totals = jnp.sum(expo, axis=-1, keepdims=True)
        soft_low = (expo / totals).astype(bf16)
        kept_lse.append(row_max + jnp.log(totals))
        outputs.append(
            jnp.einsum("hqk,khd->qhd", soft_low, v_low[:upper], preferred_element_type=f32)
        )
    att_low = jnp.concatenate(outputs, axis=0).reshape(row_count, width).astype(bf16)
    attn_out = jnp.dot(att_low, out_matrix, preferred_element_type=f32) + out_b.astype(f32)
    pre = jnp.dot(hid_low, in_matrix, preferred_element_type=f32) + in_b.astype(f32)
    gelu_exact = partial(jax.nn.gelu, approximate=False)
    act_low = gelu_exact(pre).astype(bf16)
    mlp = jnp.dot(act_low, down_matrix, preferred_element_type=f32) + down_b.astype(f32)
    mixed = (inputs + attn_out + mlp).astype(bf16)
    stream_rms = jnp.sqrt(
        jnp.stack([jnp.mean(inputs * inputs), jnp.mean(attn_out * attn_out), jnp.mean(mlp * mlp)])
    )[None, :]
    upstream = cotangent.astype(f32)
    grad_down = transposed_times(act_low, cotangent)
    grad_out = transposed_times(att_low, cotangent)
    grad_sum = jnp.sum(upstream, axis=0)
    act_grad = times_transposed(cotangent, down_matrix)
    _, gelu_pull = jax.vjp(gelu_exact, pre)
    pre_grad_low = gelu_pull(act_grad)[0].astype(bf16)
    grad_in = transposed_times(hid_low, pre_grad_low)
    grad_in_b = jnp.sum(pre_grad_low.astype(f32), axis=0)
    att_grad_low = times_transposed(cotangent, out_matrix).astype(bf16).reshape(heads)
    query_grads = []
    key_grad = jnp.zeros(heads, f32)
    value_grad = jnp.zeros(heads, f32)
    for block in range(block_count):
        lower = block * block_rows
        upper = lower + block_rows
        query_block = q_low[lower:upper]
        scores, allowed = block_scores(
            query_block, k_low[:upper], segment[lower:upper], segment[:upper],
            places[lower:upper], places[:upper],
        )
        soft = jnp.where(allowed[None], jnp.exp(scores - kept_lse[block]), 0.0)
        soft_low = soft.astype(bf16)
        out_grad = att_grad_low[lower:upper]
        value_part = jnp.einsum("hqk,qhd->khd", soft_low, out_grad, preferred_element_type=f32)
        prob_grad = jnp.einsum("qhd,khd->hqk", out_grad, v_low[:upper], preferred_element_type=f32)
        score_grad = soft * (prob_grad - jnp.sum(soft * prob_grad, axis=-1, keepdims=True))
        score_low = score_grad.astype(bf16)
        query_grads.append(
            jnp.einsum("hqk,khd->qhd", score_low, k_low[:upper], preferred_element_type=f32)
            * HEAD ** (-0.5)
        )
        key_part = jnp.einsum(
            "hqk,qhd->khd", score_low, query_block, preferred_element_type=f32
        ) * HEAD ** (-0.5)
        padding = ((0, row_count - upper), (0, 0), (0, 0))
        key_grad = key_grad + jnp.pad(key_part, padding)
        value_grad = value_grad + jnp.pad(value_part, padding)
    query_grad = unrotate(jnp.concatenate(query_grads, axis=0), cosine, sine)
    key_grad = unrotate(key_grad, cosine, sine)
    qkv_grad_low = jnp.concatenate(
        [g.reshape(row_count, width) for g in (query_grad, key_grad, value_grad)], axis=1
    ).astype(bf16)
    grad_qkv = transposed_times(hid_low, qkv_grad_low)
    grad_qkv_b = jnp.sum(qkv_grad_low.astype(f32), axis=0)
    hidden_grad = times_transposed(qkv_grad_low, qkv_matrix) + times_transposed(
        pre_grad_low, in_matrix
    )
    grad_gain = jnp.sum(hidden_grad * normed, axis=0)
    grad_shift = jnp.sum(hidden_grad, axis=0)
    scaled = hidden_grad * gain_full
    input_grad = upstream + inverse * (
        scaled
        - jnp.mean(scaled, axis=-1, keepdims=True)
        - normed * jnp.mean(scaled * normed, axis=-1, keepdims=True)
    )
    return (
        mixed, input_grad.astype(bf16), grad_gain, grad_shift, grad_qkv, grad_qkv_b,
        grad_out, grad_sum, grad_in, grad_in_b, grad_down, grad_sum, stream_rms,
    )


def generic(tokens, cotangent, seq_lens, *shards):
    axes = ("wide", "narrow")
    whole = [lax.all_gather(s, axes, axis=0, tiled=True) for s in shards]
    results = layer_math(tokens, cotangent, seq_lens, *whole)
    summed = [
        lax.psum_scatter(g, axes, scatter_dimension=0, tiled=True) for g in results[2:12]
    ]
    return (*results[:2], *summed, results[12])


def local(
    tokens, cotangent, seq_lens, norm_gain, norm_bias, qkv_weight, qkv_bias, out_weight,
    out_bias, fc_in_weight, fc_in_bias, fc_out_weight, fc_out_bias,
):
    vectors = (norm_gain, norm_bias, out_bias, fc_out_bias, qkv_bias, fc_in_bias)
    results = whole_layer(
        seq_lens, tokens, cotangent, qkv_weight, out_weight, fc_in_weight, fc_out_weight,
        *(v[None, :] for v in vectors),
    )
    results = finish(*results[:8])
    flat = (2, 3, 5, 7, 9, 11)
    return tuple(r[0] if n in flat else r for n, r in enumerate(results))


def solution(mesh):
    rows, flat = P(("wide", "narrow"), None), P(("wide", "narrow"))
    fits = mesh.shape["wide"] == 8 and mesh.shape["narrow"] == 4
    return jax.shard_map(
        local if fits else generic,
        mesh=mesh,
        in_specs=(rows, rows, rows, flat, flat, rows, flat, rows, flat, rows, flat, rows, flat),
        out_specs=(rows, rows, flat, flat, rows, flat, rows, flat, rows, flat, rows, flat, rows),
        check_vma=False,
    )
```

```python
import itertools
from functools import partial

import jax
import jax.numpy as jnp
from jax import lax
from jax.experimental import pallas as pl
from jax.experimental.pallas import tpu as pltpu
from jax.sharding import PartitionSpec as P

HEADS = 16
HEAD = 64
ROT = 16
MESH = pl.DeviceIdType.MESH
bf16 = jnp.bfloat16
f32 = jnp.float32
ALL = slice(None)

epsilon = 1e-05


def positions(lengths, count):
    ends = jnp.cumsum(lengths)
    places = jnp.arange(count, dtype=jnp.int32)
    segment = jnp.sum((places[:, None] >= ends[None, :]).astype(jnp.int32), axis=1)
    starts = ends - lengths
    slots = jnp.arange(lengths.shape[0], dtype=jnp.int32)
    begin = jnp.sum(jnp.where(segment[:, None] == slots[None, :], starts[None, :], 0), axis=1)
    return (segment, places, (places - begin).astype(jnp.float32))


def rotate(vector, cosine, sine):
    half = ROT // 2
    first = vector[..., :half]
    second = vector[..., half:ROT]
    return jnp.concatenate(
        [first * cosine - second * sine, second * cosine + first * sine, vector[..., ROT:]], axis=-1
    )


def unrotate(grad, cosine, sine):
    half = ROT // 2
    first = grad[..., :half]
    second = grad[..., half:ROT]
    return jnp.concatenate(
        [first * cosine + second * sine, second * cosine - first * sine, grad[..., ROT:]], axis=-1
    )


def times_transposed(left, right):
    return lax.dot_general(
        left, right, (((1,), (1,)), ((), ())), preferred_element_type=jnp.float32
    )


def transposed_times(left, right):
    return lax.dot_general(
        left, right, (((0,), (0,)), ((), ())), preferred_element_type=jnp.float32
    )


def block_scores(query_block, key_low, seg_query, seg_key, place_query, place_key):
    raw = jnp.einsum(
        "qhd,khd->hqk", query_block, key_low, preferred_element_type=jnp.float32
    ) * HEAD ** (-0.5)
    allowed = (seg_query[:, None] == seg_key[None, :]) & (
        place_key[None, :] <= place_query[:, None]
    )
    return (jnp.where(allowed[None], raw, -1e30), allowed)


QG = 4
LOG2E = 1.4426950408889634
LN2 = 0.6931471805599453
T = 1024
MC = 8


class Place:
    def __init__(self):
        wide, narrow = lax.axis_index("wide"), lax.axis_index("narrow")
        self.z, self.x = wide // 2, wide % 2
        self.y, self.c = narrow // 2, narrow % 2
        self.me = (self.z, self.x, self.y, self.c)
        self.zs = [(self.z + d) % 4 for d in (1, 2, 3)]

    def device(self, z, x, y, c):
        return (z * 2 + x, y * 2 + c)

    def targets(self, axis):
        z, x, y, c = self.me
        if axis == "z":
            return [(i, (other, x, y, c)) for i, other in enumerate(self.zs)]
        return [
            {"x": (3, (z, 1 - x, y, c)), "y": (4, (z, x, 1 - y, c)), "c": (5, (z, x, y, 1 - c))}[axis]
        ]

    def partners(self):
        z, x, y, c = self.me
        return [self.device(p, x, y, c) for p in self.zs] + [
            self.device(z, 1 - x, y, c),
            self.device(z, x, 1 - y, c),
            self.device(z, x, y, 1 - c),
        ]

    def greet(self):
        barrier = pltpu.get_barrier_semaphore()
        for other in self.partners():
            pl.semaphore_signal(barrier, inc=1, device_id=other, device_id_type=MESH)
        pl.semaphore_wait(barrier, 6)


def dg(a, b, ca, cb):
    return lax.dot_general(a, b, (((ca,), (cb,)), ((), ())), preferred_element_type=f32)


def exact(a, b, ca, cb):
    return lax.dot_general(
        a, b, (((ca,), (cb,)), ((), ())), precision=lax.Precision.HIGHEST,
        preferred_element_type=f32,
    )


def remote(src, dst, send, recv, device):
    return pltpu.make_async_remote_copy(
        src_ref=src, dst_ref=dst, send_sem=send, recv_sem=recv,
        device_id=device, device_id_type=MESH,
    )


class Gather:
    def __init__(self, place, view, order, send, recv):
        self.p, self.view, self.axes = place, view, order + "c"
        self.send, self.recv = send, recv

    def copies(self, i):
        me, axis = self.p.me, self.axes[i]
        part = [ALL if a in self.axes[:i] else me["zxyc".index(a)] for a in "zxyc"]
        return [
            remote(
                self.view(*part), self.view(*part), self.send(slot), self.recv(slot),
                self.p.device(*to),
            )
            for slot, to in self.p.targets(axis)
        ]

    def step(self, i):
        if i > 0:
            for copy in self.copies(i - 1):
                copy.wait_recv()
        if i < 4:
            for copy in self.copies(i):
                copy.start()

    def close(self):
        for i in range(4):
            for copy in self.copies(i):
                copy.wait_send()


class Scatter:
    def __init__(self, place, part, bufs, order, send, recv):
        self.p, self.part, self.bufs = place, part, bufs
        self.axes = "c" + order[::-1]
        self.send, self.recv = send, recv

    def index(self, i, value):
        return [
            value if a == self.axes[i] else (self.p.me[k] if a in self.axes[:i] else ALL)
            for k, a in enumerate("zxyc")
        ]

    def landing(self, i):
        buf = self.bufs[i]
        return [buf.at[n] for n in range(3)] if self.axes[i] == "z" else [buf]

    def copies(self, i):
        at = "zxyc".index(self.axes[i])
        return [
            remote(
                self.part(*self.index(i, to[at])), land, self.send(slot), self.recv(slot),
                self.p.device(*to),
            )
            for land, (slot, to) in zip(self.landing(i), self.p.targets(self.axes[i]))
        ]

    def step(self, i):
        if i > 0:
            for copy in self.copies(i - 1):
                copy.wait_recv()
            part = self.part(*self.index(i - 1, self.p.me["zxyc".index(self.axes[i - 1])]))
            for buf in self.landing(i - 1):
                for at in itertools.product(*(range(n) for n in buf.shape[:-2])):
                    part[at] = part[at] + buf[at]
        for copy in self.copies(i):
            copy.start()

    def total(self):
        for copy in self.copies(3):
            copy.wait_recv()
        out = self.part(*self.p.me)[...].astype(f32)
        for buf in self.landing(3):
            out = out + buf[...].astype(f32)
        for i in range(4):
            for copy in self.copies(i):
                copy.wait_send()
        return out


def begins(ends, t):
    first = jnp.zeros_like(t)
    for e in ends:
        first = jnp.where(t >= e, e, first)
    return first


def tables(ends, cos_ref, sin_ref):
    t = lax.broadcasted_iota(jnp.int32, (T, 128), 0)
    d = lax.broadcasted_iota(jnp.int32, (T, 128), 1) % 64
    offset = (t - begins(ends, t)).astype(f32)
    freq = jnp.exp((d % 8).astype(f32) * (-2.0 / 16 * 9.210340371976184))
    angle = offset * freq
    cos_ref[...] = jnp.where(d < 16, jnp.cos(angle), 1.0)
    sin_ref[...] = jnp.where(d < 16, jnp.where(d < 8, -1.0, 1.0) * jnp.sin(angle), 0.0)


def turn(v, cos, sin, sign):
    first = lax.broadcasted_iota(jnp.int32, cos.shape, 1) % 64 < 8
    out = []
    for i in range(2):
        w = v[:, 128 * i : 128 * (i + 1)]
        r = jnp.where(first, pltpu.roll(w, 120, 1), pltpu.roll(w, 8, 1)) * sin
        out.append(w * cos + r if sign > 0 else w * cos - r)
    return jnp.concatenate(out, axis=1)


def attention_group(flag, hid, g, W, Wo, bias, tabs, bufs, attT, dqkv, pump):
    q_s, k_s, v_s, qT, kT, vT, doT, E, DS, dv, dk, dqT = bufs
    R = 512
    for i in range(T // R):
        rows = pl.ds(i * R, R)
        tb = [t[rows, :] for t in tabs]
        h = hid[rows, :]
        q = turn(dg(h, W(0), 1, 0) + bias(0), *tb, 1) * (LOG2E / 8)
        q = q.astype(bf16)
        q_s[rows, :] = q
        qT[:, rows] = q.T
        k = turn(dg(h, W(1), 1, 0) + bias(1), *tb, 1).astype(bf16)
        k_s[rows, :] = k
        kT[:, rows] = k.T
        v = (dg(h, W(2), 1, 0) + bias(2)).astype(bf16)
        v_s[rows, :] = v
        vT[:, rows] = v.T
    pump(0)
    for i in range(T // R):
        rows = pl.ds(i * R, R)
        do = dg(g[rows, :], Wo(), 1, 1).astype(bf16)
        doT[:, rows] = do.T
    head_row = lax.broadcasted_iota(jnp.int32, (256, 256), 0) // 64
    head_lane = lax.broadcasted_iota(jnp.int32, (256, 256), 1) // 64
    causal = lax.broadcasted_iota(jnp.int32, (256, 256), 0) <= lax.broadcasted_iota(
        jnp.int32, (256, 256), 1
    )
    for qb in range(T // 256):
        kk = 256 * (qb + 1)
        cols = pl.ds(256 * qb, 256)

        def head(h):
            hc, hr = pl.ds(h * 256, 256), pl.ds(h * 64, 64)
            s = dg(k_s[0:kk, :], jnp.where(head_row == h, qT[:, cols], 0), 1, 0)
            blocks = [s[256 * b : 256 * (b + 1)] for b in range(qb + 1)]
            blocks[qb] = jnp.where(causal, blocks[qb], -1e30)
            m = jnp.max(blocks[qb], axis=0, keepdims=True)
            for b in range(qb):
                top = jnp.max(blocks[b], axis=0, keepdims=True)
                m = jnp.maximum(m, jnp.where(flag(b, qb), top, -1e30))
            total = None
            for b in range(qb + 1):
                e = jnp.exp2(blocks[b] - (m if b == qb else jnp.where(flag(b, qb), m, 1e30)))
                t = jnp.sum(e, axis=0, keepdims=True)
                total = t if total is None else total + t
                E[256 * b : 256 * (b + 1), hc] = e.astype(bf16)
            inv = 1.0 / total
            oT = dg(vT[hr, 0:kk], E[0:kk, hc], 1, 0) * inv
            attT[hr, cols] = oT.astype(bf16)
            dot = jnp.sum(doT[hr, cols].astype(f32) * oT, axis=0, keepdims=True) * inv
            doz = jnp.where(head_row == h, doT[:, cols].astype(f32) * inv, 0.0).astype(bf16)
            dp = dg(v_s[0:kk, :], doz, 1, 0)
            DS[0:kk, hc] = (E[0:kk, hc].astype(f32) * (dp - dot)).astype(bf16)
            dqT[pl.ds(256 * qb + 64 * h, 64), :] = dg(kT[hr, 0:kk], DS[0:kk, hc], 1, 0)
            return doz.T

        doz = jnp.concatenate([head(h) for h in range(4)], axis=0)
        q = q_s[cols, :]
        qz = jnp.concatenate([jnp.where(head_lane == h, q, 0) for h in range(4)], axis=0)
        pv = dg(E[0:kk, :], doz, 1, 0)
        pk = dg(DS[0:kk, :], qz, 1, 0)
        if qb > 0:
            dv[0 : 256 * qb, :] += pv[0 : 256 * qb]
            dk[0 : 256 * qb, :] += pk[0 : 256 * qb]
        dv[256 * qb : kk, :] = pv[256 * qb :]
        dk[256 * qb : kk, :] = pk[256 * qb :]
        pump(qb + 1)
    for i in range(T // R):
        rows = pl.ds(i * R, R)
        tb = [t[rows, :] for t in tabs]
        dq = jnp.concatenate(
            [dqT[R * i + 256 * b : R * i + 256 * (b + 1), :].T for b in range(R // 256)]
        )
        dqkv[rows, 0:256] = turn(dq * 0.125, *tb, -1).astype(bf16)
        dqkv[rows, 256:512] = turn(dk[rows, :] * LN2, *tb, -1).astype(bf16)
        dqkv[rows, 512:768] = dv[rows, :].astype(bf16)


def gelu_parts(x):
    a1, a2, a3, a4, a5 = 0.254829592, -0.284496736, 1.421413741, -1.453152027, 1.061405429
    ex = jnp.exp2(x * x * (-0.5 * LOG2E))
    t = 1.0 / (1.0 + (0.3275911 * 0.7071067811865476) * jnp.abs(x))
    half = ((((0.5 * a5 * t + 0.5 * a4) * t + 0.5 * a3) * t + 0.5 * a2) * t + 0.5 * a1) * t * ex
    phi = jnp.where(x < 0, half, 1.0 - half)
    return x * phi, phi + x * ex * 0.3989422804014327


def spread(kind, width):
    lane = lax.broadcasted_iota(jnp.int32, (128, width), 0)
    at = lax.broadcasted_iota(jnp.int32, (128, width), 1)
    col = lax.broadcasted_iota(jnp.int32, (32, width), 1)
    rank = lax.broadcasted_iota(jnp.int32, (32, width), 0)
    if kind == "qkv":
        return lane == at % 96, col // 96 == rank
    if kind == "fc_in":
        return lane == at // 512 * 16 + at % 16, col % 512 // 16 == rank
    return lane == at % 32 + 32 * kind, col // 32 == rank


def from_ranks(rows, kind, width):
    hot, mine = spread(kind, width)
    t = dg(rows, jnp.where(hot, 1.0, 0.0).astype(bf16), 1, 0)
    return jnp.sum(jnp.where(mine, t, 0.0), axis=0, keepdims=True)


def to_ranks(vector, kind, width):
    hot, mine = spread(kind, width)
    return exact(jnp.where(mine, vector, 0.0), jnp.where(hot, 1.0, 0.0), 1, 1)


def normalised(x):
    centred = x - jnp.mean(x, axis=-1, keepdims=True)
    inverse = lax.rsqrt(jnp.mean(centred * centred, axis=-1, keepdims=True) + epsilon)
    return centred * inverse, inverse


def swap_blocks(tiles):
    block = lax.broadcasted_iota(jnp.int32, tiles[0].shape, 1) // 16
    out = []
    for b in range(8):
        tile = None
        for a in range(8):
            moved = tiles[a] if a == b else pltpu.roll(tiles[a], (16 * (a - b)) % 128, 1)
            tile = moved if tile is None else jnp.where(block == a, moved, tile)
        out.append(tile)
    return out


NP = 4


def lanes(start, size):
    return pl.ds(pl.multiple_of(start, 128), size)


def layer_kernel(
    lens, tokens, cot, qkv, out, fc_in, down,
    v_gain, v_shift, v_out, v_down, v_qkv, v_in,
    mixed, tokens_grad, out_q, out_o, out_i, out_d, out_s, stats,
    ag_q, ag_o, ag_i, ag_d, ag_s,
    hid, g, hgrad, attT, vecs, gvecs, wide_b, wide_g, sv,
    cos, sin, wo, wq, wd, dqkv, q_s, k_s, v_s, qT, kT, vT, doT, E, DS, mlp,
    packed, mixed_in, part, r1, r2, r3, rz, part_s, s1, s2, s3, sz,
    own, io, fetch, send, recv, gsend, grecv,
):
    place = Place()
    me = place.me

    def gather(n, views, orders=("zxy", "zyx")):
        return [
            Gather(place, view, order, lambda s, k=k: gsend.at[n, k, s], lambda s, k=k: grecv.at[n, k, s])
            for k, (view, order) in enumerate(zip(views, orders))
        ]

    def gather_q(i):
        return gather(
            i, [lambda *a, h=h: ag_q.at[(i,) + a + (pl.ds(16 * h, 16),)] for h in range(2)]
        )

    def gather_o():
        views = [lambda *a, h=h: ag_o.at[a + (pl.ds(16 * h, 16),)] for h in range(2)]
        return gather(4, views)

    def gather_m(j, odd):
        down_view = lambda *a: ag_d.at[(j,) + a]
        if not odd:
            return gather(5 + j, [lambda *a: ag_i.at[(j,) + a], down_view])
        views = [lambda *a, h=h: ag_i.at[(j,) + a + (pl.ds(16 * h, 16),)] for h in range(2)]
        return gather(5 + j, views + [down_view], ("zxy", "zyx", "xyz"))

    def step(arrays, i):
        for array in arrays:
            array.step(i)

    vectors = gather(13, [lambda *a: ag_s.at[a]])

    def sums(n, width):
        return [
            Scatter(
                place,
                lambda *a, k=k: part.at[(k, n % NP) + a + (ALL, pl.ds(0, width))],
                [
                    b.at[(k, n % count) + (ALL,) * d + (ALL, pl.ds(0, width))]
                    for b, d, count in ((r1, 3, 2), (r2, 2, 4), (r3, 1, 4), (rz, 1, 4))
                ],
                ("zxy", "zyx")[k],
                lambda s, k=k: send.at[n, k, s],
                lambda s, k=k: recv.at[n, k, s],
            )
            for k in range(2)
        ]

    def end_q(i):
        totals = [array.total() for array in sums(i, 768)]
        for h in range(2):
            for j in range(3):
                out_q[pl.ds(16 * h, 16), lanes(1024 * j + 256 * i, 256)] = totals[h][
                    :, 256 * j : 256 * (j + 1)
                ]

    def end_o():
        totals = [array.total() for array in sums(4, 1024)]
        for h in range(2):
            out_o[pl.ds(16 * h, 16), :] = totals[h]

    def end_m(j):
        totals = [array.total() for array in sums(5 + j, 1024)]
        for h in range(2):
            out_i[pl.ds(16 * h, 16), lanes(512 * j, 512)] = totals[0][
                :, 512 * h : 512 * (h + 1)
            ]
        out_d[pl.ds(pl.multiple_of(16 * j, 16), 16), :] = totals[1]

    own_copies = []

    def own_copy(src, dst):
        copy = pltpu.make_async_copy(src, dst, own.at[len(own_copies)])
        copy.start()
        own_copies.append(copy)
        return copy

    for i in range(QG):
        for j in range(3):
            own_copy(
                qkv.at[:, pl.ds(1024 * j + 256 * i, 256)],
                ag_q.at[(i,) + me + (ALL, pl.ds(256 * j, 256))],
            )
        if i == 0:
            own_copy(out, ag_o.at[me])
    for j in range(MC):
        own_copy(down.at[pl.ds(16 * j, 16)], ag_d.at[(j,) + me])
    load_x = pltpu.make_async_copy(tokens, attT, io.at[0])
    load_x.start()
    load_g = pltpu.make_async_copy(cot, g, io.at[1])
    load_g.start()
    packed[...] = jnp.zeros_like(packed)
    for i, vector in enumerate((v_gain, v_shift, v_out, v_down)):
        packed[0:1, 32 * i : 32 * (i + 1)] = vector[...].astype(f32)
    packed[1:2, 0:96] = v_qkv[...].astype(f32)
    packed[2:3, :] = v_in[...].astype(f32)
    own_s = pltpu.make_async_copy(packed, ag_s.at[me], io.at[2])
    own_s.start()
    place.greet()
    own_s.wait()
    step(vectors, 0)
    for copy in own_copies[:4]:
        copy.wait()
    q0, o = gather_q(0), gather_o()
    step(q0, 0)
    for t in range(4):
        tiles = [fc_in[:, 128 * (8 * t + r) : 128 * (8 * t + r + 1)].astype(f32) for r in range(8)]
        for j, tile in enumerate(swap_blocks(tiles)):
            mixed_in[j, :, 128 * t : 128 * (t + 1)] = tile.astype(bf16)
    for j in range(MC):
        own_copy(mixed_in.at[j], ag_i.at[(j,) + me])
    step(vectors, 1)
    ends = [lens[0, 0], lens[0, 0] + lens[0, 1], lens[0, 0] + lens[0, 1] + lens[0, 2]]

    def flag(b, qb):
        return 256 * b >= begins(ends, jnp.full((1, 256), 256 * qb, jnp.int32))

    tables(ends, cos, sin)
    step(o, 0)
    step(vectors, 2)
    step(q0, 1)
    for copy in own_copies[4:]:
        copy.wait()
    step(vectors, 3)
    step(gather_q(1), 0)
    step(vectors, 4)
    load_s = pltpu.make_async_copy(ag_s, sv, io.at[2])
    load_s.start()
    step(q0, 2)
    step(o, 1)
    load_s.wait()
    rows = sv[...].reshape(32, 8, 128)
    row0, row1, row2 = (rows[:, i, :].astype(bf16) for i in range(3))
    for i in range(4):
        vecs[i : i + 1, :] = from_ranks(row0, i, 1024)
    wide_b[0:1, 0:3072] = from_ranks(row1, "qkv", 3072)
    wide_b[1:2, :] = from_ranks(row2, "fc_in", 4096)
    load_x.wait()
    for i in range(4):
        rows = pl.ds(256 * i, 256)
        normed, _ = normalised(attT[rows, :].astype(f32))
        hid[rows, :] = (normed * vecs[0:1, :] + vecs[1:2, :]).astype(bf16)
        if i == 1:
            step(q0, 3)
            step(gather_m(0, False), 0)
    step(o, 2)
    step(gather_q(1), 1)
    step(gather_m(1, True), 0)
    step(gather_q(2), 0)
    step(q0, 4)

    def fetch_q(i):
        return pltpu.make_async_copy(ag_q.at[i], wq.at[i % 2], fetch.at[i % 2])

    fetch_q(0).start()
    hgrad[...] = jnp.zeros_like(hgrad)
    load_g.wait()

    bufs = (
        q_s, k_s, v_s, qT, kT, vT, doT, E, DS,
        mlp.at[:, pl.ds(0, 256)], mlp.at[:, pl.ds(256, 256)], mlp.at[:, pl.ds(512, 256)],
    )

    def attention_step(i, carry):
        fetch_q(i).wait()
        more, before = i < QG - 1, i > 0
        a, b = gather_m(2 * i, False), gather_m(2 * i + 1, True)
        b, slow = b[:2], b[2:]

        @pl.when(before)
        def _():
            step(slow, 2)

        @pl.when(more)
        def _():
            step(gather_m(2 * i + 2, False), 0)

        def pump(p):
            if p == 0:

                @pl.when(i == 0)
                def _():
                    step(o, 3)
                    step(gather_m(0, False), 1)
                    step(o, 4)
                    fetch_o = pltpu.make_async_copy(ag_o, wo, fetch.at[2])
                    fetch_o.start()
                    fetch_o.wait()
                    step(gather_q(1), 2)

                @pl.when(before)
                def _():
                    step(sums(i - 1, 768), 1)


                @pl.when(more)
                def _():
                    step(gather_m(2 * i + 3, True), 0)

            elif p == 1:

                @pl.when(i == 0)
                def _():
                    step(gather_m(1, True), 1)

                step(a, 2)

                @pl.when(i < QG - 2)
                def _():
                    step(gather_q(i + 2), 1)

            elif p == 2:

                @pl.when(i == 0)
                def _():
                    step(slow, 2)

                @pl.when(more)
                def _():
                    step(gather_q(i + 1), 3)

                @pl.when(before)
                def _():
                    step(sums(i - 1, 768), 2)

                @pl.when(i > 1)
                def _():
                    end_q(i - 2)

                @pl.when(before)
                def _():
                    step(gather_m(2 * i - 2, False), 4)
                    step(gather_m(2 * i - 1, True), 4)

            elif p == 3:
                step(b, 2)

                @pl.when(more)
                def _():
                    step(gather_m(2 * i + 3, True)[2:], 1)

                @pl.when(i < QG - 3)
                def _():
                    step(gather_q(i + 3), 0)

            elif p == 4:
                step(a, 3)

                @pl.when(more)
                def _():
                    step(gather_q(i + 1), 4)
                    fetch_q(i + 1).start()
                    step(gather_m(2 * i + 2, False), 1)

                @pl.when(before)
                def _():
                    step(sums(i - 1, 768), 3)

            elif p == 6:

                @pl.when(i < QG - 2)
                def _():
                    step(gather_q(i + 2), 2)

                @pl.when(more)
                def _():
                    step(gather_m(2 * i + 3, True)[:2], 1)

                step(b, 3)
                step(slow, 3)

        def W(j):
            return wq[i % 2, :, :, :, :, :, 256 * j : 256 * (j + 1)].reshape(T, 256)

        def bias(j):
            return wide_b[0:1, lanes(1024 * j + 256 * i, 256)]

        attention_group(
            flag, hid, g, W, lambda: wo[i].reshape(256, T), bias, (cos, sin), bufs,
            attT.at[pl.ds(pl.multiple_of(256 * i, 256), 256)], dqkv, pump,
        )
        for b_ in range(2):
            v = dg(hid[:, 512 * b_ : 512 * (b_ + 1)], dqkv[...], 0, 0).astype(bf16)
            v = v.reshape(2, 2, 2, 2, 2, 16, 768)
            for h in range(2):
                part[h, i % NP, 2 * b_ : 2 * b_ + 2, :, :, :, :, 0:768] = v[:, :, :, :, h]
        step(sums(i, 768), 0)
        pump(5)
        total = jnp.sum(dqkv[...].astype(f32), axis=0, keepdims=True)
        for j in range(3):
            wide_g[0:1, lanes(1024 * j + 256 * i, 256)] = total[:, 256 * j : 256 * (j + 1)]
        whole_w = wq[i % 2].reshape(T, 768)
        for b_ in range(2):
            rows = pl.ds(512 * b_, 512)
            hgrad[rows, :] += dg(dqkv[rows, :], whole_w, 1, 1)
        pump(6)
        return carry

    lax.fori_loop(0, QG, attention_step, 0)

    def fetch_m(j):
        return [
            pltpu.make_async_copy(
                ag_i.at[j], wq.at[j % 2, :, :, :, :, :, pl.ds(0, 512)], fetch.at[j % 2]
            ),
            pltpu.make_async_copy(ag_d.at[j], wd.at[j % 2], fetch.at[2 + j % 2]),
        ]

    for copy in fetch_m(0):
        copy.start()
    for b in range(2):
        v = dg(attT[512 * b : 512 * (b + 1), :], g[...], 1, 0).astype(bf16)
        v = v.reshape(2, 2, 2, 2, 2, 16, T)
        for h in range(2):
            part[h, 4 % NP, 2 * b : 2 * b + 2] = v[:, :, :, :, h]
    step(sums(3, 768), 1)
    step(sums(4, 1024), 0)
    mlp[...] = jnp.zeros_like(mlp)
    step(gather_m(MC - 2, False), 4)
    step(gather_m(MC - 1, True), 4)

    act, pg = DS.at[:, pl.ds(0, 512)], DS.at[:, pl.ds(512, 512)]

    def mlp_step(j, carry):
        for copy in fetch_m(j):
            copy.wait()

        @pl.when(j < MC - 1)
        def _():
            for copy in fetch_m(j + 1):
                copy.start()

        w_in = wq[j % 2, :, :, :, :, :, 0:512].reshape(T, 512)
        w_down = wd[j % 2].reshape(512, T)
        bias = wide_b[1:2, lanes(512 * j, 512)]
        for b in range(2):
            rows = pl.ds(512 * b, 512)
            pre = dg(hid[rows, :], w_in, 1, 0) + bias
            a, d = gelu_parts(pre)
            act[rows, :] = a.astype(bf16)
            pg[rows, :] = (dg(g[rows, :], w_down, 1, 1) * d).astype(bf16)
            if b == 0:
                step(sums(j + 4, 1024), 1)
        wide_g[1:2, lanes(512 * j, 512)] = jnp.sum(pg[...].astype(f32), axis=0, keepdims=True)

        @pl.when(j == 0)
        def _():
            step(sums(3, 768), 2)

        @pl.when(j == 1)
        def _():
            end_q(2)
            step(sums(3, 768), 3)

        @pl.when(j == 2)
        def _():
            end_q(3)
            step(sums(4, 1024), 3)

        @pl.when(j == 3)
        def _():
            end_o()

        @pl.when(j > 3)
        def _():
            end_m(j - 4)

        @pl.when(j > 2)
        def _():
            step(sums(j + 2, 1024), 3)

        @pl.when(j > 0)
        def _():
            step(sums(j + 3, 1024), 2)

        slot = (j + 5) % NP
        for b in range(2):
            v = dg(hid[:, 512 * b : 512 * (b + 1)], pg[...], 0, 0).astype(bf16)
            v = v.reshape(2, 2, 2, 2, 2, 16, 512)
            for h in range(2):
                part[0, slot, 2 * b : 2 * b + 2, :, :, :, :, 512 * h : 512 * (h + 1)] = v[
                    :, :, :, :, h
                ]
            v = dg(act[:, 256 * b : 256 * (b + 1)], g[...], 0, 0).astype(bf16)
            part[1, slot, 2 * b : 2 * b + 2] = v.reshape(2, 2, 2, 2, 16, T)
        step(sums(j + 5, 1024), 0)
        for b in range(2):
            rows = pl.ds(512 * b, 512)
            mlp[rows, :] += dg(act[rows, :], w_down, 1, 0)
            hgrad[rows, :] += dg(pg[rows, :], w_in, 1, 1)
        return carry

    lax.fori_loop(0, MC, mlp_step, 0)

    last = MC + 4
    reload_x = pltpu.make_async_copy(tokens, hid, io.at[0])
    reload_x.start()
    step(sums(last, 1024), 1)
    step(sums(last - 1, 1024), 2)
    step(sums(last - 2, 1024), 3)
    end_m(MC - 4)
    reload_x.wait()
    for i in range(4):
        rows = pl.ds(256 * i, 256)
        normed, inverse = normalised(hid[rows, :].astype(f32))
        h = hgrad[rows, :]
        up_g = g[rows, :].astype(f32)
        for k, v in enumerate((h * normed, h, up_g)):
            v = jnp.sum(v, axis=0, keepdims=True)
            gvecs[k : k + 1, :] = v if i == 0 else gvecs[k : k + 1, :] + v
        n = h * vecs[0:1, :]
        d = n - jnp.mean(n, axis=-1, keepdims=True)
        d = d - normed * jnp.mean(n * normed, axis=-1, keepdims=True)
        E[rows, :] = (up_g + inverse * d).astype(bf16)
    put_tg = pltpu.make_async_copy(E, tokens_grad, io.at[1])
    put_tg.start()
    step(sums(last, 1024), 2)
    step(sums(last - 1, 1024), 3)
    row0 = sum(to_ranks(gvecs[min(k, 2) : min(k, 2) + 1, :], k, 1024) for k in range(4))
    row1 = to_ranks(wide_g[0:1, 0:3072], "qkv", 3072)
    row2 = to_ranks(wide_g[1:2, :], "fc_in", 4096)
    for r in range(32):
        part_s[r // 8, r // 4 % 2, r // 2 % 2, r % 2] = jnp.concatenate(
            [row0[r : r + 1], row1[r : r + 1], row2[r : r + 1], jnp.zeros((5, 128), f32)]
        )
    tiny = Scatter(
        place, lambda *a: part_s.at[a], [s1, s2, s3, sz], "zxy",
        lambda s: send.at[13, 0, s], lambda s: recv.at[13, 0, s],
    )
    tiny.step(0)
    end_m(MC - 3)
    tiny.step(1)
    step(sums(last, 1024), 3)
    tiny.step(2)
    w_out = wo[...].reshape(T, T)
    squares = [jnp.zeros((1, T), f32)] * 3
    for i in range(4):
        rows = pl.ds(256 * i, 256)
        x = hid[rows, :].astype(f32)
        a = dg(attT[:, rows], w_out, 0, 0) + vecs[2:3, :]
        m = mlp[rows, :] + vecs[3:4, :]
        hid[rows, :] = (x + a + m).astype(bf16)
        squares = [
            s + jnp.sum(v * v, axis=0, keepdims=True) for s, v in zip(squares, (x, a, m))
        ]
        if i == 1:
            tiny.step(3)
    put_mixed = pltpu.make_async_copy(hid, mixed, io.at[0])
    put_mixed.start()
    for i in range(3):
        total = jnp.sum(squares[i], axis=1, keepdims=True)
        stats[i : i + 1, :] = jnp.broadcast_to(total, (1, 128))
    end_m(MC - 2)
    end_m(MC - 1)
    out_s[...] = tiny.total()
    put_tg.wait()
    put_mixed.wait()
    for arrays in [vectors, o] + [gather_q(i) for i in range(QG)]:
        for array in arrays:
            array.close()

    def close_m(j, carry):
        for array in gather_m(2 * j, False) + gather_m(2 * j + 1, True):
            array.close()
        return carry

    lax.fori_loop(0, MC // 2, close_m, 0)


def whole_layer(lens, tokens, cot, qkv, out, fc_in, down, *vectors):
    any_ = pl.BlockSpec(memory_space=pl.ANY)
    vmem = pl.BlockSpec(memory_space=pltpu.VMEM)
    sd = jax.ShapeDtypeStruct
    ranks = (4, 2, 2, 2)
    dma = pltpu.SemaphoreType.DMA
    return pl.pallas_call(
        layer_kernel,
        out_shape=[
            sd((T, T), bf16),
            sd((T, T), bf16),
            sd((32, 3072), f32),
            sd((32, 1024), f32),
            sd((32, 4096), f32),
            sd((128, 1024), f32),
            sd((8, 128), f32),
            sd((8, 128), f32),
            sd((QG,) + ranks + (32, 768), bf16),
            sd(ranks + (32, 1024), bf16),
            sd((MC,) + ranks + (32, 512), bf16),
            sd((MC,) + ranks + (16, 1024), bf16),
            sd(ranks + (8, 128), f32),
        ],
        in_specs=[pl.BlockSpec(memory_space=pltpu.SMEM)]
        + [any_] * 2
        + [vmem] * 10,
        out_specs=[any_] * 2 + [vmem] * 6 + [any_] * 5,
        scratch_shapes=[
            pltpu.VMEM((T, T), bf16),
            pltpu.VMEM((T, T), bf16),
            pltpu.VMEM((T, T), f32),
            pltpu.VMEM((T, T), bf16),
            pltpu.VMEM((8, 1024), f32),
            pltpu.VMEM((8, 1024), f32),
            pltpu.VMEM((8, 4096), f32),
            pltpu.VMEM((8, 4096), f32),
            pltpu.VMEM(ranks + (8, 128), f32),
            pltpu.VMEM((T, 128), f32),
            pltpu.VMEM((T, 128), f32),
            pltpu.VMEM(ranks + (32, 1024), bf16),
            pltpu.VMEM((2,) + ranks + (32, 768), bf16),
            pltpu.VMEM((2,) + ranks + (16, 1024), bf16),
            pltpu.VMEM((T, 768), bf16),
            pltpu.VMEM((T, 256), bf16),
            pltpu.VMEM((T, 256), bf16),
            pltpu.VMEM((T, 256), bf16),
            pltpu.VMEM((256, T), bf16),
            pltpu.VMEM((256, T), bf16),
            pltpu.VMEM((256, T), bf16),
            pltpu.VMEM((256, T), bf16),
            pltpu.VMEM((T, T), bf16),
            pltpu.VMEM((T, T), bf16),
            pltpu.VMEM((T, T), f32),
            pltpu.VMEM((8, 128), f32),
            pltpu.VMEM((MC, 32, 512), bf16),
            pltpu.VMEM((2, NP) + ranks + (16, 1024), bf16),
            pltpu.VMEM((2, 2, 4, 2, 2, 16, 1024), bf16),
            pltpu.VMEM((2, 4, 4, 2, 16, 1024), bf16),
            pltpu.VMEM((2, 4, 4, 16, 1024), bf16),
            pltpu.VMEM((2, 4, 3, 16, 1024), bf16),
            pltpu.VMEM(ranks + (8, 128), f32),
            pltpu.VMEM((4, 2, 2, 8, 128), f32),
            pltpu.VMEM((4, 2, 8, 128), f32),
            pltpu.VMEM((4, 8, 128), f32),
            pltpu.VMEM((3, 8, 128), f32),
            dma((30,)),
            dma((3,)),
            dma((4,)),
            dma((14, 2, 6)),
            dma((14, 2, 6)),
            dma((14, 3, 6)),
            dma((14, 3, 6)),
        ],
        compiler_params=pltpu.CompilerParams(
            collective_id=0, has_side_effects=True, vmem_limit_bytes=63 * 2**20
        ),
    )(lens, tokens, cot, qkv, out, fc_in, down, *vectors)


def finish_kernel(
    mixed, tokens_grad, q, o, i_, d, s, stats,
    f_mixed, f_tokens, f_gain, f_shift, f_q, f_qb, f_o, f_ob, f_i, f_ib, f_d, f_db, f_rms,
    held, held_q, held_o, held_d, held_i, turned, sem,
):
    count = iter(range(16))

    def move(src, there, dst):
        n = next(count)
        into = pltpu.make_async_copy(src, there, sem.at[n])
        into.start()
        return into, pltpu.make_async_copy(there, dst, sem.at[n])

    load_i = pltpu.make_async_copy(i_, held_i, sem.at[15])
    load_i.start()
    moves = []
    for n, (a, b) in enumerate(((mixed, f_mixed), (tokens_grad, f_tokens))):
        for k in range(4):
            rows = pl.ds(256 * k, 256)
            moves.append(move(a.at[rows], held.at[n, rows], b.at[rows]))
    moves += [move(q, held_q, f_q), move(o, held_o, f_o), move(d, held_d, f_d)]
    load_i.wait()
    for t in range(4):
        tiles = [held_i[:, 512 * j + 128 * t : 512 * j + 128 * (t + 1)] for j in range(MC)]
        for r, tile in enumerate(swap_blocks(tiles)):
            turned[:, 128 * (8 * t + r) : 128 * (8 * t + r + 1)] = tile
        for into, out in moves[3 * t : 3 * t + 3]:
            into.wait()
            out.start()
    put_i = pltpu.make_async_copy(turned, f_i, sem.at[15])
    put_i.start()
    f_gain[...] = s[0:1, 0:32]
    f_shift[...] = s[0:1, 32:64]
    f_ob[...] = s[0:1, 64:96]
    f_db[...] = s[0:1, 96:128]
    f_qb[...] = s[1:2, 0:96]
    f_ib[...] = s[2:3, :]
    lane = lax.broadcasted_iota(jnp.int32, (1, 128), 1)
    mean = jnp.where(lane == 0, stats[0:1, :], jnp.where(lane == 1, stats[1:2, :], stats[2:3, :]))
    f_rms[...] = jnp.sqrt(mean * (1.0 / (T * T)))[:, 0:3]
    put_i.wait()
    for _, out in moves:
        out.wait()


def finish(mixed, tokens_grad, q, o, i_, d, s, stats):
    any_ = pl.BlockSpec(memory_space=pl.ANY)
    vmem = pl.BlockSpec(memory_space=pltpu.VMEM)
    sd = jax.ShapeDtypeStruct
    return pl.pallas_call(
        finish_kernel,
        out_shape=[
            sd((T, T), bf16), sd((T, T), bf16), sd((1, 32), f32), sd((1, 32), f32),
            sd((32, 3072), f32), sd((1, 96), f32), sd((32, 1024), f32), sd((1, 32), f32),
            sd((32, 4096), f32), sd((1, 128), f32), sd((128, 1024), f32), sd((1, 32), f32),
            sd((1, 3), f32),
        ],
        in_specs=[any_] * 6 + [vmem, vmem],
        out_specs=[any_, any_, vmem, vmem, any_, vmem, any_, vmem, any_, vmem, any_, vmem, vmem],
        scratch_shapes=[
            pltpu.VMEM((2, T, T), bf16),
            pltpu.VMEM((32, 3072), f32),
            pltpu.VMEM((32, 1024), f32),
            pltpu.VMEM((128, 1024), f32),
            pltpu.VMEM((32, 4096), f32),
            pltpu.VMEM((32, 4096), f32),
            pltpu.SemaphoreType.DMA((16,)),
        ],
    )(mixed, tokens_grad, q, o, i_, d, s, stats)


def layer_math(
    tokens, cotangent, seq_lens, gain, shift, qkv_matrix, qkv_b, out_matrix, out_b,
    in_matrix, in_b, down_matrix, down_b,
):
    gain_full, shift_full = gain.astype(f32), shift.astype(f32)
    row_count, width = tokens.shape
    inputs = tokens.astype(f32)
    centred = inputs - jnp.mean(inputs, axis=-1, keepdims=True)
    inverse = lax.rsqrt(jnp.mean(centred * centred, axis=-1, keepdims=True) + epsilon)
    normed = centred * inverse
    hid_low = (normed * gain_full + shift_full).astype(bf16)
    qkv = jnp.dot(hid_low, qkv_matrix, preferred_element_type=f32) + qkv_b.astype(f32)
    segment, places, offset = positions(seq_lens[0], row_count)
    freqs = 10000.0 ** (-jnp.arange(ROT // 2, dtype=f32) * 2.0 / ROT)
    angle = offset[:, None] * freqs[None, :]
    cosine = jnp.cos(angle)[:, None, :]
    sine = jnp.sin(angle)[:, None, :]
    heads = (row_count, HEADS, HEAD)
    q_low = rotate(qkv[:, :width].reshape(heads), cosine, sine).astype(bf16)
    k_low = rotate(qkv[:, width : 2 * width].reshape(heads), cosine, sine).astype(bf16)
    v_low = qkv[:, 2 * width :].reshape(heads).astype(bf16)
    block_rows = min(512, row_count)
    block_count = row_count // block_rows
    outputs = []
    kept_lse = []
    for block in range(block_count):
        lower = block * block_rows
        upper = lower + block_rows
        scores, allowed = block_scores(
            q_low[lower:upper], k_low[:upper], segment[lower:upper], segment[:upper],
            places[lower:upper], places[:upper],
        )
        row_max = jnp.max(scores, axis=-1, keepdims=True)
        expo = jnp.exp(scores - row_max)
        totals = jnp.sum(expo, axis=-1, keepdims=True)
        soft_low = (expo / totals).astype(bf16)
        kept_lse.append(row_max + jnp.log(totals))
        outputs.append(
            jnp.einsum("hqk,khd->qhd", soft_low, v_low[:upper], preferred_element_type=f32)
        )
    att_low = jnp.concatenate(outputs, axis=0).reshape(row_count, width).astype(bf16)
    attn_out = jnp.dot(att_low, out_matrix, preferred_element_type=f32) + out_b.astype(f32)
    pre = jnp.dot(hid_low, in_matrix, preferred_element_type=f32) + in_b.astype(f32)
    gelu_exact = partial(jax.nn.gelu, approximate=False)
    act_low = gelu_exact(pre).astype(bf16)
    mlp = jnp.dot(act_low, down_matrix, preferred_element_type=f32) + down_b.astype(f32)
    mixed = (inputs + attn_out + mlp).astype(bf16)
    stream_rms = jnp.sqrt(
        jnp.stack([jnp.mean(inputs * inputs), jnp.mean(attn_out * attn_out), jnp.mean(mlp * mlp)])
    )[None, :]
    upstream = cotangent.astype(f32)
    grad_down = transposed_times(act_low, cotangent)
    grad_out = transposed_times(att_low, cotangent)
    grad_sum = jnp.sum(upstream, axis=0)
    act_grad = times_transposed(cotangent, down_matrix)
    _, gelu_pull = jax.vjp(gelu_exact, pre)
    pre_grad_low = gelu_pull(act_grad)[0].astype(bf16)
    grad_in = transposed_times(hid_low, pre_grad_low)
    grad_in_b = jnp.sum(pre_grad_low.astype(f32), axis=0)
    att_grad_low = times_transposed(cotangent, out_matrix).astype(bf16).reshape(heads)
    query_grads = []
    key_grad = jnp.zeros(heads, f32)
    value_grad = jnp.zeros(heads, f32)
    for block in range(block_count):
        lower = block * block_rows
        upper = lower + block_rows
        query_block = q_low[lower:upper]
        scores, allowed = block_scores(
            query_block, k_low[:upper], segment[lower:upper], segment[:upper],
            places[lower:upper], places[:upper],
        )
        soft = jnp.where(allowed[None], jnp.exp(scores - kept_lse[block]), 0.0)
        soft_low = soft.astype(bf16)
        out_grad = att_grad_low[lower:upper]
        value_part = jnp.einsum("hqk,qhd->khd", soft_low, out_grad, preferred_element_type=f32)
        prob_grad = jnp.einsum("qhd,khd->hqk", out_grad, v_low[:upper], preferred_element_type=f32)
        score_grad = soft * (prob_grad - jnp.sum(soft * prob_grad, axis=-1, keepdims=True))
        score_low = score_grad.astype(bf16)
        query_grads.append(
            jnp.einsum("hqk,khd->qhd", score_low, k_low[:upper], preferred_element_type=f32)
            * HEAD ** (-0.5)
        )
        key_part = jnp.einsum(
            "hqk,qhd->khd", score_low, query_block, preferred_element_type=f32
        ) * HEAD ** (-0.5)
        padding = ((0, row_count - upper), (0, 0), (0, 0))
        key_grad = key_grad + jnp.pad(key_part, padding)
        value_grad = value_grad + jnp.pad(value_part, padding)
    query_grad = unrotate(jnp.concatenate(query_grads, axis=0), cosine, sine)
    key_grad = unrotate(key_grad, cosine, sine)
    qkv_grad_low = jnp.concatenate(
        [g.reshape(row_count, width) for g in (query_grad, key_grad, value_grad)], axis=1
    ).astype(bf16)
    grad_qkv = transposed_times(hid_low, qkv_grad_low)
    grad_qkv_b = jnp.sum(qkv_grad_low.astype(f32), axis=0)
    hidden_grad = times_transposed(qkv_grad_low, qkv_matrix) + times_transposed(
        pre_grad_low, in_matrix
    )
    grad_gain = jnp.sum(hidden_grad * normed, axis=0)
    grad_shift = jnp.sum(hidden_grad, axis=0)
    scaled = hidden_grad * gain_full
    input_grad = upstream + inverse * (
        scaled
        - jnp.mean(scaled, axis=-1, keepdims=True)
        - normed * jnp.mean(scaled * normed, axis=-1, keepdims=True)
    )
    return (
        mixed, input_grad.astype(bf16), grad_gain, grad_shift, grad_qkv, grad_qkv_b,
        grad_out, grad_sum, grad_in, grad_in_b, grad_down, grad_sum, stream_rms,
    )


def generic(tokens, cotangent, seq_lens, *shards):
    axes = ("wide", "narrow")
    whole = [lax.all_gather(s, axes, axis=0, tiled=True) for s in shards]
    results = layer_math(tokens, cotangent, seq_lens, *whole)
    summed = [
        lax.psum_scatter(g, axes, scatter_dimension=0, tiled=True) for g in results[2:12]
    ]
    return (*results[:2], *summed, results[12])


def local(
    tokens, cotangent, seq_lens, norm_gain, norm_bias, qkv_weight, qkv_bias, out_weight,
    out_bias, fc_in_weight, fc_in_bias, fc_out_weight, fc_out_bias,
):
    vectors = (norm_gain, norm_bias, out_bias, fc_out_bias, qkv_bias, fc_in_bias)
    results = whole_layer(
        seq_lens, tokens, cotangent, qkv_weight, out_weight, fc_in_weight, fc_out_weight,
        *(v[None, :] for v in vectors),
    )
    results = finish(*results[:8])
    flat = (2, 3, 5, 7, 9, 11)
    return tuple(r[0] if n in flat else r for n, r in enumerate(results))


def solution(mesh):
    rows, flat = P(("wide", "narrow"), None), P(("wide", "narrow"))
    fits = mesh.shape["wide"] == 8 and mesh.shape["narrow"] == 4
    return jax.shard_map(
        local if fits else generic,
        mesh=mesh,
        in_specs=(rows, rows, rows, flat, flat, rows, flat, rows, flat, rows, flat, rows, flat),
        out_specs=(rows, rows, flat, flat, rows, flat, rows, flat, rows, flat, rows, flat, rows),
        check_vma=False,
    )
```

```python
import itertools
from functools import partial

import jax
import jax.numpy as jnp
from jax import lax
from jax.experimental import pallas as pl
from jax.experimental.pallas import tpu as pltpu
from jax.sharding import PartitionSpec as P

HEADS = 16
HEAD = 64
ROT = 16
MESH = pl.DeviceIdType.MESH
bf16 = jnp.bfloat16
f32 = jnp.float32
ALL = slice(None)

epsilon = 1e-05


def positions(lengths, count):
    ends = jnp.cumsum(lengths)
    places = jnp.arange(count, dtype=jnp.int32)
    segment = jnp.sum((places[:, None] >= ends[None, :]).astype(jnp.int32), axis=1)
    starts = ends - lengths
    slots = jnp.arange(lengths.shape[0], dtype=jnp.int32)
    begin = jnp.sum(jnp.where(segment[:, None] == slots[None, :], starts[None, :], 0), axis=1)
    return (segment, places, (places - begin).astype(jnp.float32))


def rotate(vector, cosine, sine):
    half = ROT // 2
    first = vector[..., :half]
    second = vector[..., half:ROT]
    return jnp.concatenate(
        [first * cosine - second * sine, second * cosine + first * sine, vector[..., ROT:]], axis=-1
    )


def unrotate(grad, cosine, sine):
    half = ROT // 2
    first = grad[..., :half]
    second = grad[..., half:ROT]
    return jnp.concatenate(
        [first * cosine + second * sine, second * cosine - first * sine, grad[..., ROT:]], axis=-1
    )


def times_transposed(left, right):
    return lax.dot_general(
        left, right, (((1,), (1,)), ((), ())), preferred_element_type=jnp.float32
    )


def transposed_times(left, right):
    return lax.dot_general(
        left, right, (((0,), (0,)), ((), ())), preferred_element_type=jnp.float32
    )


def block_scores(query_block, key_low, seg_query, seg_key, place_query, place_key):
    raw = jnp.einsum(
        "qhd,khd->hqk", query_block, key_low, preferred_element_type=jnp.float32
    ) * HEAD ** (-0.5)
    allowed = (seg_query[:, None] == seg_key[None, :]) & (
        place_key[None, :] <= place_query[:, None]
    )
    return (jnp.where(allowed[None], raw, -1e30), allowed)


QG = 4
LOG2E = 1.4426950408889634
LN2 = 0.6931471805599453
T = 1024
MC = 8


class Place:
    def __init__(self):
        wide, narrow = lax.axis_index("wide"), lax.axis_index("narrow")
        self.z, self.x = wide // 2, wide % 2
        self.y, self.c = narrow // 2, narrow % 2
        self.me = (self.z, self.x, self.y, self.c)
        self.zs = [(self.z + d) % 4 for d in (1, 2, 3)]

    def device(self, z, x, y, c):
        return (z * 2 + x, y * 2 + c)

    def targets(self, axis):
        z, x, y, c = self.me
        if axis == "z":
            return [(i, (other, x, y, c)) for i, other in enumerate(self.zs)]
        return [
            {"x": (3, (z, 1 - x, y, c)), "y": (4, (z, x, 1 - y, c)), "c": (5, (z, x, y, 1 - c))}[axis]
        ]

    def partners(self):
        z, x, y, c = self.me
        return [self.device(p, x, y, c) for p in self.zs] + [
            self.device(z, 1 - x, y, c),
            self.device(z, x, 1 - y, c),
            self.device(z, x, y, 1 - c),
        ]

    def greet(self):
        barrier = pltpu.get_barrier_semaphore()
        for other in self.partners():
            pl.semaphore_signal(barrier, inc=1, device_id=other, device_id_type=MESH)
        pl.semaphore_wait(barrier, 6)


def dg(a, b, ca, cb):
    return lax.dot_general(a, b, (((ca,), (cb,)), ((), ())), preferred_element_type=f32)


def exact(a, b, ca, cb):
    return lax.dot_general(
        a, b, (((ca,), (cb,)), ((), ())), precision=lax.Precision.HIGHEST,
        preferred_element_type=f32,
    )


def remote(src, dst, send, recv, device):
    return pltpu.make_async_remote_copy(
        src_ref=src, dst_ref=dst, send_sem=send, recv_sem=recv,
        device_id=device, device_id_type=MESH,
    )


class Gather:
    def __init__(self, place, view, order, send, recv):
        self.p, self.view, self.axes = place, view, order + "c"
        self.send, self.recv = send, recv

    def copies(self, i):
        me, axis = self.p.me, self.axes[i]
        part = [ALL if a in self.axes[:i] else me["zxyc".index(a)] for a in "zxyc"]
        return [
            remote(
                self.view(*part), self.view(*part), self.send(slot), self.recv(slot),
                self.p.device(*to),
            )
            for slot, to in self.p.targets(axis)
        ]

    def step(self, i):
        if i > 0:
            for copy in self.copies(i - 1):
                copy.wait_recv()
        if i < 4:
            for copy in self.copies(i):
                copy.start()

    def close(self):
        for i in range(4):
            for copy in self.copies(i):
                copy.wait_send()


class Scatter:
    def __init__(self, place, part, bufs, order, send, recv):
        self.p, self.part, self.bufs = place, part, bufs
        self.axes = "c" + order[::-1]
        self.send, self.recv = send, recv

    def index(self, i, value):
        return [
            value if a == self.axes[i] else (self.p.me[k] if a in self.axes[:i] else ALL)
            for k, a in enumerate("zxyc")
        ]

    def landing(self, i):
        buf = self.bufs[i]
        return [buf.at[n] for n in range(3)] if self.axes[i] == "z" else [buf]

    def copies(self, i):
        at = "zxyc".index(self.axes[i])
        return [
            remote(
                self.part(*self.index(i, to[at])), land, self.send(slot), self.recv(slot),
                self.p.device(*to),
            )
            for land, (slot, to) in zip(self.landing(i), self.p.targets(self.axes[i]))
        ]

    def step(self, i):
        if i > 0:
            for copy in self.copies(i - 1):
                copy.wait_recv()
            part = self.part(*self.index(i - 1, self.p.me["zxyc".index(self.axes[i - 1])]))
            for buf in self.landing(i - 1):
                for at in itertools.product(*(range(n) for n in buf.shape[:-2])):
                    part[at] = part[at] + buf[at]
        for copy in self.copies(i):
            copy.start()

    def total(self):
        for copy in self.copies(3):
            copy.wait_recv()
        out = self.part(*self.p.me)[...].astype(f32)
        for buf in self.landing(3):
            out = out + buf[...].astype(f32)
        for i in range(4):
            for copy in self.copies(i):
                copy.wait_send()
        return out


def begins(ends, t):
    first = jnp.zeros_like(t)
    for e in ends:
        first = jnp.where(t >= e, e, first)
    return first


def tables(ends, cos_ref, sin_ref):
    t = lax.broadcasted_iota(jnp.int32, (T, 128), 0)
    d = lax.broadcasted_iota(jnp.int32, (T, 128), 1) % 64
    offset = (t - begins(ends, t)).astype(f32)
    freq = jnp.exp((d % 8).astype(f32) * (-2.0 / 16 * 9.210340371976184))
    angle = offset * freq
    cos_ref[...] = jnp.where(d < 16, jnp.cos(angle), 1.0)
    sin_ref[...] = jnp.where(d < 16, jnp.where(d < 8, -1.0, 1.0) * jnp.sin(angle), 0.0)


def turn(v, cos, sin, sign):
    first = lax.broadcasted_iota(jnp.int32, cos.shape, 1) % 64 < 8
    out = []
    for i in range(2):
        w = v[:, 128 * i : 128 * (i + 1)]
        r = jnp.where(first, pltpu.roll(w, 120, 1), pltpu.roll(w, 8, 1)) * sin
        out.append(w * cos + r if sign > 0 else w * cos - r)
    return jnp.concatenate(out, axis=1)


def attention_group(flag, hid, g, W, Wo, bias, tabs, bufs, attT, dqkv, pump):
    q_s, k_s, v_s, qT, kT, vT, doT, E, DS, dv, dk, dqT = bufs
    R = 512
    for i in range(T // R):
        rows = pl.ds(i * R, R)
        tb = [t[rows, :] for t in tabs]
        h = hid[rows, :]
        q = turn(dg(h, W(0), 1, 0) + bias(0), *tb, 1) * (LOG2E / 8)
        q = q.astype(bf16)
        q_s[rows, :] = q
        qT[:, rows] = q.T
        k = turn(dg(h, W(1), 1, 0) + bias(1), *tb, 1).astype(bf16)
        k_s[rows, :] = k
        kT[:, rows] = k.T
        v = (dg(h, W(2), 1, 0) + bias(2)).astype(bf16)
        v_s[rows, :] = v
        vT[:, rows] = v.T
    pump(0)
    for i in range(T // R):
        rows = pl.ds(i * R, R)
        do = dg(g[rows, :], Wo(), 1, 1).astype(bf16)
        doT[:, rows] = do.T
    head_row = lax.broadcasted_iota(jnp.int32, (256, 256), 0) // 64
    head_lane = lax.broadcasted_iota(jnp.int32, (256, 256), 1) // 64
    causal = lax.broadcasted_iota(jnp.int32, (256, 256), 0) <= lax.broadcasted_iota(
        jnp.int32, (256, 256), 1
    )
    for qb in range(T // 256):
        kk = 256 * (qb + 1)
        cols = pl.ds(256 * qb, 256)

        def head(h):
            hc, hr = pl.ds(h * 256, 256), pl.ds(h * 64, 64)
            s = dg(k_s[0:kk, :], jnp.where(head_row == h, qT[:, cols], 0), 1, 0)
            blocks = [s[256 * b : 256 * (b + 1)] for b in range(qb + 1)]
            blocks[qb] = jnp.where(causal, blocks[qb], -1e30)
            m = jnp.max(blocks[qb], axis=0, keepdims=True)
            for b in range(qb):
                top = jnp.max(blocks[b], axis=0, keepdims=True)
                m = jnp.maximum(m, jnp.where(flag(b, qb), top, -1e30))
            total = None
            for b in range(qb + 1):
                e = jnp.exp2(blocks[b] - (m if b == qb else jnp.where(flag(b, qb), m, 1e30)))
                t = jnp.sum(e, axis=0, keepdims=True)
                total = t if total is None else total + t
                E[256 * b : 256 * (b + 1), hc] = e.astype(bf16)
            inv = 1.0 / total
            oT = dg(vT[hr, 0:kk], E[0:kk, hc], 1, 0) * inv
            attT[hr, cols] = oT.astype(bf16)
            dot = jnp.sum(doT[hr, cols].astype(f32) * oT, axis=0, keepdims=True) * inv
            doz = jnp.where(head_row == h, doT[:, cols].astype(f32) * inv, 0.0).astype(bf16)
            dp = dg(v_s[0:kk, :], doz, 1, 0)
            DS[0:kk, hc] = (E[0:kk, hc].astype(f32) * (dp - dot)).astype(bf16)
            dqT[pl.ds(256 * qb + 64 * h, 64), :] = dg(kT[hr, 0:kk], DS[0:kk, hc], 1, 0)
            return doz.T

        doz = jnp.concatenate([head(h) for h in range(4)], axis=0)
        q = q_s[cols, :]
        qz = jnp.concatenate([jnp.where(head_lane == h, q, 0) for h in range(4)], axis=0)
        pv = dg(E[0:kk, :], doz, 1, 0)
        pk = dg(DS[0:kk, :], qz, 1, 0)
        if qb > 0:
            dv[0 : 256 * qb, :] += pv[0 : 256 * qb]
            dk[0 : 256 * qb, :] += pk[0 : 256 * qb]
        dv[256 * qb : kk, :] = pv[256 * qb :]
        dk[256 * qb : kk, :] = pk[256 * qb :]
        pump(qb + 1)
    for i in range(T // R):
        rows = pl.ds(i * R, R)
        tb = [t[rows, :] for t in tabs]
        dq = jnp.concatenate(
            [dqT[R * i + 256 * b : R * i + 256 * (b + 1), :].T for b in range(R // 256)]
        )
        dqkv[rows, 0:256] = turn(dq * 0.125, *tb, -1).astype(bf16)
        dqkv[rows, 256:512] = turn(dk[rows, :] * LN2, *tb, -1).astype(bf16)
        dqkv[rows, 512:768] = dv[rows, :].astype(bf16)


def gelu_parts(x):
    a1, a2, a3, a4, a5 = 0.254829592, -0.284496736, 1.421413741, -1.453152027, 1.061405429
    ex = jnp.exp2(x * x * (-0.5 * LOG2E))
    t = 1.0 / (1.0 + (0.3275911 * 0.7071067811865476) * jnp.abs(x))
    half = ((((0.5 * a5 * t + 0.5 * a4) * t + 0.5 * a3) * t + 0.5 * a2) * t + 0.5 * a1) * t * ex
    phi = jnp.where(x < 0, half, 1.0 - half)
    return x * phi, phi + x * ex * 0.3989422804014327


def spread(kind, width):
    lane = lax.broadcasted_iota(jnp.int32, (128, width), 0)
    at = lax.broadcasted_iota(jnp.int32, (128, width), 1)
    col = lax.broadcasted_iota(jnp.int32, (32, width), 1)
    rank = lax.broadcasted_iota(jnp.int32, (32, width), 0)
    if kind == "qkv":
        return lane == at % 96, col // 96 == rank
    if kind == "fc_in":
        return lane == at // 512 * 16 + at % 16, col % 512 // 16 == rank
    return lane == at % 32 + 32 * kind, col // 32 == rank


def from_ranks(rows, kind, width):
    hot, mine = spread(kind, width)
    t = dg(rows, jnp.where(hot, 1.0, 0.0).astype(bf16), 1, 0)
    return jnp.sum(jnp.where(mine, t, 0.0), axis=0, keepdims=True)


def to_ranks(vector, kind, width):
    hot, mine = spread(kind, width)
    return exact(jnp.where(mine, vector, 0.0), jnp.where(hot, 1.0, 0.0), 1, 1)


def normalised(x):
    centred = x - jnp.mean(x, axis=-1, keepdims=True)
    inverse = lax.rsqrt(jnp.mean(centred * centred, axis=-1, keepdims=True) + epsilon)
    return centred * inverse, inverse


def swap_blocks(tiles):
    block = lax.broadcasted_iota(jnp.int32, tiles[0].shape, 1) // 16
    out = []
    for b in range(8):
        tile = None
        for a in range(8):
            moved = tiles[a] if a == b else pltpu.roll(tiles[a], (16 * (a - b)) % 128, 1)
            tile = moved if tile is None else jnp.where(block == a, moved, tile)
        out.append(tile)
    return out


NP = 4


def lanes(start, size):
    return pl.ds(pl.multiple_of(start, 128), size)


def layer_kernel(
    lens, tokens, cot, qkv, out, fc_in, down,
    v_gain, v_shift, v_out, v_down, v_qkv, v_in,
    mixed, tokens_grad, out_q, out_o, out_i, out_d, out_s, stats,
    ag_q, ag_o, ag_i, ag_d, ag_s,
    hid, g, hgrad, attT, vecs, gvecs, wide_b, wide_g, sv,
    cos, sin, wo, wq, wd, dqkv, q_s, k_s, v_s, qT, kT, vT, doT, E, DS, mlp,
    packed, mixed_in, part, r1, r2, r3, rz, part_s, s1, s2, s3, sz,
    own, io, fetch, send, recv, gsend, grecv,
):
    place = Place()
    me = place.me

    def gather(n, views, orders=("zxy", "zyx")):
        return [
            Gather(place, view, order, lambda s, k=k: gsend.at[n, k, s], lambda s, k=k: grecv.at[n, k, s])
            for k, (view, order) in enumerate(zip(views, orders))
        ]

    def gather_q(i):
        return gather(
            i, [lambda *a, h=h: ag_q.at[(i,) + a + (pl.ds(16 * h, 16),)] for h in range(2)]
        )

    def gather_o():
        views = [lambda *a, h=h: ag_o.at[a + (pl.ds(16 * h, 16),)] for h in range(2)]
        return gather(4, views)

    def gather_m(j, odd):
        down_view = lambda *a: ag_d.at[(j,) + a]
        if not odd:
            return gather(5 + j, [lambda *a: ag_i.at[(j,) + a], down_view])
        views = [lambda *a, h=h: ag_i.at[(j,) + a + (pl.ds(16 * h, 16),)] for h in range(2)]
        return gather(5 + j, views + [down_view], ("zxy", "zyx", "xyz"))

    def step(arrays, i):
        for array in arrays:
            array.step(i)

    vectors = gather(13, [lambda *a: ag_s.at[a]])

    def sums(n, width):
        return [
            Scatter(
                place,
                lambda *a, k=k: part.at[(k, n % NP) + a + (ALL, pl.ds(0, width))],
                [
                    b.at[(k, n % count) + (ALL,) * d + (ALL, pl.ds(0, width))]
                    for b, d, count in ((r1, 3, 2), (r2, 2, 4), (r3, 1, 4), (rz, 1, 4))
                ],
                ("zxy", "zyx")[k],
                lambda s, k=k: send.at[n, k, s],
                lambda s, k=k: recv.at[n, k, s],
            )
            for k in range(2)
        ]

    def end_q(i):
        totals = [array.total() for array in sums(i, 768)]
        for h in range(2):
            for j in range(3):
                out_q[pl.ds(16 * h, 16), lanes(1024 * j + 256 * i, 256)] = totals[h][
                    :, 256 * j : 256 * (j + 1)
                ]

    def end_o():
        totals = [array.total() for array in sums(4, 1024)]
        for h in range(2):
            out_o[pl.ds(16 * h, 16), :] = totals[h]

    def end_m(j):
        totals = [array.total() for array in sums(5 + j, 1024)]
        for h in range(2):
            out_i[pl.ds(16 * h, 16), lanes(512 * j, 512)] = totals[0][
                :, 512 * h : 512 * (h + 1)
            ]
        out_d[pl.ds(pl.multiple_of(16 * j, 16), 16), :] = totals[1]

    own_copies = []

    def own_copy(src, dst):
        copy = pltpu.make_async_copy(src, dst, own.at[len(own_copies)])
        copy.start()
        own_copies.append(copy)
        return copy

    for i in range(QG):
        for j in range(3):
            own_copy(
                qkv.at[:, pl.ds(1024 * j + 256 * i, 256)],
                ag_q.at[(i,) + me + (ALL, pl.ds(256 * j, 256))],
            )
        if i == 0:
            own_copy(out, ag_o.at[me])
    for j in range(MC):
        own_copy(down.at[pl.ds(16 * j, 16)], ag_d.at[(j,) + me])
    load_x = pltpu.make_async_copy(tokens, attT, io.at[0])
    load_x.start()
    load_g = pltpu.make_async_copy(cot, g, io.at[1])
    load_g.start()
    packed[...] = jnp.zeros_like(packed)
    for i, vector in enumerate((v_gain, v_shift, v_out, v_down)):
        packed[0:1, 32 * i : 32 * (i + 1)] = vector[...].astype(f32)
    packed[1:2, 0:96] = v_qkv[...].astype(f32)
    packed[2:3, :] = v_in[...].astype(f32)
    own_s = pltpu.make_async_copy(packed, ag_s.at[me], io.at[2])
    own_s.start()
    place.greet()
    own_s.wait()
    step(vectors, 0)
    for copy in own_copies[:4]:
        copy.wait()
    q0, o = gather_q(0), gather_o()
    step(q0, 0)
    for t in range(4):
        tiles = [fc_in[:, 128 * (8 * t + r) : 128 * (8 * t + r + 1)].astype(f32) for r in range(8)]
        for j, tile in enumerate(swap_blocks(tiles)):
            mixed_in[j, :, 128 * t : 128 * (t + 1)] = tile.astype(bf16)
    for j in range(MC):
        own_copy(mixed_in.at[j], ag_i.at[(j,) + me])
    step(vectors, 1)
    ends = [lens[0, 0], lens[0, 0] + lens[0, 1], lens[0, 0] + lens[0, 1] + lens[0, 2]]

    def flag(b, qb):
        return 256 * b >= begins(ends, jnp.full((1, 256), 256 * qb, jnp.int32))

    tables(ends, cos, sin)
    step(o, 0)
    step(vectors, 2)
    step(q0, 1)
    for copy in own_copies[4:]:
        copy.wait()
    step(vectors, 3)
    step(gather_q(1), 0)
    step(vectors, 4)
    load_s = pltpu.make_async_copy(ag_s, sv, io.at[2])
    load_s.start()
    step(q0, 2)
    step(o, 1)
    load_s.wait()
    rows = sv[...].reshape(32, 8, 128)
    row0, row1, row2 = (rows[:, i, :].astype(bf16) for i in range(3))
    for i in range(4):
        vecs[i : i + 1, :] = from_ranks(row0, i, 1024)
    wide_b[0:1, 0:3072] = from_ranks(row1, "qkv", 3072)
    wide_b[1:2, :] = from_ranks(row2, "fc_in", 4096)
    load_x.wait()
    for i in range(4):
        rows = pl.ds(256 * i, 256)
        normed, _ = normalised(attT[rows, :].astype(f32))
        hid[rows, :] = (normed * vecs[0:1, :] + vecs[1:2, :]).astype(bf16)
        if i == 1:
            step(q0, 3)
            step(gather_m(0, False), 0)
    step(o, 2)
    step(gather_q(1), 1)
    step(gather_m(1, True), 0)
    step(gather_q(2), 0)
    step(q0, 4)

    def fetch_q(i):
        return pltpu.make_async_copy(ag_q.at[i], wq.at[i % 2], fetch.at[i % 2])

    fetch_q(0).start()
    hgrad[...] = jnp.zeros_like(hgrad)
    load_g.wait()

    bufs = (
        q_s, k_s, v_s, qT, kT, vT, doT, E, DS,
        mlp.at[:, pl.ds(0, 256)], mlp.at[:, pl.ds(256, 256)], mlp.at[:, pl.ds(512, 256)],
    )

    def attention_step(i, carry):
        fetch_q(i).wait()
        more, before = i < QG - 1, i > 0
        a, b = gather_m(2 * i, False), gather_m(2 * i + 1, True)
        b, slow = b[:2], b[2:]

        @pl.when(before)
        def _():
            step(slow, 2)

        @pl.when(more)
        def _():
            step(gather_m(2 * i + 2, False), 0)

        def pump(p):
            if p == 0:

                @pl.when(i == 0)
                def _():
                    step(o, 3)
                    step(gather_m(0, False), 1)
                    step(o, 4)
                    fetch_o = pltpu.make_async_copy(ag_o, wo, fetch.at[2])
                    fetch_o.start()
                    fetch_o.wait()
                    step(gather_q(1), 2)

                @pl.when(before)
                def _():
                    step(sums(i - 1, 768), 1)


                @pl.when(more)
                def _():
                    step(gather_m(2 * i + 3, True), 0)

            elif p == 1:

                @pl.when(i == 0)
                def _():
                    step(gather_m(1, True), 1)

                step(a, 2)

                @pl.when(i < QG - 2)
                def _():
                    step(gather_q(i + 2), 1)

            elif p == 2:

                @pl.when(i == 0)
                def _():
                    step(slow, 2)

                @pl.when(more)
                def _():
                    step(gather_q(i + 1), 3)

                @pl.when(before)
                def _():
                    step(sums(i - 1, 768), 2)

                @pl.when(i > 1)
                def _():
                    end_q(i - 2)

                @pl.when(before)
                def _():
                    step(gather_m(2 * i - 2, False), 4)
                    step(gather_m(2 * i - 1, True), 4)

            elif p == 3:
                step(b, 2)

                @pl.when(more)
                def _():
                    step(gather_m(2 * i + 3, True)[2:], 1)

                @pl.when(i < QG - 3)
                def _():
                    step(gather_q(i + 3), 0)

            elif p == 4:
                step(a, 3)

                @pl.when(more)
                def _():
                    step(gather_q(i + 1), 4)
                    fetch_q(i + 1).start()
                    step(gather_m(2 * i + 2, False), 1)

                @pl.when(before)
                def _():
                    step(sums(i - 1, 768), 3)

            elif p == 6:

                @pl.when(i < QG - 2)
                def _():
                    step(gather_q(i + 2), 2)

                @pl.when(more)
                def _():
                    step(gather_m(2 * i + 3, True)[:2], 1)

                step(b, 3)
                step(slow, 3)

        def W(j):
            return wq[i % 2, :, :, :, :, :, 256 * j : 256 * (j + 1)].reshape(T, 256)

        def bias(j):
            return wide_b[0:1, lanes(1024 * j + 256 * i, 256)]

        attention_group(
            flag, hid, g, W, lambda: wo[i].reshape(256, T), bias, (cos, sin), bufs,
            attT.at[pl.ds(pl.multiple_of(256 * i, 256), 256)], dqkv, pump,
        )
        for b_ in range(2):
            v = dg(hid[:, 512 * b_ : 512 * (b_ + 1)], dqkv[...], 0, 0).astype(bf16)
            v = v.reshape(2, 2, 2, 2, 2, 16, 768)
            for h in range(2):
                part[h, i % NP, 2 * b_ : 2 * b_ + 2, :, :, :, :, 0:768] = v[:, :, :, :, h]
        step(sums(i, 768), 0)
        pump(5)
        total = jnp.sum(dqkv[...].astype(f32), axis=0, keepdims=True)
        for j in range(3):
            wide_g[0:1, lanes(1024 * j + 256 * i, 256)] = total[:, 256 * j : 256 * (j + 1)]
        whole_w = wq[i % 2].reshape(T, 768)
        for b_ in range(2):
            rows = pl.ds(512 * b_, 512)
            hgrad[rows, :] += dg(dqkv[rows, :], whole_w, 1, 1)
        pump(6)
        return carry

    lax.fori_loop(0, QG, attention_step, 0)

    def fetch_m(j):
        return [
            pltpu.make_async_copy(
                ag_i.at[j], wq.at[j % 2, :, :, :, :, :, pl.ds(0, 512)], fetch.at[j % 2]
            ),
            pltpu.make_async_copy(ag_d.at[j], wd.at[j % 2], fetch.at[2 + j % 2]),
        ]

    for copy in fetch_m(0):
        copy.start()
    for b in range(2):
        v = dg(attT[512 * b : 512 * (b + 1), :], g[...], 1, 0).astype(bf16)
        v = v.reshape(2, 2, 2, 2, 2, 16, T)
        for h in range(2):
            part[h, 4 % NP, 2 * b : 2 * b + 2] = v[:, :, :, :, h]
    step(sums(3, 768), 1)
    step(sums(4, 1024), 0)
    mlp[...] = jnp.zeros_like(mlp)
    step(gather_m(MC - 2, False), 4)
    step(gather_m(MC - 1, True), 4)

    act, pg = DS.at[:, pl.ds(0, 512)], DS.at[:, pl.ds(512, 512)]

    def mlp_step(j, carry):
        for copy in fetch_m(j):
            copy.wait()

        @pl.when(j < MC - 1)
        def _():
            for copy in fetch_m(j + 1):
                copy.start()

        w_in = wq[j % 2, :, :, :, :, :, 0:512].reshape(T, 512)
        w_down = wd[j % 2].reshape(512, T)
        bias = wide_b[1:2, lanes(512 * j, 512)]
        for b in range(2):
            rows = pl.ds(512 * b, 512)
            pre = dg(hid[rows, :], w_in, 1, 0) + bias
            a, d = gelu_parts(pre)
            act[rows, :] = a.astype(bf16)
            pg[rows, :] = (dg(g[rows, :], w_down, 1, 1) * d).astype(bf16)
            if b == 0:
                step(sums(j + 4, 1024), 1)
        wide_g[1:2, lanes(512 * j, 512)] = jnp.sum(pg[...].astype(f32), axis=0, keepdims=True)

        @pl.when(j == 0)
        def _():
            step(sums(3, 768), 2)

        @pl.when(j == 1)
        def _():
            end_q(2)
            step(sums(3, 768), 3)

        @pl.when(j == 2)
        def _():
            end_q(3)
            step(sums(4, 1024), 3)

        @pl.when(j == 3)
        def _():
            end_o()

        @pl.when(j > 3)
        def _():
            end_m(j - 4)

        @pl.when(j > 2)
        def _():
            step(sums(j + 2, 1024), 3)

        @pl.when(j > 0)
        def _():
            step(sums(j + 3, 1024), 2)

        slot = (j + 5) % NP
        for b in range(2):
            v = dg(hid[:, 512 * b : 512 * (b + 1)], pg[...], 0, 0).astype(bf16)
            v = v.reshape(2, 2, 2, 2, 2, 16, 512)
            for h in range(2):
                part[0, slot, 2 * b : 2 * b + 2, :, :, :, :, 512 * h : 512 * (h + 1)] = v[
                    :, :, :, :, h
                ]
            v = dg(act[:, 256 * b : 256 * (b + 1)], g[...], 0, 0).astype(bf16)
            part[1, slot, 2 * b : 2 * b + 2] = v.reshape(2, 2, 2, 2, 16, T)
        step(sums(j + 5, 1024), 0)
        for b in range(2):
            rows = pl.ds(512 * b, 512)
            mlp[rows, :] += dg(act[rows, :], w_down, 1, 0)
            hgrad[rows, :] += dg(pg[rows, :], w_in, 1, 1)
        return carry

    lax.fori_loop(0, MC, mlp_step, 0)

    last = MC + 4
    reload_x = pltpu.make_async_copy(tokens, hid, io.at[0])
    reload_x.start()
    step(sums(last, 1024), 1)
    step(sums(last - 1, 1024), 2)
    step(sums(last - 2, 1024), 3)
    end_m(MC - 4)
    reload_x.wait()
    for i in range(4):
        rows = pl.ds(256 * i, 256)
        normed, inverse = normalised(hid[rows, :].astype(f32))
        h = hgrad[rows, :]
        up_g = g[rows, :].astype(f32)
        for k, v in enumerate((h * normed, h, up_g)):
            v = jnp.sum(v, axis=0, keepdims=True)
            gvecs[k : k + 1, :] = v if i == 0 else gvecs[k : k + 1, :] + v
        n = h * vecs[0:1, :]
        d = n - jnp.mean(n, axis=-1, keepdims=True)
        d = d - normed * jnp.mean(n * normed, axis=-1, keepdims=True)
        E[rows, :] = (up_g + inverse * d).astype(bf16)
    put_tg = pltpu.make_async_copy(E, tokens_grad, io.at[1])
    put_tg.start()
    @pl.when(place.z >= 0)
    def _():
        row0 = sum(to_ranks(gvecs[min(k, 2) : min(k, 2) + 1, :], k, 1024) for k in range(4))
        row1 = to_ranks(wide_g[0:1, 0:3072], "qkv", 3072)
        row2 = to_ranks(wide_g[1:2, :], "fc_in", 4096)
        for r in range(32):
            part_s[r // 8, r // 4 % 2, r // 2 % 2, r % 2] = jnp.concatenate(
                [row0[r : r + 1], row1[r : r + 1], row2[r : r + 1], jnp.zeros((5, 128), f32)]
            )

    tiny = Scatter(
        place, lambda *a: part_s.at[a], [s1, s2, s3, sz], "zxy",
        lambda s: send.at[13, 0, s], lambda s: recv.at[13, 0, s],
    )
    tiny.step(0)
    step(sums(last, 1024), 2)
    step(sums(last - 1, 1024), 3)
    end_m(MC - 3)
    tiny.step(1)
    step(sums(last, 1024), 3)
    tiny.step(2)
    w_out = wo[...].reshape(T, T)
    squares = [jnp.zeros((1, T), f32)] * 3
    for i in range(4):
        rows = pl.ds(256 * i, 256)
        x = hid[rows, :].astype(f32)
        a = dg(attT[:, rows], w_out, 0, 0) + vecs[2:3, :]
        m = mlp[rows, :] + vecs[3:4, :]
        hid[rows, :] = (x + a + m).astype(bf16)
        squares = [
            s + jnp.sum(v * v, axis=0, keepdims=True) for s, v in zip(squares, (x, a, m))
        ]
        if i == 1:
            tiny.step(3)
    put_mixed = pltpu.make_async_copy(hid, mixed, io.at[0])
    put_mixed.start()
    for i in range(3):
        total = jnp.sum(squares[i], axis=1, keepdims=True)
        stats[i : i + 1, :] = jnp.broadcast_to(total, (1, 128))
    end_m(MC - 2)
    end_m(MC - 1)
    out_s[...] = tiny.total()
    put_tg.wait()
    put_mixed.wait()
    for arrays in [vectors, o] + [gather_q(i) for i in range(QG)]:
        for array in arrays:
            array.close()

    def close_m(j, carry):
        for array in gather_m(2 * j, False) + gather_m(2 * j + 1, True):
            array.close()
        return carry

    lax.fori_loop(0, MC // 2, close_m, 0)


def whole_layer(lens, tokens, cot, qkv, out, fc_in, down, *vectors):
    any_ = pl.BlockSpec(memory_space=pl.ANY)
    vmem = pl.BlockSpec(memory_space=pltpu.VMEM)
    sd = jax.ShapeDtypeStruct
    ranks = (4, 2, 2, 2)
    dma = pltpu.SemaphoreType.DMA
    return pl.pallas_call(
        layer_kernel,
        out_shape=[
            sd((T, T), bf16),
            sd((T, T), bf16),
            sd((32, 3072), f32),
            sd((32, 1024), f32),
            sd((32, 4096), f32),
            sd((128, 1024), f32),
            sd((8, 128), f32),
            sd((8, 128), f32),
            sd((QG,) + ranks + (32, 768), bf16),
            sd(ranks + (32, 1024), bf16),
            sd((MC,) + ranks + (32, 512), bf16),
            sd((MC,) + ranks + (16, 1024), bf16),
            sd(ranks + (8, 128), f32),
        ],
        in_specs=[pl.BlockSpec(memory_space=pltpu.SMEM)]
        + [any_] * 2
        + [vmem] * 10,
        out_specs=[any_] * 2 + [vmem] * 6 + [any_] * 5,
        scratch_shapes=[
            pltpu.VMEM((T, T), bf16),
            pltpu.VMEM((T, T), bf16),
            pltpu.VMEM((T, T), f32),
            pltpu.VMEM((T, T), bf16),
            pltpu.VMEM((8, 1024), f32),
            pltpu.VMEM((8, 1024), f32),
            pltpu.VMEM((8, 4096), f32),
            pltpu.VMEM((8, 4096), f32),
            pltpu.VMEM(ranks + (8, 128), f32),
            pltpu.VMEM((T, 128), f32),
            pltpu.VMEM((T, 128), f32),
            pltpu.VMEM(ranks + (32, 1024), bf16),
            pltpu.VMEM((2,) + ranks + (32, 768), bf16),
            pltpu.VMEM((2,) + ranks + (16, 1024), bf16),
            pltpu.VMEM((T, 768), bf16),
            pltpu.VMEM((T, 256), bf16),
            pltpu.VMEM((T, 256), bf16),
            pltpu.VMEM((T, 256), bf16),
            pltpu.VMEM((256, T), bf16),
            pltpu.VMEM((256, T), bf16),
            pltpu.VMEM((256, T), bf16),
            pltpu.VMEM((256, T), bf16),
            pltpu.VMEM((T, T), bf16),
            pltpu.VMEM((T, T), bf16),
            pltpu.VMEM((T, T), f32),
            pltpu.VMEM((8, 128), f32),
            pltpu.VMEM((MC, 32, 512), bf16),
            pltpu.VMEM((2, NP) + ranks + (16, 1024), bf16),
            pltpu.VMEM((2, 2, 4, 2, 2, 16, 1024), bf16),
            pltpu.VMEM((2, 4, 4, 2, 16, 1024), bf16),
            pltpu.VMEM((2, 4, 4, 16, 1024), bf16),
            pltpu.VMEM((2, 4, 3, 16, 1024), bf16),
            pltpu.VMEM(ranks + (8, 128), f32),
            pltpu.VMEM((4, 2, 2, 8, 128), f32),
            pltpu.VMEM((4, 2, 8, 128), f32),
            pltpu.VMEM((4, 8, 128), f32),
            pltpu.VMEM((3, 8, 128), f32),
            dma((30,)),
            dma((3,)),
            dma((4,)),
            dma((14, 2, 6)),
            dma((14, 2, 6)),
            dma((14, 3, 6)),
            dma((14, 3, 6)),
        ],
        compiler_params=pltpu.CompilerParams(
            collective_id=0, has_side_effects=True, vmem_limit_bytes=63 * 2**20
        ),
    )(lens, tokens, cot, qkv, out, fc_in, down, *vectors)


def finish_kernel(
    mixed, tokens_grad, q, o, i_, d, s, stats,
    f_mixed, f_tokens, f_gain, f_shift, f_q, f_qb, f_o, f_ob, f_i, f_ib, f_d, f_db, f_rms,
    held, held_q, held_o, held_d, held_i, turned, sem,
):
    count = iter(range(16))

    def move(src, there, dst):
        n = next(count)
        into = pltpu.make_async_copy(src, there, sem.at[n])
        into.start()
        return into, pltpu.make_async_copy(there, dst, sem.at[n])

    load_i = pltpu.make_async_copy(i_, held_i, sem.at[15])
    load_i.start()
    moves = []
    for n, (a, b) in enumerate(((mixed, f_mixed), (tokens_grad, f_tokens))):
        for k in range(4):
            rows = pl.ds(256 * k, 256)
            moves.append(move(a.at[rows], held.at[n, rows], b.at[rows]))
    moves += [move(q, held_q, f_q), move(o, held_o, f_o), move(d, held_d, f_d)]
    load_i.wait()
    for t in range(4):
        tiles = [held_i[:, 512 * j + 128 * t : 512 * j + 128 * (t + 1)] for j in range(MC)]
        for r, tile in enumerate(swap_blocks(tiles)):
            turned[:, 128 * (8 * t + r) : 128 * (8 * t + r + 1)] = tile
        for into, out in moves[3 * t : 3 * t + 3]:
            into.wait()
            out.start()
    put_i = pltpu.make_async_copy(turned, f_i, sem.at[15])
    put_i.start()
    f_gain[...] = s[0:1, 0:32]
    f_shift[...] = s[0:1, 32:64]
    f_ob[...] = s[0:1, 64:96]
    f_db[...] = s[0:1, 96:128]
    f_qb[...] = s[1:2, 0:96]
    f_ib[...] = s[2:3, :]
    lane = lax.broadcasted_iota(jnp.int32, (1, 128), 1)
    mean = jnp.where(lane == 0, stats[0:1, :], jnp.where(lane == 1, stats[1:2, :], stats[2:3, :]))
    f_rms[...] = jnp.sqrt(mean * (1.0 / (T * T)))[:, 0:3]
    put_i.wait()
    for _, out in moves:
        out.wait()


def finish(mixed, tokens_grad, q, o, i_, d, s, stats):
    any_ = pl.BlockSpec(memory_space=pl.ANY)
    vmem = pl.BlockSpec(memory_space=pltpu.VMEM)
    sd = jax.ShapeDtypeStruct
    return pl.pallas_call(
        finish_kernel,
        out_shape=[
            sd((T, T), bf16), sd((T, T), bf16), sd((1, 32), f32), sd((1, 32), f32),
            sd((32, 3072), f32), sd((1, 96), f32), sd((32, 1024), f32), sd((1, 32), f32),
            sd((32, 4096), f32), sd((1, 128), f32), sd((128, 1024), f32), sd((1, 32), f32),
            sd((1, 3), f32),
        ],
        in_specs=[any_] * 6 + [vmem, vmem],
        out_specs=[any_, any_, vmem, vmem, any_, vmem, any_, vmem, any_, vmem, any_, vmem, vmem],
        scratch_shapes=[
            pltpu.VMEM((2, T, T), bf16),
            pltpu.VMEM((32, 3072), f32),
            pltpu.VMEM((32, 1024), f32),
            pltpu.VMEM((128, 1024), f32),
            pltpu.VMEM((32, 4096), f32),
            pltpu.VMEM((32, 4096), f32),
            pltpu.SemaphoreType.DMA((16,)),
        ],
    )(mixed, tokens_grad, q, o, i_, d, s, stats)


def layer_math(
    tokens, cotangent, seq_lens, gain, shift, qkv_matrix, qkv_b, out_matrix, out_b,
    in_matrix, in_b, down_matrix, down_b,
):
    gain_full, shift_full = gain.astype(f32), shift.astype(f32)
    row_count, width = tokens.shape
    inputs = tokens.astype(f32)
    centred = inputs - jnp.mean(inputs, axis=-1, keepdims=True)
    inverse = lax.rsqrt(jnp.mean(centred * centred, axis=-1, keepdims=True) + epsilon)
    normed = centred * inverse
    hid_low = (normed * gain_full + shift_full).astype(bf16)
    qkv = jnp.dot(hid_low, qkv_matrix, preferred_element_type=f32) + qkv_b.astype(f32)
    segment, places, offset = positions(seq_lens[0], row_count)
    freqs = 10000.0 ** (-jnp.arange(ROT // 2, dtype=f32) * 2.0 / ROT)
    angle = offset[:, None] * freqs[None, :]
    cosine = jnp.cos(angle)[:, None, :]
    sine = jnp.sin(angle)[:, None, :]
    heads = (row_count, HEADS, HEAD)
    q_low = rotate(qkv[:, :width].reshape(heads), cosine, sine).astype(bf16)
    k_low = rotate(qkv[:, width : 2 * width].reshape(heads), cosine, sine).astype(bf16)
    v_low = qkv[:, 2 * width :].reshape(heads).astype(bf16)
    block_rows = min(512, row_count)
    block_count = row_count // block_rows
    outputs = []
    kept_lse = []
    for block in range(block_count):
        lower = block * block_rows
        upper = lower + block_rows
        scores, allowed = block_scores(
            q_low[lower:upper], k_low[:upper], segment[lower:upper], segment[:upper],
            places[lower:upper], places[:upper],
        )
        row_max = jnp.max(scores, axis=-1, keepdims=True)
        expo = jnp.exp(scores - row_max)
        totals = jnp.sum(expo, axis=-1, keepdims=True)
        soft_low = (expo / totals).astype(bf16)
        kept_lse.append(row_max + jnp.log(totals))
        outputs.append(
            jnp.einsum("hqk,khd->qhd", soft_low, v_low[:upper], preferred_element_type=f32)
        )
    att_low = jnp.concatenate(outputs, axis=0).reshape(row_count, width).astype(bf16)
    attn_out = jnp.dot(att_low, out_matrix, preferred_element_type=f32) + out_b.astype(f32)
    pre = jnp.dot(hid_low, in_matrix, preferred_element_type=f32) + in_b.astype(f32)
    gelu_exact = partial(jax.nn.gelu, approximate=False)
    act_low = gelu_exact(pre).astype(bf16)
    mlp = jnp.dot(act_low, down_matrix, preferred_element_type=f32) + down_b.astype(f32)
    mixed = (inputs + attn_out + mlp).astype(bf16)
    stream_rms = jnp.sqrt(
        jnp.stack([jnp.mean(inputs * inputs), jnp.mean(attn_out * attn_out), jnp.mean(mlp * mlp)])
    )[None, :]
    upstream = cotangent.astype(f32)
    grad_down = transposed_times(act_low, cotangent)
    grad_out = transposed_times(att_low, cotangent)
    grad_sum = jnp.sum(upstream, axis=0)
    act_grad = times_transposed(cotangent, down_matrix)
    _, gelu_pull = jax.vjp(gelu_exact, pre)
    pre_grad_low = gelu_pull(act_grad)[0].astype(bf16)
    grad_in = transposed_times(hid_low, pre_grad_low)
    grad_in_b = jnp.sum(pre_grad_low.astype(f32), axis=0)
    att_grad_low = times_transposed(cotangent, out_matrix).astype(bf16).reshape(heads)
    query_grads = []
    key_grad = jnp.zeros(heads, f32)
    value_grad = jnp.zeros(heads, f32)
    for block in range(block_count):
        lower = block * block_rows
        upper = lower + block_rows
        query_block = q_low[lower:upper]
        scores, allowed = block_scores(
            query_block, k_low[:upper], segment[lower:upper], segment[:upper],
            places[lower:upper], places[:upper],
        )
        soft = jnp.where(allowed[None], jnp.exp(scores - kept_lse[block]), 0.0)
        soft_low = soft.astype(bf16)
        out_grad = att_grad_low[lower:upper]
        value_part = jnp.einsum("hqk,qhd->khd", soft_low, out_grad, preferred_element_type=f32)
        prob_grad = jnp.einsum("qhd,khd->hqk", out_grad, v_low[:upper], preferred_element_type=f32)
        score_grad = soft * (prob_grad - jnp.sum(soft * prob_grad, axis=-1, keepdims=True))
        score_low = score_grad.astype(bf16)
        query_grads.append(
            jnp.einsum("hqk,khd->qhd", score_low, k_low[:upper], preferred_element_type=f32)
            * HEAD ** (-0.5)
        )
        key_part = jnp.einsum(
            "hqk,qhd->khd", score_low, query_block, preferred_element_type=f32
        ) * HEAD ** (-0.5)
        padding = ((0, row_count - upper), (0, 0), (0, 0))
        key_grad = key_grad + jnp.pad(key_part, padding)
        value_grad = value_grad + jnp.pad(value_part, padding)
    query_grad = unrotate(jnp.concatenate(query_grads, axis=0), cosine, sine)
    key_grad = unrotate(key_grad, cosine, sine)
    qkv_grad_low = jnp.concatenate(
        [g.reshape(row_count, width) for g in (query_grad, key_grad, value_grad)], axis=1
    ).astype(bf16)
    grad_qkv = transposed_times(hid_low, qkv_grad_low)
    grad_qkv_b = jnp.sum(qkv_grad_low.astype(f32), axis=0)
    hidden_grad = times_transposed(qkv_grad_low, qkv_matrix) + times_transposed(
        pre_grad_low, in_matrix
    )
    grad_gain = jnp.sum(hidden_grad * normed, axis=0)
    grad_shift = jnp.sum(hidden_grad, axis=0)
    scaled = hidden_grad * gain_full
    input_grad = upstream + inverse * (
        scaled
        - jnp.mean(scaled, axis=-1, keepdims=True)
        - normed * jnp.mean(scaled * normed, axis=-1, keepdims=True)
    )
    return (
        mixed, input_grad.astype(bf16), grad_gain, grad_shift, grad_qkv, grad_qkv_b,
        grad_out, grad_sum, grad_in, grad_in_b, grad_down, grad_sum, stream_rms,
    )


def generic(tokens, cotangent, seq_lens, *shards):
    axes = ("wide", "narrow")
    whole = [lax.all_gather(s, axes, axis=0, tiled=True) for s in shards]
    results = layer_math(tokens, cotangent, seq_lens, *whole)
    summed = [
        lax.psum_scatter(g, axes, scatter_dimension=0, tiled=True) for g in results[2:12]
    ]
    return (*results[:2], *summed, results[12])


def local(
    tokens, cotangent, seq_lens, norm_gain, norm_bias, qkv_weight, qkv_bias, out_weight,
    out_bias, fc_in_weight, fc_in_bias, fc_out_weight, fc_out_bias,
):
    vectors = (norm_gain, norm_bias, out_bias, fc_out_bias, qkv_bias, fc_in_bias)
    results = whole_layer(
        seq_lens, tokens, cotangent, qkv_weight, out_weight, fc_in_weight, fc_out_weight,
        *(v[None, :] for v in vectors),
    )
    results = finish(*results[:8])
    flat = (2, 3, 5, 7, 9, 11)
    return tuple(r[0] if n in flat else r for n, r in enumerate(results))


def solution(mesh):
    rows, flat = P(("wide", "narrow"), None), P(("wide", "narrow"))
    fits = mesh.shape["wide"] == 8 and mesh.shape["narrow"] == 4
    return jax.shard_map(
        local if fits else generic,
        mesh=mesh,
        in_specs=(rows, rows, rows, flat, flat, rows, flat, rows, flat, rows, flat, rows, flat),
        out_specs=(rows, rows, flat, flat, rows, flat, rows, flat, rows, flat, rows, flat, rows),
        check_vma=False,
    )
```
